32 devices in a mesh: src: 4 (over y, x), ch: 8 (over z, core).
Axes of the slice: x: 2, y: 2, z: 4, core: 2. Of those that a mesh axis runs over, the one named last changes fastest.
Arguments:
- dry_signal: bfloat16 [64, 40960], P(('src', 'ch')), may hold values from -6 to 6
- room_spectra: bfloat16 [64, 8, 64, 2, 1024], P('src', None, 'ch'), may hold values from -0.1875 to 0.1875
- render_slot: int32 [64], P('src'), may hold values from 0 to 63, as said below
- decoder: bfloat16 [64, 1024], replicated, may hold values from -0.75 to 0.75
Outputs:
- speakers: bfloat16 [32768, 1024], P(('src', 'ch'))
The draws below stay inside these ranges and needn't reach their ends.
Inputs may be any that keep to these rules, and one draw needn't show every extreme that they name: render_slot is a permutation that keeps each group: sources g * 16 to (g + 1) * 16 - 1 are mapped onto the rows of that same range, each row once.
All inputs are finite; a program needn't handle non-finite values.
Results may differ from the reference program's by a relative error of at most 0.018.
Values may be sent and summed in bfloat16 or wider, within the bound.
No kernel may reach another device: no remote copies, remote signals or barrier semaphores. Data moves between devices by JAX's collectives and lax.ppermute only.
A program may use at most 128 MiB of HBM per device.

```python
import math
import jax
import jax.numpy as jnp
from jax import lax

CH = 64
BLOCK = 1024
PARTITIONS = 8
SPK = 1024
GROUP = 16
NBLK = 32
SOURCES = 64


def draw_render_slot(key, part):
    groups = SOURCES // GROUP
    subkeys = jax.random.split(key, groups)
    orders = jax.vmap(lambda subkey: jax.random.permutation(subkey, GROUP))(subkeys)
    offsets = jnp.arange(groups, dtype=jnp.int32)[:, None] * GROUP
    return (orders.astype(jnp.int32) + offsets).reshape(SOURCES)


def steps_of(key, shape, shards, least, top_value):
    def one(dim, shards_of):
        steps = jax.random.uniform(jax.random.fold_in(jax.random.fold_in(key, 6), dim), (shards_of,), jnp.float32, least / len(shards), top_value / len(shards))
        return jnp.repeat(jnp.exp(steps), shape[dim] // shards_of).reshape((-1,) + (1,) * (len(shape) - dim - 1))

    loudness = one(*shards[0])
    for cut in shards[1:]:
        loudness = loudness * one(*cut)
    return loudness


def gaussian(stream_key, extent, scale, most, cuts=(), kind=jnp.bfloat16):
    entries = jax.random.normal(stream_key, extent, jnp.float32) * scale
    if len(cuts) > 0:
        entries = steps_of(stream_key, extent, cuts, -0.22, 0.18) * entries
    return jnp.clip(entries, min=-most, max=most).astype(kind)


def setup_inputs(seed: int = 0) -> dict:
    key_of = jax.random.split(jax.random.key(seed), 5)
    return {
        "dry_signal": gaussian(key_of[0], (SOURCES, (NBLK + PARTITIONS) * BLOCK), 1.0, 6.0, ((0, 32),)),
        "room_spectra": gaussian(key_of[1], (SOURCES, PARTITIONS, CH, 2, BLOCK), (2 * SOURCES * PARTITIONS) ** -0.5, 0.1875, ((0, 4), (2, 8))),
        "render_slot": draw_render_slot(jax.random.fold_in(key_of[4], 71), 0),
        "decoder": gaussian(key_of[3], (CH, SPK), CH ** -0.5, 0.75),
    }


def make_tables(block_len):
    size = 2 * block_len
    rows = jnp.arange(size, dtype=jnp.int32)[:, None]
    bins = jnp.arange(block_len, dtype=jnp.int32)[None, :]
    phase = ((rows * bins) % size).astype(jnp.float32) * (2.0 * math.pi / size)
    signs = (1 - 2 * (rows % 2)).astype(jnp.float32)
    fwd_imag = jnp.where(bins == 0, signs, -jnp.sin(phase))
    fwd_table = jnp.stack([jnp.cos(phase), fwd_imag], axis=1).astype(jnp.bfloat16)
    freq = jnp.arange(block_len, dtype=jnp.int32)[:, None]
    times = jnp.arange(block_len, dtype=jnp.int32)[None, :] + block_len
    angle = ((freq * times) % size).astype(jnp.float32) * (2.0 * math.pi / size)
    weight = jnp.where(freq == 0, 1.0, 2.0).astype(jnp.float32)
    inv_real = weight * jnp.cos(angle) / size
    tsign = (1 - 2 * (times % 2)).astype(jnp.float32) / size
    inv_imag = jnp.where(freq == 0, tsign, -2.0 * jnp.sin(angle) / size)
    inv_table = jnp.stack([inv_real, inv_imag], axis=0)
    return fwd_table, inv_table


def reference(dry_signal, room_spectra, render_slot, decoder):
    blocks = dry_signal.reshape(SOURCES, NBLK + PARTITIONS, BLOCK)
    frames = jnp.concatenate([blocks[:, :-1], blocks[:, 1:]], axis=-1)
    fwd_table, inv_table = make_tables(BLOCK)
    spectra = jnp.einsum("sfn,njk->sfjk", frames.astype(jnp.float32), fwd_table.astype(jnp.float32),
                         precision=lax.Precision.HIGHEST).astype(jnp.bfloat16)
    ordered = jnp.zeros_like(spectra).at[render_slot].set(spectra)
    bin_index = jnp.arange(BLOCK, dtype=jnp.int32)
    bin_mask = (bin_index > 0).astype(jnp.float32)
    mix_real = jnp.zeros((CH, NBLK, BLOCK), jnp.float32)
    mix_imag = jnp.zeros((CH, NBLK, BLOCK), jnp.float32)
    for p in range(PARTITIONS):
        window = ordered[:, PARTITIONS - 1 - p:PARTITIONS - 1 - p + NBLK].astype(jnp.float32)
        response = room_spectra[:, p].astype(jnp.float32)
        spec_real = window[:, :, 0]
        spec_imag = window[:, :, 1]
        resp_real = response[:, :, 0]
        resp_imag = response[:, :, 1]
        resp_masked = resp_imag * bin_mask
        resp_mixed = jnp.where(bin_index == 0, resp_imag, resp_real)

        def product_sum(left, right):
            return jnp.einsum("sbk,sck->cbk", left, right, precision=lax.Precision.HIGHEST)

        mix_real = mix_real + product_sum(spec_real, resp_real) - product_sum(spec_imag, resp_masked)
        mix_imag = mix_imag + product_sum(spec_real, resp_masked) + product_sum(spec_imag, resp_mixed)
    sh_sum = jnp.einsum("cbk,km->cbm", mix_real, inv_table[0])
    sh_sum = sh_sum + jnp.einsum("cbk,km->cbm", mix_imag, inv_table[1])
    sh_signal = sh_sum.reshape(CH, NBLK * BLOCK).astype(jnp.bfloat16)
    return jnp.dot(sh_signal.T, decoder, preferred_element_type=jnp.float32).astype(jnp.bfloat16)
```

```python
import functools
import math

import jax
import jax.numpy as jnp
import ml_dtypes
import numpy as np
from jax import lax
from jax.experimental import pallas as pl
from jax.experimental.pallas import tpu as pltpu
from jax.sharding import PartitionSpec as P

BF16 = jnp.bfloat16
F32 = jnp.float32
LANES = 256
STEPS = 24
SEGS = 2
KEEP = 16


def bf16_table(values):
    return np.asarray(values, dtype=np.float32).astype(ml_dtypes.bfloat16)


@functools.lru_cache(maxsize=None)
def block_tables(block_len):
    size = 2 * block_len
    n = np.arange(block_len)[:, None]
    k = np.arange(block_len)[None, :]
    angle = ((n * k) % size) * (2.0 * math.pi / size)
    fwd_real = np.cos(angle)
    fwd_imag = np.where(k == 0, 1.0 - 2.0 * (n % 2), -np.sin(angle))
    kk = np.arange(block_len)[:, None]
    m = np.arange(block_len)[None, :] + block_len
    angle = ((kk * m) % size) * (2.0 * math.pi / size)
    weight = np.where(kk == 0, 1.0, 2.0)
    inv_real = weight * np.cos(angle) / size
    inv_imag = np.where(kk == 0, (1.0 - 2.0 * (m % 2)) / size, -2.0 * np.sin(angle) / size)
    return (
        bf16_table(np.stack([fwd_real, fwd_imag])),
        bf16_table(np.stack([inv_real, inv_imag])),
    )


@functools.lru_cache(maxsize=None)
def step_tables(parts, frames, rows):
    half = STEPS // 2
    theta = 2.0 * math.pi * (np.arange(STEPS) + 0.5) / STEPS
    first = (np.arange(STEPS) < half).astype(np.float64)[:, None]

    def forward(steps):
        cos = np.cos(theta[:, None] * steps[None, :])
        sin = np.sin(theta[:, None] * steps[None, :])
        plain = np.block([[cos, sin], [-sin, cos]])
        packed = np.block([[cos * first, cos * (1 - first)], [-sin * first, -sin * (1 - first)]])
        return plain, packed

    spec = np.zeros((2, 2, SEGS, STEPS, 2, frames))
    used = parts - 1 + KEEP
    for kind, table in enumerate(forward(np.arange(used))):
        table = table.reshape(2, STEPS, 2, used)
        for seg in range(SEGS):
            spec[kind, :, seg, :, :, seg * KEEP : seg * KEEP + used] = table
    spec = spec.reshape(2, 2 * SEGS * STEPS, 2 * frames)
    spec = np.concatenate([spec[0], spec[1]], axis=1)

    resp = np.zeros((rows, 2, STEPS, 2, rows, parts, 2))
    for kind, table in enumerate(forward(np.arange(parts))):
        table = table.reshape(2, STEPS, 2, parts).transpose(0, 1, 3, 2)
        for r in range(rows):
            resp[r, :, :, kind, r] = table
    resp = resp.reshape(rows * 2 * STEPS, 2 * rows * parts * 2)

    back = np.zeros((2, 2, SEGS, KEEP, 2, SEGS, STEPS))
    steps = np.arange(KEEP) + parts - 1
    cos = np.cos(theta[None, :] * steps[:, None]) / STEPS
    sin = np.sin(theta[None, :] * steps[:, None]) / STEPS
    firsts = first[:, 0][None, :]
    for seg in range(SEGS):
        back[0, 0, seg, :, 0, seg] = cos
        back[0, 0, seg, :, 1, seg] = -sin
        back[0, 1, seg, :, 0, seg] = sin
        back[0, 1, seg, :, 1, seg] = cos
        back[1, 0, seg, :, 0, seg] = 2 * cos * firsts
        back[1, 0, seg, :, 1, seg] = -2 * sin * firsts
        back[1, 1, seg, :, 0, seg] = 2 * cos * (1 - firsts)
        back[1, 1, seg, :, 1, seg] = -2 * sin * (1 - firsts)
    back = back.reshape(2, 2 * SEGS * KEEP, 2 * SEGS * STEPS)
    back = np.concatenate([back[0], back[1]], axis=1)
    return bf16_table(spec), bf16_table(resp), bf16_table(back)


def dot(left, right):
    return jnp.dot(left, right, preferred_element_type=F32)


def mix_kernel(pieces, rows, channels, blocks, shares, has_total, last, scal, *refs):
    refs = list(refs)
    x_refs = [refs.pop(0) for _ in range(pieces)]
    h_refs = [refs.pop(0) for _ in range(rows)]
    table_ref, spec_ref, resp_ref = [refs.pop(0) for _ in range(3)]
    total_ref = refs.pop(0) if has_total else None
    if last:
        back_ref, inv_ref = refs.pop(0), refs.pop(0)
        out_refs = [refs.pop(0) for _ in range(shares)]
    else:
        out_ref = refs.pop(0)
    s_ref, hat_ref = refs.pop(0), refs.pop(0)
    if last:
        y_ref, left_re, left_im, time_ref = refs

    step = pl.program_id(0)
    lane = lax.broadcasted_iota(jnp.int32, (1, LANES), 1) + step * LANES
    packed = (lane == 0).astype(F32)
    plain = 1.0 - packed
    packed16, plain16 = packed.astype(BF16), plain.astype(BF16)
    sign = (1 - 2 * (lane % 2)).astype(F32)

    x = jnp.concatenate([ref[...] for ref in x_refs], axis=0)
    count = x.shape[0] // rows
    spectra = []
    for j in range(2):
        one = dot(x, table_ref[j])
        spectra.append(one + sign * pltpu.roll(one, one.shape[0] - 1, axis=0))
    for r in range(rows):
        both = jnp.concatenate([s[r * count : (r + 1) * count] for s in spectra], axis=0)
        both = jnp.concatenate([both * plain, both * packed], axis=0).astype(BF16)
        s_ref[r] = dot(spec_ref[...], both)

    wide = SEGS * STEPS
    for c in range(channels):
        h = jnp.concatenate([ref[0, c] for ref in h_refs], axis=0)
        h = jnp.concatenate([h * plain16, h * packed16], axis=0)
        hat = hat_ref.at[c % 2]
        hat[...] = dot(resp_ref[...], h)
        for cut in range(LANES // 128):
            at = slice(cut * 128, (cut + 1) * 128)
            for seg in range(SEGS):
                re_rows = slice(seg * STEPS, (seg + 1) * STEPS)
                im_rows = slice(wide + seg * STEPS, wide + (seg + 1) * STEPS)
                if has_total:
                    re, im = total_ref[c, re_rows, at], total_ref[c, im_rows, at]
                else:
                    re, im = None, None
                for r in range(rows):
                    base = r * 2 * STEPS
                    h_re = hat[base : base + STEPS, at]
                    h_im = hat[base + STEPS : base + 2 * STEPS, at]
                    s_re, s_im = s_ref[r, re_rows, at], s_ref[r, im_rows, at]
                    add_re = s_re * h_re - s_im * h_im
                    add_im = s_re * h_im + s_im * h_re
                    re = add_re if re is None else re + add_re
                    im = add_im if im is None else im + add_im
                if last:
                    y_ref[re_rows, at] = re
                    y_ref[im_rows, at] = im
                else:
                    out_ref[c, re_rows, at] = re
                    out_ref[c, im_rows, at] = im
        if last:
            y = y_ref[...]
            y = jnp.concatenate([y * plain, y * packed], axis=0).astype(BF16)
            mix = dot(back_ref[...], y).astype(BF16)
            left_re[c * blocks : (c + 1) * blocks] = mix[:blocks]
            left_im[c * blocks : (c + 1) * blocks] = mix[blocks:]

    if last:
        part = dot(left_re[...], inv_ref[0]) + dot(left_im[...], inv_ref[1])
        each = blocks // shares
        spans = [
            (t, c, part[c * blocks + t * each : c * blocks + (t + 1) * each])
            for t in range(shares)
            for c in range(channels)
        ]

        @pl.when(step == 0)
        def _():
            for t, c, span in spans:
                time_ref[t, c] = span

        @pl.when(step > 0)
        def _():
            for t, c, span in spans:
                time_ref[t, c] += span

        @pl.when(step == pl.num_programs(0) - 1)
        def _():
            me = scal[rows]
            for d in range(shares):
                out_refs[d][...] = time_ref[me ^ d].astype(BF16)


def add_sources(x_list, slots, responses, total, last, shares, me):
    rows_total, channels, _, block_len = responses.shape
    parts = responses.shape[2] // 2
    rows = slots.shape[0]
    frames = x_list[0].shape[0] * len(x_list) // rows
    blocks = frames - parts
    wide = 2 * SEGS * STEPS
    table, inverse = block_tables(block_len)
    spec, resp, back = step_tables(parts, frames, rows)
    scal = jnp.concatenate([slots, me[None]]).astype(jnp.int32)
    grid = (block_len // LANES,)

    def whole(shape):
        return pl.BlockSpec(shape, lambda k, s: (0,) * len(shape))

    def row_of(i):
        return pl.BlockSpec((1, channels, 2 * parts, LANES), lambda k, s: (s[i], 0, 0, k))

    operands = list(x_list) + [responses] * rows + [jnp.asarray(table), jnp.asarray(spec), jnp.asarray(resp)]
    specs = [whole(x.shape) for x in x_list] + [row_of(i) for i in range(rows)]
    specs += [
        pl.BlockSpec((2, block_len, LANES), lambda k, s: (0, 0, k)),
        whole(spec.shape),
        whole(resp.shape),
    ]
    total_spec = pl.BlockSpec((channels, wide, LANES), lambda k, s: (0, 0, k))
    if total is not None:
        operands.append(total)
        specs.append(total_spec)
    scratch = [
        pltpu.VMEM((rows, wide, LANES), F32),
        pltpu.VMEM((2, rows * 2 * STEPS, LANES), F32),
    ]
    if last:
        operands += [jnp.asarray(back), jnp.asarray(inverse)]
        specs += [
            whole(back.shape),
            pl.BlockSpec((2, LANES, block_len), lambda k, s: (0, k, 0)),
        ]
        each = blocks // shares
        out_shape = [jax.ShapeDtypeStruct((channels, each, block_len), BF16)] * shares
        out_specs = [whole((channels, each, block_len))] * shares
        scratch += [
            pltpu.VMEM((wide, LANES), F32),
            pltpu.VMEM((channels * blocks, LANES), BF16),
            pltpu.VMEM((channels * blocks, LANES), BF16),
            pltpu.VMEM((shares, channels, each, block_len), F32),
        ]
    else:
        out_shape = jax.ShapeDtypeStruct((channels, wide, block_len), F32)
        out_specs = total_spec
    flops = 2 * block_len * (
        rows * frames * 2 * block_len + channels * rows * wide * 8 + (channels * blocks * 2 * block_len if last else 0)
    )
    body = functools.partial(
        mix_kernel, len(x_list), rows, channels, blocks, shares, total is not None, last
    )
    return pl.pallas_call(
        body,
        grid_spec=pltpu.PrefetchScalarGridSpec(
            num_scalar_prefetch=1,
            grid=grid,
            in_specs=specs,
            out_specs=out_specs,
            scratch_shapes=scratch,
        ),
        out_shape=out_shape,
        compiler_params=pltpu.CompilerParams(
            dimension_semantics=("arbitrary",), vmem_limit_bytes=40 * 2**20
        ),
        cost_estimate=pl.CostEstimate(flops=flops, bytes_accessed=12 * 2**20, transcendentals=0),
    )(scal, *operands)


def per_device(src_count, ch_count, dry_signal, room_spectra, render_slot, decoder):
    rows_total, parts, channels, _, block_len = room_spectra.shape
    own = dry_signal.shape[0]
    frames = dry_signal.shape[1] // block_len
    blocks = frames - parts
    src_me = lax.axis_index("src").astype(jnp.int32)
    ch_me = lax.axis_index("ch").astype(jnp.int32)

    x_own = dry_signal.reshape(own * frames, block_len)

    def swap(value, axis, count, flip):
        return lax.ppermute(value, axis, [(i, i ^ flip) for i in range(count)])

    lanes = [x_own] + [swap(x_own, "ch", ch_count, 2 * d) for d in range(1, ch_count // 2)]
    mates = [swap(x, "ch", ch_count, 1) for x in lanes]

    responses = room_spectra.transpose(0, 2, 1, 3, 4).reshape(
        rows_total, channels, 2 * parts, block_len
    )
    slot_local = render_slot % rows_total

    def slots_of(flip):
        start = (ch_me ^ flip) * own
        return lax.dynamic_slice(slot_local, (start,), (own,))

    total = None
    chips = ch_count // 2
    per_call = max(1, chips // 4)
    calls = chips // per_call
    for call in range(calls):
        x_list, slots = [], []
        for d in range(call * per_call, (call + 1) * per_call):
            x_list += [lanes[d], mates[d]]
            slots += [slots_of(2 * d), slots_of(2 * d + 1)]
        total = add_sources(
            x_list, jnp.concatenate(slots), responses, total, call == calls - 1, src_count, src_me
        )

    signal = total[0].astype(F32)
    for d in range(1, src_count):
        signal = signal + swap(total[d], "src", src_count, d).astype(F32)
    signal = signal.astype(BF16).reshape(channels, -1)
    gathered = lax.all_to_all(signal, "ch", split_axis=1, concat_axis=0, tiled=True)
    decoded = lax.dot_general(
        gathered, decoder, (((0,), (0,)), ((), ())), preferred_element_type=F32
    )
    return decoded.astype(BF16)


def solution(mesh):
    body = functools.partial(per_device, mesh.shape["src"], mesh.shape["ch"])
    return jax.shard_map(
        body,
        mesh=mesh,
        in_specs=(P(("src", "ch"), None), P("src", None, "ch", None, None), P("src"), P()),
        out_specs=P(("src", "ch"), None),
        check_vma=False,
    )
```

```python
import functools
import math

import jax
import jax.numpy as jnp
import ml_dtypes
import numpy as np
from jax import lax
from jax.experimental import pallas as pl
from jax.experimental.pallas import tpu as pltpu
from jax.sharding import PartitionSpec as P

BF16 = jnp.bfloat16
F32 = jnp.float32
LANES = 256
STEPS = 24
SEGS = 2
KEEP = 16


def bf16_table(values):
    return np.asarray(values, dtype=np.float32).astype(ml_dtypes.bfloat16)


@functools.lru_cache(maxsize=None)
def block_tables(block_len):
    size = 2 * block_len
    n = np.arange(block_len)[:, None]
    k = np.arange(block_len)[None, :]
    angle = ((n * k) % size) * (2.0 * math.pi / size)
    fwd_real = np.cos(angle)
    fwd_imag = np.where(k == 0, 1.0 - 2.0 * (n % 2), -np.sin(angle))
    kk = np.arange(block_len)[:, None]
    m = np.arange(block_len)[None, :] + block_len
    angle = ((kk * m) % size) * (2.0 * math.pi / size)
    weight = np.where(kk == 0, 1.0, 2.0)
    inv_real = weight * np.cos(angle) / size
    inv_imag = np.where(kk == 0, (1.0 - 2.0 * (m % 2)) / size, -2.0 * np.sin(angle) / size)
    return (
        bf16_table(np.stack([fwd_real, fwd_imag])),
        bf16_table(np.stack([inv_real, inv_imag])),
    )


@functools.lru_cache(maxsize=None)
def step_tables(parts, frames, channels):
    half = STEPS // 2
    theta = 2.0 * math.pi * (np.arange(STEPS) + 0.5) / STEPS
    first = (np.arange(STEPS) < half).astype(np.float64)[:, None]

    def forward(steps):
        cos = np.cos(theta[:, None] * steps[None, :])
        sin = np.sin(theta[:, None] * steps[None, :])
        plain = np.block([[cos, sin], [-sin, cos]])
        packed = np.block([[cos * first, cos * (1 - first)], [-sin * first, -sin * (1 - first)]])
        return plain, packed

    spec = np.zeros((2, 2, SEGS, STEPS, 2, frames))
    used = parts - 1 + KEEP
    for kind, table in enumerate(forward(np.arange(used))):
        table = table.reshape(2, STEPS, 2, used)
        for seg in range(SEGS):
            spec[kind, :, seg, :, :, seg * KEEP : seg * KEEP + used] = table
    spec = spec.reshape(2, 2 * SEGS * STEPS, 2 * frames)
    spec = np.concatenate([spec[0], spec[1]], axis=1)

    resp = np.zeros((channels, 2, STEPS, 2, parts, channels, 2))
    for kind, table in enumerate(forward(np.arange(parts))):
        table = table.reshape(2, STEPS, 2, parts).transpose(0, 1, 3, 2)
        for c in range(channels):
            resp[c, :, :, kind, :, c] = table
    resp = resp.reshape(channels * 2 * STEPS, 2 * parts * channels * 2)

    back = np.zeros((2, 2, SEGS, KEEP, 2, SEGS, STEPS))
    steps = np.arange(KEEP) + parts - 1
    cos = np.cos(theta[None, :] * steps[:, None]) / STEPS
    sin = np.sin(theta[None, :] * steps[:, None]) / STEPS
    firsts = first[:, 0][None, :]
    for seg in range(SEGS):
        back[0, 0, seg, :, 0, seg] = cos
        back[0, 0, seg, :, 1, seg] = -sin
        back[0, 1, seg, :, 0, seg] = sin
        back[0, 1, seg, :, 1, seg] = cos
        back[1, 0, seg, :, 0, seg] = 2 * cos * firsts
        back[1, 0, seg, :, 1, seg] = -2 * sin * firsts
        back[1, 1, seg, :, 0, seg] = 2 * cos * (1 - firsts)
        back[1, 1, seg, :, 1, seg] = -2 * sin * (1 - firsts)
    back = back.reshape(2, 2 * SEGS * KEEP, 2 * SEGS * STEPS)
    back = np.concatenate([back[0], back[1]], axis=1)
    return bf16_table(spec), bf16_table(resp), bf16_table(back)


def dot(left, right):
    return jnp.dot(left, right, preferred_element_type=F32)


def lane_masks(start, width):
    lane = lax.broadcasted_iota(jnp.int32, (1, width), 1) + start
    packed = (lane == 0).astype(F32)
    sign = (1 - 2 * (lane % 2)).astype(F32)
    return 1.0 - packed, packed, sign


def response_kernel(rows, bins, room_ref, table_ref, hat_ref):
    depth = room_ref.shape[1] * room_ref.shape[2] * 2
    flat = room_ref.reshape(rows, depth, bins)
    plain, packed, _ = lane_masks(0, LANES)
    plain, packed = plain.astype(BF16), packed.astype(BF16)

    def one(r, carry):
        for step in range(bins // LANES):
            at = slice(step * LANES, (step + 1) * LANES)
            h = flat[r, :, at]
            if step == 0:
                h = jnp.concatenate([h * plain, h * packed], axis=0)
                hat = dot(table_ref[...], h)
            else:
                hat = dot(table_ref[:, :depth], h)
            hat_ref[r, :, at] = hat.astype(BF16)
        return carry

    lax.fori_loop(0, rows, one, 0)


def transform_responses(room):
    rows, parts, channels, _, bins = room.shape
    _, resp, _ = step_tables(parts, parts + SEGS * KEEP, channels)
    vmem = pl.BlockSpec(memory_space=pltpu.VMEM)
    flops = 2 * rows * channels * 2 * STEPS * parts * channels * 2 * bins
    return pl.pallas_call(
        functools.partial(response_kernel, rows, bins),
        in_specs=[vmem, vmem],
        out_specs=vmem,
        out_shape=jax.ShapeDtypeStruct((rows, channels * 2 * STEPS, bins), BF16),
        compiler_params=pltpu.CompilerParams(vmem_limit_bytes=24 * 2**20),
        cost_estimate=pl.CostEstimate(flops=flops, bytes_accessed=16 * 2**20, transcendentals=0),
    )(room, jnp.asarray(resp))


def mix_kernel(pieces, rows, channels, blocks, shares, has_total, last, scal, *refs):
    refs = list(refs)
    x_refs = [refs.pop(0) for _ in range(pieces)]
    hat_ref, table_ref, spec_ref = [refs.pop(0) for _ in range(3)]
    total_ref = refs.pop(0) if has_total else None
    if last:
        back_ref, inv_ref = refs.pop(0), refs.pop(0)
        out_refs = [refs.pop(0) for _ in range(shares)]
    else:
        out_ref = refs.pop(0)
    s_ref = refs.pop(0)
    if last:
        y_ref, left_re, left_im, time_ref = refs

    bins = table_ref.shape[2]
    wide = SEGS * STEPS
    x = jnp.concatenate([ref[...] for ref in x_refs], axis=0)
    count = x.shape[0] // rows

    def bin_step(step, carry):
        start = pl.multiple_of(step * LANES, LANES)
        here = pl.ds(start, LANES)
        plain, packed, sign = lane_masks(start, LANES)
        spectra = []
        for j in range(2):
            one = dot(x, table_ref[j, :, here])
            spectra.append(one + sign * pltpu.roll(one, one.shape[0] - 1, axis=0))
        for r in range(rows):
            both = jnp.concatenate([s[r * count : (r + 1) * count] for s in spectra], axis=0)
            both = jnp.concatenate([both * plain, both * packed], axis=0).astype(BF16)
            s_ref[r] = dot(spec_ref[...], both)

        for c in range(channels):
            for cut in range(LANES // 128):
                at = slice(cut * 128, (cut + 1) * 128)
                far = pl.ds(pl.multiple_of(start + cut * 128, 128), 128)
                for seg in range(SEGS):
                    re_rows = slice(seg * STEPS, (seg + 1) * STEPS)
                    im_rows = slice(wide + seg * STEPS, wide + (seg + 1) * STEPS)
                    if has_total:
                        re, im = total_ref[c, re_rows, far], total_ref[c, im_rows, far]
                    else:
                        re, im = None, None
                    for r in range(rows):
                        hat = hat_ref[scal[r], c * 2 * STEPS : (c + 1) * 2 * STEPS, far].astype(F32)
                        h_re, h_im = hat[:STEPS], hat[STEPS:]
                        s_re, s_im = s_ref[r, re_rows, at], s_ref[r, im_rows, at]
                        add_re = s_re * h_re - s_im * h_im
                        add_im = s_re * h_im + s_im * h_re
                        re = add_re if re is None else re + add_re
                        im = add_im if im is None else im + add_im
                    if last:
                        y_ref[re_rows, at] = re
                        y_ref[im_rows, at] = im
                    else:
                        out_ref[c, re_rows, far] = re
                        out_ref[c, im_rows, far] = im
            if last:
                y = y_ref[...]
                y = jnp.concatenate([y * plain, y * packed], axis=0).astype(BF16)
                mix = dot(back_ref[...], y).astype(BF16)
                left_re[c * blocks : (c + 1) * blocks, here] = mix[:blocks]
                left_im[c * blocks : (c + 1) * blocks, here] = mix[blocks:]
        return carry

    lax.fori_loop(0, bins // LANES, bin_step, 0)
    if last:
        each = blocks // shares

        def time_step(step, carry):
            here = pl.ds(pl.multiple_of(step * LANES, LANES), LANES)
            part = dot(left_re[...], inv_ref[0, :, here]) + dot(left_im[...], inv_ref[1, :, here])
            for t in range(shares):
                for c in range(channels):
                    row = c * blocks + t * each
                    time_ref[t, c, :, here] = part[row : row + each]
            return carry

        lax.fori_loop(0, bins // LANES, time_step, 0)
        me = scal[rows]
        for d in range(shares):
            out_refs[d][...] = time_ref[me ^ d].astype(BF16)


def add_sources(x_list, slots, hat, total, last, shares, me, channels, parts):
    bins = hat.shape[2]
    rows = slots.shape[0]
    frames = x_list[0].shape[0] * len(x_list) // rows
    blocks = frames - parts
    wide = 2 * SEGS * STEPS
    table, inverse = block_tables(bins)
    spec, _, back = step_tables(parts, frames, channels)
    scal = jnp.concatenate([slots, me[None]]).astype(jnp.int32)
    vmem = pl.BlockSpec(memory_space=pltpu.VMEM)

    operands = [scal] + list(x_list) + [hat, jnp.asarray(table), jnp.asarray(spec)]
    aliases = {}
    if total is not None:
        if not last:
            aliases = {len(operands): 0}
        operands.append(total)
    scratch = [pltpu.VMEM((rows, wide, LANES), F32)]
    if last:
        operands += [jnp.asarray(back), jnp.asarray(inverse)]
        each = blocks // shares
        out_shape = [jax.ShapeDtypeStruct((channels, each, bins), BF16)] * shares
        scratch += [
            pltpu.VMEM((wide, LANES), F32),
            pltpu.VMEM((channels * blocks, bins), BF16),
            pltpu.VMEM((channels * blocks, bins), BF16),
            pltpu.VMEM((shares, channels, each, bins), F32),
        ]
    else:
        out_shape = jax.ShapeDtypeStruct((channels, wide, bins), F32)
    flops = 2 * bins * (
        rows * frames * 2 * bins + channels * rows * wide * 16 + (channels * blocks * 2 * bins if last else 0)
    )
    body = functools.partial(
        mix_kernel, len(x_list), rows, channels, blocks, shares, total is not None, last
    )
    return pl.pallas_call(
        body,
        in_specs=[pl.BlockSpec(memory_space=pltpu.SMEM)] + [vmem] * (len(operands) - 1),
        out_specs=[vmem] * shares if last else vmem,
        out_shape=out_shape,
        scratch_shapes=scratch,
        input_output_aliases=aliases,
        compiler_params=pltpu.CompilerParams(vmem_limit_bytes=16 * 2**20),
        cost_estimate=pl.CostEstimate(flops=flops, bytes_accessed=8 * 2**20, transcendentals=0),
    )(*operands)


def per_device(src_count, ch_count, dry_signal, room_spectra, render_slot, decoder):
    rows_total, parts, channels, _, block_len = room_spectra.shape
    own = dry_signal.shape[0]
    frames = dry_signal.shape[1] // block_len
    blocks = frames - parts
    src_me = lax.axis_index("src").astype(jnp.int32)
    ch_me = lax.axis_index("ch").astype(jnp.int32)

    x_own = dry_signal.reshape(own * frames, block_len)

    def swap(value, axis, count, flip):
        return lax.ppermute(value, axis, [(i, i ^ flip) for i in range(count)])

    lanes = [x_own] + [swap(x_own, "ch", ch_count, 2 * d) for d in range(1, ch_count // 2)]
    mates = [swap(x, "ch", ch_count, 1) for x in lanes]

    hat = transform_responses(room_spectra)
    slot_local = render_slot % rows_total

    def slots_of(flip):
        start = (ch_me ^ flip) * own
        return lax.dynamic_slice(slot_local, (start,), (own,))

    total = None
    chips = ch_count // 2
    per_call = max(1, chips // 4)
    calls = chips // per_call
    for call in range(calls):
        x_list, slots = [], []
        for d in range(call * per_call, (call + 1) * per_call):
            x_list += [lanes[d], mates[d]]
            slots += [slots_of(2 * d), slots_of(2 * d + 1)]
        total = add_sources(
            x_list,
            jnp.concatenate(slots),
            hat,
            total,
            call == calls - 1,
            src_count,
            src_me,
            channels,
            parts,
        )

    signal = total[0].astype(F32)
    for d in range(1, src_count):
        signal = signal + swap(total[d], "src", src_count, d).astype(F32)
    signal = signal.astype(BF16).reshape(channels, -1)
    gathered = lax.all_to_all(signal, "ch", split_axis=1, concat_axis=0, tiled=True)
    decoded = lax.dot_general(
        gathered, decoder, (((0,), (0,)), ((), ())), preferred_element_type=F32
    )
    return decoded.astype(BF16)


def solution(mesh):
    body = functools.partial(per_device, mesh.shape["src"], mesh.shape["ch"])
    return jax.shard_map(
        body,
        mesh=mesh,
        in_specs=(P(("src", "ch"), None), P("src", None, "ch", None, None), P("src"), P()),
        out_specs=P(("src", "ch"), None),
        check_vma=False,
    )
```

```python
import functools
import math

import jax
import jax.numpy as jnp
import ml_dtypes
import numpy as np
from jax import lax
from jax.experimental import pallas as pl
from jax.experimental.pallas import tpu as pltpu
from jax.sharding import PartitionSpec as P

BF16 = jnp.bfloat16
F32 = jnp.float32
LANES = 256
STEPS = 24
SEGS = 2
KEEP = 16


def bf16_table(values):
    return np.asarray(values, dtype=np.float32).astype(ml_dtypes.bfloat16)


@functools.lru_cache(maxsize=None)
def block_tables(block_len):
    size = 2 * block_len
    n = np.arange(block_len)[:, None]
    k = np.arange(block_len)[None, :]
    angle = ((n * k) % size) * (2.0 * math.pi / size)
    fwd_real = np.cos(angle)
    fwd_imag = np.where(k == 0, 1.0 - 2.0 * (n % 2), -np.sin(angle))
    kk = np.arange(block_len)[:, None]
    m = np.arange(block_len)[None, :] + block_len
    angle = ((kk * m) % size) * (2.0 * math.pi / size)
    weight = np.where(kk == 0, 1.0, 2.0)
    inv_real = weight * np.cos(angle) / size
    inv_imag = np.where(kk == 0, (1.0 - 2.0 * (m % 2)) / size, -2.0 * np.sin(angle) / size)
    return (
        bf16_table(np.stack([fwd_real, fwd_imag])),
        bf16_table(np.stack([inv_real, inv_imag])),
    )


@functools.lru_cache(maxsize=None)
def step_tables(parts, frames, channels):
    half = STEPS // 2
    theta = 2.0 * math.pi * (np.arange(STEPS) + 0.5) / STEPS
    first = (np.arange(STEPS) < half).astype(np.float64)[:, None]

    def forward(steps):
        cos = np.cos(theta[:, None] * steps[None, :])
        sin = np.sin(theta[:, None] * steps[None, :])
        plain = np.block([[cos, sin], [-sin, cos]])
        packed = np.block([[cos * first, cos * (1 - first)], [-sin * first, -sin * (1 - first)]])
        return plain, packed

    spec = np.zeros((2, SEGS, 2, 2, STEPS, 2, frames))
    used = parts - 1 + KEEP
    for kind, table in enumerate(forward(np.arange(used))):
        table = table.reshape(2, 1, STEPS, 2, used)
        for seg in range(SEGS):
            spec[kind, seg, :, :, :, :, seg * KEEP : seg * KEEP + used] = table
    spec = spec.reshape(2, SEGS * 4 * STEPS, 2 * frames)
    spec = np.concatenate([spec[0], spec[1]], axis=1)

    resp = np.zeros((channels // 2, 2, 2, STEPS, 2, parts, channels, 2))
    for kind, table in enumerate(forward(np.arange(parts))):
        table = table.reshape(2, STEPS, 2, parts).transpose(0, 1, 3, 2)
        for c in range(channels):
            resp[c // 2, :, c % 2, :, kind, :, c] = table
    resp = resp.reshape(channels * 2 * STEPS, 2 * parts * channels * 2)

    back = np.zeros((2, 2, 2, SEGS, KEEP, SEGS, 2, 2, STEPS))
    steps = np.arange(KEEP) + parts - 1
    cos = np.cos(theta[None, :] * steps[:, None]) / STEPS
    sin = np.sin(theta[None, :] * steps[:, None]) / STEPS
    firsts = first[:, 0][None, :]
    for seg in range(SEGS):
        for c in range(2):
            back[0, c, 0, seg, :, seg, 0, c] = cos
            back[0, c, 0, seg, :, seg, 1, c] = -sin
            back[0, c, 1, seg, :, seg, 0, c] = sin
            back[0, c, 1, seg, :, seg, 1, c] = cos
            back[1, c, 0, seg, :, seg, 0, c] = 2 * cos * firsts
            back[1, c, 0, seg, :, seg, 1, c] = -2 * sin * firsts
            back[1, c, 1, seg, :, seg, 0, c] = 2 * cos * (1 - firsts)
            back[1, c, 1, seg, :, seg, 1, c] = -2 * sin * (1 - firsts)
    back = back.reshape(2, 4 * SEGS * KEEP, 4 * SEGS * STEPS)
    return bf16_table(spec), bf16_table(resp), bf16_table(back)


def dot(left, right):
    return jnp.dot(left, right, preferred_element_type=F32)


def lane_masks(start, width):
    lane = lax.broadcasted_iota(jnp.int32, (1, width), 1) + start
    packed = (lane == 0).astype(F32)
    sign = (1 - 2 * (lane % 2)).astype(F32)
    return 1.0 - packed, packed, sign


def response_kernel(rows, bins, room_hbm, table_ref, hat_ref, room_ref, sems):
    depth = room_ref.shape[1] * room_ref.shape[2] * 2
    flat = room_ref.reshape(rows, depth, bins)
    plain, packed, _ = lane_masks(0, LANES)
    plain, packed = plain.astype(BF16), packed.astype(BF16)

    def copy(r):
        return pltpu.make_async_copy(room_hbm.at[r], room_ref.at[r], sems.at[r])

    for r in range(rows):
        copy(r).start()

    def one(r, carry):
        copy(r).wait()
        for step in range(bins // LANES):
            at = slice(step * LANES, (step + 1) * LANES)
            h = flat[r, :, at]
            if step == 0:
                h = jnp.concatenate([h * plain, h * packed], axis=0)
                hat = dot(table_ref[...], h)
            else:
                hat = dot(table_ref[:, :depth], h)
            hat_ref[r, :, at] = hat.astype(BF16)
        return carry

    lax.fori_loop(0, rows, one, 0)


def transform_responses(room):
    rows, parts, channels, _, bins = room.shape
    _, resp, _ = step_tables(parts, parts + SEGS * KEEP, channels)
    vmem = pl.BlockSpec(memory_space=pltpu.VMEM)
    flops = 2 * rows * channels * 2 * STEPS * parts * channels * 2 * bins
    return pl.pallas_call(
        functools.partial(response_kernel, rows, bins),
        in_specs=[pl.BlockSpec(memory_space=pl.ANY), vmem],
        out_specs=vmem,
        out_shape=jax.ShapeDtypeStruct((rows, channels * 2 * STEPS, bins), BF16),
        scratch_shapes=[pltpu.VMEM(room.shape, BF16), pltpu.SemaphoreType.DMA((rows,))],
        compiler_params=pltpu.CompilerParams(vmem_limit_bytes=24 * 2**20),
        cost_estimate=pl.CostEstimate(flops=flops, bytes_accessed=16 * 2**20, transcendentals=0),
    )(room, jnp.asarray(resp))


def mix_kernel(pieces, rows, channels, blocks, shares, has_total, last, scal, *refs):
    refs = list(refs)
    x_refs = [refs.pop(0) for _ in range(pieces)]
    hat_ref, table_ref, spec_ref = [refs.pop(0) for _ in range(3)]
    total_ref = refs.pop(0) if has_total else None
    if last:
        back_ref, inv_ref = refs.pop(0), refs.pop(0)
        out_refs = [refs.pop(0) for _ in range(shares)]
    else:
        out_ref = refs.pop(0)
    s_ref = refs.pop(0)
    if last:
        y_ref, left_re, left_im, time_ref = refs

    bins = table_ref.shape[2]
    half = 2 * STEPS
    x = jnp.concatenate([ref[...] for ref in x_refs], axis=0)
    count = x.shape[0] // rows
    cols = 2 * count

    def spectra_step(step):
        here = slice(step * LANES, (step + 1) * LANES)
        plain, packed, sign = lane_masks(step * LANES, LANES)
        spectra = []
        for j in range(2):
            one = dot(x, table_ref[j, :, here])
            spectra.append(one + sign * pltpu.roll(one, one.shape[0] - 1, axis=0))
        for r in range(rows):
            both = jnp.concatenate([s[r * count : (r + 1) * count] for s in spectra], axis=0)
            if step == 0:
                both = jnp.concatenate([both * plain, both * packed], axis=0).astype(BF16)
                s_ref[step, r] = dot(spec_ref[...], both).astype(BF16)
            else:
                s_ref[step, r] = dot(spec_ref[:, :cols], both.astype(BF16)).astype(BF16)

    def product_step(step):
        for pair in range(channels // 2):
            for cut in range(LANES // 128):
                at = slice(cut * 128, (cut + 1) * 128)
                far = slice(step * LANES + cut * 128, step * LANES + (cut + 1) * 128)
                base = pair * 2 * half
                hats = [
                    (hat_ref[scal[r], base : base + half, far], hat_ref[scal[r], base + half : base + 2 * half, far])
                    for r in range(rows)
                ]
                for seg in range(SEGS):
                    re_rows = slice(2 * seg * half, (2 * seg + 1) * half)
                    im_rows = slice((2 * seg + 1) * half, (2 * seg + 2) * half)
                    re, im = None, None
                    for r in range(rows):
                        h_re, h_im = hats[r]
                        s_re, s_im = s_ref[step, r, re_rows, at], s_ref[step, r, im_rows, at]
                        add_re = s_re * h_re - s_im * h_im
                        add_im = s_re * h_im + s_im * h_re
                        re = add_re if re is None else re + add_re
                        im = add_im if im is None else im + add_im
                    re, im = re.astype(F32), im.astype(F32)
                    if has_total:
                        re, im = re + total_ref[pair, re_rows, far], im + total_ref[pair, im_rows, far]
                    if last:
                        y_ref[step, pair, re_rows, at] = re.astype(BF16)
                        y_ref[step, pair, im_rows, at] = im.astype(BF16)
                    else:
                        out_ref[pair, re_rows, far] = re
                        out_ref[pair, im_rows, far] = im
            if last:
                here = slice(step * LANES, (step + 1) * LANES)
                y = y_ref[step, pair]
                if step == 0:
                    plain, packed, _ = lane_masks(0, LANES)
                    mix = dot(back_ref[0], y * plain.astype(BF16)) + dot(back_ref[1], y * packed.astype(BF16))
                else:
                    mix = dot(back_ref[0], y)
                mix = mix.astype(BF16)
                for c in range(2):
                    rows_to = slice((2 * pair + c) * blocks, (2 * pair + c + 1) * blocks)
                    left_re[rows_to, here] = mix[2 * c * blocks : (2 * c + 1) * blocks]
                    left_im[rows_to, here] = mix[(2 * c + 1) * blocks : (2 * c + 2) * blocks]

    steps = bins // LANES
    spectra_step(0)
    for step in range(steps):
        if step + 1 < steps:
            spectra_step(step + 1)
        product_step(step)

    if last:
        each = blocks // shares
        for step in range(steps):
            here = slice(step * LANES, (step + 1) * LANES)
            part = dot(left_re[...], inv_ref[0, :, here]) + dot(left_im[...], inv_ref[1, :, here])
            for t in range(shares):
                for c in range(channels):
                    row = c * blocks + t * each
                    time_ref[t, c, :, here] = part[row : row + each]
        me = scal[rows]
        for d in range(shares):
            out_refs[d][...] = time_ref[me ^ d].astype(BF16)


def add_sources(x_list, slots, hat, total, last, shares, me, channels, parts):
    bins = hat.shape[2]
    rows = slots.shape[0]
    frames = x_list[0].shape[0] * len(x_list) // rows
    blocks = frames - parts
    wide = 2 * SEGS * STEPS
    table, inverse = block_tables(bins)
    spec, _, back = step_tables(parts, frames, channels)
    scal = jnp.concatenate([slots, me[None]]).astype(jnp.int32)
    vmem = pl.BlockSpec(memory_space=pltpu.VMEM)

    operands = [scal] + list(x_list) + [hat, jnp.asarray(table), jnp.asarray(spec)]
    aliases = {}
    if total is not None:
        if not last:
            aliases = {len(operands): 0}
        operands.append(total)
    scratch = [pltpu.VMEM((bins // LANES, rows, 2 * wide, LANES), BF16)]
    if last:
        operands += [jnp.asarray(back), jnp.asarray(inverse)]
        each = blocks // shares
        out_shape = [jax.ShapeDtypeStruct((channels, each, bins), BF16)] * shares
        scratch += [
            pltpu.VMEM((bins // LANES, channels // 2, 2 * wide, LANES), BF16),
            pltpu.VMEM((channels * blocks, bins), BF16),
            pltpu.VMEM((channels * blocks, bins), BF16),
            pltpu.VMEM((shares, channels, each, bins), F32),
        ]
    else:
        out_shape = jax.ShapeDtypeStruct((channels // 2, 2 * wide, bins), F32)
    flops = 2 * bins * (
        rows * frames * 2 * bins + channels * rows * wide * 16 + (channels * blocks * 2 * bins if last else 0)
    )
    body = functools.partial(
        mix_kernel, len(x_list), rows, channels, blocks, shares, total is not None, last
    )
    return pl.pallas_call(
        body,
        in_specs=[pl.BlockSpec(memory_space=pltpu.SMEM)] + [vmem] * (len(operands) - 1),
        out_specs=[vmem] * shares if last else vmem,
        out_shape=out_shape,
        scratch_shapes=scratch,
        input_output_aliases=aliases,
        compiler_params=pltpu.CompilerParams(vmem_limit_bytes=20 * 2**20),
        cost_estimate=pl.CostEstimate(flops=flops, bytes_accessed=8 * 2**20, transcendentals=0),
    )(*operands)


def sum_kernel(count, each, me_ref, *refs):
    parts, outs, sum_ref = refs[:count], refs[count:-1], refs[-1]
    total = parts[0][...].astype(F32)
    for part in parts[1:]:
        total = total + part[...].astype(F32)
    sum_ref[...] = total
    for d in range(each):
        outs[d][...] = sum_ref[:, pl.ds(me_ref[0] ^ d, 1), :].reshape(outs[d].shape).astype(BF16)


def sum_groups(parts, me):
    channels, each, bins = parts[0].shape
    vmem = pl.BlockSpec(memory_space=pltpu.VMEM)
    return pl.pallas_call(
        functools.partial(sum_kernel, len(parts), each),
        in_specs=[pl.BlockSpec(memory_space=pltpu.SMEM)] + [vmem] * len(parts),
        out_specs=[vmem] * each,
        out_shape=[jax.ShapeDtypeStruct((channels, bins), BF16)] * each,
        scratch_shapes=[pltpu.VMEM(parts[0].shape, F32)],
        compiler_params=pltpu.CompilerParams(vmem_limit_bytes=8 * 2**20),
    )(me[None], *parts)


def per_device(src_count, ch_count, dry_signal, room_spectra, render_slot, decoder):
    rows_total, parts, channels, _, block_len = room_spectra.shape
    own = dry_signal.shape[0]
    frames = dry_signal.shape[1] // block_len
    blocks = frames - parts
    src_me = lax.axis_index("src").astype(jnp.int32)
    ch_me = lax.axis_index("ch").astype(jnp.int32)

    x_own = dry_signal.reshape(own * frames, block_len)

    def swap(value, axis, count, flip):
        return lax.ppermute(value, axis, [(i, i ^ flip) for i in range(count)])

    lanes = [x_own] + [swap(x_own, "ch", ch_count, 2 * d) for d in range(1, ch_count // 2)]
    mates = [swap(x, "ch", ch_count, 1) for x in lanes]

    hat = transform_responses(room_spectra)
    slot_local = render_slot % rows_total

    row = jnp.arange(ch_count * channels, dtype=jnp.int32)
    takes = ((row // channels) ^ ch_me) * channels + row % channels
    order = (takes[:, None] == row[None, :]).astype(BF16)
    own_order = dot(order, decoder).astype(BF16)

    def slots_of(flip):
        start = (ch_me ^ flip) * own
        return lax.dynamic_slice(slot_local, (start,), (own,))

    total = None
    chips = ch_count // 2
    per_call = max(1, chips // 4)
    calls = chips // per_call
    for call in range(calls):
        x_list, slots = [], []
        for d in range(call * per_call, (call + 1) * per_call):
            x_list += [lanes[d], mates[d]]
            slots += [slots_of(2 * d), slots_of(2 * d + 1)]
        total = add_sources(
            x_list,
            jnp.concatenate(slots),
            hat,
            total,
            call == calls - 1,
            src_count,
            src_me,
            channels,
            parts,
        )

    parts_in = [total[0]] + [swap(total[d], "src", src_count, d) for d in range(1, src_count)]
    each = blocks // src_count
    if each == ch_count:
        pieces = sum_groups(parts_in, ch_me)
        pieces = [pieces[0]] + [swap(pieces[d], "ch", ch_count, d) for d in range(1, ch_count)]
        gathered = jnp.concatenate(pieces, axis=0)
        matrix = own_order
    else:
        signal = parts_in[0].astype(F32)
        for part in parts_in[1:]:
            signal = signal + part.astype(F32)
        signal = signal.astype(BF16).reshape(channels, -1)
        gathered = lax.all_to_all(signal, "ch", split_axis=1, concat_axis=0, tiled=True)
        matrix = decoder
    decoded = lax.dot_general(
        gathered, matrix, (((0,), (0,)), ((), ())), preferred_element_type=F32
    )
    return decoded.astype(BF16)


def solution(mesh):
    body = functools.partial(per_device, mesh.shape["src"], mesh.shape["ch"])
    return jax.shard_map(
        body,
        mesh=mesh,
        in_specs=(P(("src", "ch"), None), P("src", None, "ch", None, None), P("src"), P()),
        out_specs=P(("src", "ch"), None),
        check_vma=False,
    )
```

```python
import functools
import math

import jax
import jax.numpy as jnp
import ml_dtypes
import numpy as np
from jax import lax
from jax.experimental import pallas as pl
from jax.experimental.pallas import tpu as pltpu
from jax.sharding import PartitionSpec as P

BF16 = jnp.bfloat16
F32 = jnp.float32
LANES = 256
SLAB = 128
GROUP = 4
STEPS = 24
SEGS = 2
KEEP = 16


def bf16_table(values):
    return np.asarray(values, dtype=np.float32).astype(ml_dtypes.bfloat16)


@functools.lru_cache(maxsize=None)
def block_tables(block_len):
    size = 2 * block_len
    n = np.arange(block_len)[:, None]
    k = np.arange(block_len)[None, :]
    angle = ((n * k) % size) * (2.0 * math.pi / size)
    fwd_real = np.cos(angle)
    fwd_imag = np.where(k == 0, 1.0 - 2.0 * (n % 2), -np.sin(angle))
    kk = np.arange(block_len)[:, None]
    m = np.arange(block_len)[None, :] + block_len
    angle = ((kk * m) % size) * (2.0 * math.pi / size)
    weight = np.where(kk == 0, 1.0, 2.0)
    inv_real = weight * np.cos(angle) / size
    inv_imag = np.where(kk == 0, (1.0 - 2.0 * (m % 2)) / size, -2.0 * np.sin(angle) / size)
    def slabs(pair):
        return bf16_table(np.stack(pair).reshape(2, block_len, -1, SLAB).transpose(0, 2, 1, 3))

    return slabs([fwd_real, fwd_imag]), slabs([inv_real, inv_imag])


@functools.lru_cache(maxsize=None)
def step_tables(parts, frames, channels):
    half = STEPS // 2
    theta = 2.0 * math.pi * (np.arange(STEPS) + 0.5) / STEPS
    first = (np.arange(STEPS) < half).astype(np.float64)[:, None]

    def forward(steps):
        cos = np.cos(theta[:, None] * steps[None, :])
        sin = np.sin(theta[:, None] * steps[None, :])
        plain = np.block([[cos, sin], [-sin, cos]])
        packed = np.block([[cos * first, cos * (1 - first)], [-sin * first, -sin * (1 - first)]])
        return plain, packed

    spec = np.zeros((2, SEGS, 2, 2, STEPS, 2, frames))
    used = parts - 1 + KEEP
    for kind, table in enumerate(forward(np.arange(used))):
        table = table.reshape(2, 1, STEPS, 2, used)
        for seg in range(SEGS):
            spec[kind, seg, :, :, :, :, seg * KEEP : seg * KEEP + used] = table
    spec = spec.reshape(2, SEGS * 4 * STEPS, 2 * frames)
    spec = np.concatenate([spec[0], spec[1]], axis=1)

    resp = np.zeros((channels // 2, 2, 2, STEPS, 2, parts, channels, 2))
    for kind, table in enumerate(forward(np.arange(parts))):
        table = table.reshape(2, STEPS, 2, parts).transpose(0, 1, 3, 2)
        for c in range(channels):
            resp[c // 2, :, c % 2, :, kind, :, c] = table
    resp = resp.reshape(channels * 2 * STEPS, 2 * parts * channels * 2)

    back = np.zeros((2, 2, 2, SEGS, KEEP, SEGS, 2, 2, STEPS))
    steps = np.arange(KEEP) + parts - 1
    cos = np.cos(theta[None, :] * steps[:, None]) / STEPS
    sin = np.sin(theta[None, :] * steps[:, None]) / STEPS
    firsts = first[:, 0][None, :]
    for seg in range(SEGS):
        for c in range(2):
            back[0, c, 0, seg, :, seg, 0, c] = cos
            back[0, c, 0, seg, :, seg, 1, c] = -sin
            back[0, c, 1, seg, :, seg, 0, c] = sin
            back[0, c, 1, seg, :, seg, 1, c] = cos
            back[1, c, 0, seg, :, seg, 0, c] = 2 * cos * firsts
            back[1, c, 0, seg, :, seg, 1, c] = -2 * sin * firsts
            back[1, c, 1, seg, :, seg, 0, c] = 2 * cos * (1 - firsts)
            back[1, c, 1, seg, :, seg, 1, c] = -2 * sin * (1 - firsts)
    back = back.reshape(2, 4 * SEGS * KEEP, 4 * SEGS * STEPS)
    return bf16_table(spec), bf16_table(resp), bf16_table(back)


def dot(left, right):
    return jnp.dot(left, right, preferred_element_type=F32)


def lane_masks(start, width):
    lane = lax.broadcasted_iota(jnp.int32, (1, width), 1) + start
    packed = (lane == 0).astype(F32)
    sign = (1 - 2 * (lane % 2)).astype(F32)
    return 1.0 - packed, packed, sign


def two_slabs(ref, step, *index):
    first = step * (LANES // SLAB)
    return jnp.concatenate([ref[(*index, first + i)] for i in range(LANES // SLAB)], axis=-1)


def response_kernel(rows, bins, room_hbm, table_ref, hat_ref, room_ref, sems):
    slabs = bins // SLAB
    depth = room_ref.shape[2] * room_ref.shape[3] * 2
    flat = room_ref.reshape(rows, slabs, depth, SLAB)
    plain, packed, _ = lane_masks(0, LANES)
    plain, packed = plain.astype(BF16), packed.astype(BF16)

    def copies(r):
        return [
            pltpu.make_async_copy(
                room_hbm.at[r, :, :, :, pl.ds(i * SLAB, SLAB)], room_ref.at[r, i], sems.at[r, i]
            )
            for i in range(slabs)
        ]

    for r in range(rows):
        for copy in copies(r):
            copy.start()

    def one(r, carry):
        for copy in copies(r):
            copy.wait()
        for step in range(bins // LANES):
            h = two_slabs(flat, step, r)
            if step == 0:
                h = jnp.concatenate([h * plain, h * packed], axis=0)
                hat = dot(table_ref[...], h)
            else:
                hat = dot(table_ref[:, :depth], h)
            hat = hat.astype(BF16)
            for i in range(LANES // SLAB):
                hat_ref[r, step * (LANES // SLAB) + i] = hat[:, i * SLAB : (i + 1) * SLAB]
        return carry

    lax.fori_loop(0, rows, one, 0)


def transform_responses(room):
    rows, parts, channels, _, bins = room.shape
    slabs = bins // SLAB
    _, resp, _ = step_tables(parts, parts + SEGS * KEEP, channels)
    vmem = pl.BlockSpec(memory_space=pltpu.VMEM)
    flops = 2 * rows * channels * 2 * STEPS * parts * channels * 2 * bins
    return pl.pallas_call(
        functools.partial(response_kernel, rows, bins),
        in_specs=[pl.BlockSpec(memory_space=pltpu.HBM), vmem],
        out_specs=vmem,
        out_shape=jax.ShapeDtypeStruct((rows, slabs, channels * 2 * STEPS, SLAB), BF16),
        scratch_shapes=[
            pltpu.VMEM((rows, slabs, parts, channels, 2, SLAB), BF16),
            pltpu.SemaphoreType.DMA((rows, slabs)),
        ],
        compiler_params=pltpu.CompilerParams(vmem_limit_bytes=24 * 2**20),
        cost_estimate=pl.CostEstimate(flops=flops, bytes_accessed=16 * 2**20, transcendentals=0),
    )(room, jnp.asarray(resp))


def mix_kernel(flips, own, channels, blocks, shares, has_total, last, me_ref, slot_ref, *refs):
    refs = list(refs)
    x_refs = [refs.pop(0) for _ in flips]
    hat_ref, table_ref, spec_ref = [refs.pop(0) for _ in range(3)]
    total_ref = refs.pop(0) if has_total else None
    if last:
        back_ref, inv_ref = refs.pop(0), refs.pop(0)
        out_refs = [refs.pop(0) for _ in range(shares)]
    else:
        out_ref = refs.pop(0)
    s_ref = refs.pop(0)
    if last:
        y_ref, left_re, left_im, time_ref = refs

    slabs = hat_ref.shape[1]
    bins = slabs * SLAB
    steps = bins // LANES
    rows = own * len(flips)
    half = 2 * STEPS
    x = jnp.concatenate([ref[...] for ref in x_refs], axis=0)
    count = x.shape[0] // rows
    cols = 2 * count
    slots = [
        lax.rem(slot_ref[(me_ref[1] ^ flip) * own + i], hat_ref.shape[0])
        for flip in flips
        for i in range(own)
    ]

    def spectra_step(step):
        plain, packed, sign = lane_masks(step * LANES, LANES)
        spectra = []
        for j in range(2):
            one = dot(x, two_slabs(table_ref, step, j))
            spectra.append(one + sign * pltpu.roll(one, one.shape[0] - 1, axis=0))
        for r in range(rows):
            both = jnp.concatenate([s[r * count : (r + 1) * count] for s in spectra], axis=0)
            if step == 0:
                both = jnp.concatenate([both * plain, both * packed], axis=0).astype(BF16)
                hat = dot(spec_ref[...], both).astype(BF16)
            else:
                hat = dot(spec_ref[:, :cols], both.astype(BF16)).astype(BF16)
            for i in range(LANES // SLAB):
                s_ref[step * (LANES // SLAB) + i, r] = hat[:, i * SLAB : (i + 1) * SLAB]

    def product_slab(slab, pair):
        far = slice(slab * SLAB, (slab + 1) * SLAB)
        base = pair * 2 * half
        for seg in range(SEGS):
            re_rows = slice(2 * seg * half, (2 * seg + 1) * half)
            im_rows = slice((2 * seg + 1) * half, (2 * seg + 2) * half)
            re_sum = total_ref[pair, re_rows, far] if has_total else None
            im_sum = total_ref[pair, im_rows, far] if has_total else None
            for start in range(0, rows, GROUP):
                re, im = None, None
                for r in range(start, min(start + GROUP, rows)):
                    h_re = hat_ref[slots[r], slab, base : base + half]
                    h_im = hat_ref[slots[r], slab, base + half : base + 2 * half]
                    s_re, s_im = s_ref[slab, r, re_rows], s_ref[slab, r, im_rows]
                    add_re = s_re * h_re - s_im * h_im
                    add_im = s_re * h_im + s_im * h_re
                    re = add_re if re is None else re + add_re
                    im = add_im if im is None else im + add_im
                re, im = re.astype(F32), im.astype(F32)
                re_sum = re if re_sum is None else re_sum + re
                im_sum = im if im_sum is None else im_sum + im
            if last:
                y_ref[slab, pair, re_rows] = re_sum.astype(BF16)
                y_ref[slab, pair, im_rows] = im_sum.astype(BF16)
            else:
                out_ref[pair, re_rows, far] = re_sum
                out_ref[pair, im_rows, far] = im_sum

    def product_step(step):
        for pair in range(channels // 2):
            first = step * (LANES // SLAB)
            for i in range(LANES // SLAB):
                product_slab(first + i, pair)
            if last:
                y = jnp.concatenate([y_ref[first + i, pair] for i in range(LANES // SLAB)], axis=-1)
                if step == 0:
                    plain, packed, _ = lane_masks(0, LANES)
                    mix = dot(back_ref[0], y * plain.astype(BF16)) + dot(back_ref[1], y * packed.astype(BF16))
                else:
                    mix = dot(back_ref[0], y)
                mix = mix.astype(BF16)
                here = slice(step * LANES, (step + 1) * LANES)
                for c in range(2):
                    rows_to = slice((2 * pair + c) * blocks, (2 * pair + c + 1) * blocks)
                    left_re[rows_to, here] = mix[2 * c * blocks : (2 * c + 1) * blocks]
                    left_im[rows_to, here] = mix[(2 * c + 1) * blocks : (2 * c + 2) * blocks]

    spectra_step(0)
    for step in range(steps):
        if step + 1 < steps:
            spectra_step(step + 1)
        product_step(step)

    if last:
        each = blocks // shares
        for step in range(steps):
            here = slice(step * LANES, (step + 1) * LANES)
            part = dot(left_re[...], two_slabs(inv_ref, step, 0)) + dot(left_im[...], two_slabs(inv_ref, step, 1))
            for t in range(shares):
                for c in range(channels):
                    row = c * blocks + t * each
                    time_ref[t, c, :, here] = part[row : row + each]
        for d in range(shares):
            out_refs[d][...] = time_ref[me_ref[0] ^ d].astype(BF16)


def add_sources(x_list, flips, me, slots, hat, total, last, shares, channels, parts):
    slabs = hat.shape[1]
    bins = slabs * SLAB
    frames = parts + SEGS * KEEP
    own = x_list[0].shape[0] // frames
    rows = own * len(x_list)
    blocks = frames - parts
    wide = 2 * SEGS * STEPS
    table, inverse = block_tables(bins)
    spec, _, back = step_tables(parts, frames, channels)
    vmem = pl.BlockSpec(memory_space=pltpu.VMEM)
    smem = pl.BlockSpec(memory_space=pltpu.SMEM)

    operands = [me, slots] + list(x_list) + [hat, jnp.asarray(table), jnp.asarray(spec)]
    aliases = {}
    if total is not None:
        if not last:
            aliases = {len(operands): 0}
        operands.append(total)
    scratch = [pltpu.VMEM((slabs, rows, 2 * wide, SLAB), BF16)]
    if last:
        operands += [jnp.asarray(back), jnp.asarray(inverse)]
        each = blocks // shares
        out_shape = [jax.ShapeDtypeStruct((channels, each, bins), BF16)] * shares
        scratch += [
            pltpu.VMEM((slabs, channels // 2, 2 * wide, SLAB), BF16),
            pltpu.VMEM((channels * blocks, bins), BF16),
            pltpu.VMEM((channels * blocks, bins), BF16),
            pltpu.VMEM((shares, channels, each, bins), F32),
        ]
    else:
        out_shape = jax.ShapeDtypeStruct((channels // 2, 2 * wide, bins), F32)
    flops = 2 * bins * (
        rows * frames * 2 * bins + channels * rows * wide * 16 + (channels * blocks * 2 * bins if last else 0)
    )
    body = functools.partial(
        mix_kernel, tuple(flips), own, channels, blocks, shares, total is not None, last
    )
    return pl.pallas_call(
        body,
        in_specs=[smem, smem] + [vmem] * (len(operands) - 2),
        out_specs=[vmem] * shares if last else vmem,
        out_shape=out_shape,
        scratch_shapes=scratch,
        input_output_aliases=aliases,
        compiler_params=pltpu.CompilerParams(vmem_limit_bytes=24 * 2**20),
        cost_estimate=pl.CostEstimate(flops=flops, bytes_accessed=8 * 2**20, transcendentals=0),
    )(*operands)


def sum_kernel(count, each, me_ref, *refs):
    parts, outs, sum_ref = refs[:count], refs[count:-1], refs[-1]
    total = parts[0][...].astype(F32)
    for part in parts[1:]:
        total = total + part[...].astype(F32)
    sum_ref[...] = total
    for d in range(each):
        outs[d][...] = sum_ref[:, pl.ds(me_ref[0] ^ d, 1), :].reshape(outs[d].shape).astype(BF16)


def sum_groups(parts, me):
    channels, each, bins = parts[0].shape
    vmem = pl.BlockSpec(memory_space=pltpu.VMEM)
    return pl.pallas_call(
        functools.partial(sum_kernel, len(parts), each),
        in_specs=[pl.BlockSpec(memory_space=pltpu.SMEM)] + [vmem] * len(parts),
        out_specs=[vmem] * each,
        out_shape=[jax.ShapeDtypeStruct((channels, bins), BF16)] * each,
        scratch_shapes=[pltpu.VMEM(parts[0].shape, F32)],
        compiler_params=pltpu.CompilerParams(vmem_limit_bytes=8 * 2**20),
    )(me[None], *parts)


def per_device(src_count, ch_count, dry_signal, room_spectra, render_slot, decoder):
    rows_total, parts, channels, _, block_len = room_spectra.shape
    own = dry_signal.shape[0]
    frames = dry_signal.shape[1] // block_len
    blocks = frames - parts
    src_me = lax.axis_index("src").astype(jnp.int32)
    ch_me = lax.axis_index("ch").astype(jnp.int32)

    x_own = dry_signal.reshape(own * frames, block_len)

    def swap(value, axis, count, flip):
        return lax.ppermute(value, axis, [(i, i ^ flip) for i in range(count)])

    chips = ch_count // 2
    lanes = [x_own] + [swap(x_own, "ch", ch_count, 2 * d) for d in range(1, chips)]
    mates = [swap(x_own, "ch", ch_count, 1)]

    row = jnp.arange(ch_count * channels, dtype=jnp.int32)
    takes = ((row // channels) ^ ch_me) * channels + row % channels
    order = (takes[:, None] == row[None, :]).astype(BF16)
    own_order = dot(order, decoder).astype(BF16)

    hat = transform_responses(room_spectra)
    me = jnp.stack([src_me, ch_me])

    def add(x_list, flips, total, last):
        return add_sources(
            x_list, flips, me, render_slot, hat, total, last, src_count, channels, parts
        )

    total = add([lanes[0], mates[0]], [0, 1], None, False)
    mates.append(swap(lanes[1], "ch", ch_count, 1))
    *late, total = lax.optimization_barrier((*lanes[2:], total))
    lanes[2:] = late
    mates += [swap(x, "ch", ch_count, 1) for x in late]
    x_list, flips = [], []
    for d in range(1, chips):
        x_list += [lanes[d], mates[d]]
        flips += [2 * d, 2 * d + 1]
    total = add(x_list, flips, total, True)

    parts_in = [total[0]] + [swap(total[d], "src", src_count, d) for d in range(1, src_count)]
    each = blocks // src_count
    if each == ch_count:
        pieces = sum_groups(parts_in, ch_me)
        given = swap(jnp.concatenate(pieces[1::2], axis=0), "ch", ch_count, 1)
        both = [
            jnp.concatenate([pieces[2 * d], given[d * channels : (d + 1) * channels]], axis=0)
            for d in range(chips)
        ]
        both[1:] = [swap(both[d], "ch", ch_count, 2 * d) for d in range(1, chips)]
        gathered = jnp.concatenate(both, axis=0)
        matrix = own_order
    else:
        signal = parts_in[0].astype(F32)
        for part in parts_in[1:]:
            signal = signal + part.astype(F32)
        signal = signal.astype(BF16).reshape(channels, -1)
        gathered = lax.all_to_all(signal, "ch", split_axis=1, concat_axis=0, tiled=True)
        matrix = decoder
    decoded = lax.dot_general(
        gathered, matrix, (((0,), (0,)), ((), ())), preferred_element_type=F32
    )
    return decoded.astype(BF16)


def solution(mesh):
    body = functools.partial(per_device, mesh.shape["src"], mesh.shape["ch"])
    return jax.shard_map(
        body,
        mesh=mesh,
        in_specs=(P(("src", "ch"), None), P("src", None, "ch", None, None), P("src"), P()),
        out_specs=P(("src", "ch"), None),
        check_vma=False,
    )
```

```python
import functools
import math

import jax
import jax.numpy as jnp
import ml_dtypes
import numpy as np
from jax import lax
from jax.experimental import pallas as pl
from jax.experimental.pallas import tpu as pltpu
from jax.sharding import PartitionSpec as P

BF16 = jnp.bfloat16
F32 = jnp.float32
LANES = 256
SLAB = 128
GROUP = 4
ROWS = 4
STEPS = 24
SEGS = 2
KEEP = 16


def bf16_table(values):
    return np.asarray(values, dtype=np.float32).astype(ml_dtypes.bfloat16)


@functools.lru_cache(maxsize=None)
def block_tables(block_len):
    size = 2 * block_len
    n = np.arange(block_len)[:, None]
    k = np.arange(block_len)[None, :]
    angle = ((n * k) % size) * (2.0 * math.pi / size)
    fwd_real = np.cos(angle)
    fwd_imag = np.where(k == 0, 1.0 - 2.0 * (n % 2), -np.sin(angle))
    kk = np.arange(block_len)[:, None]
    m = np.arange(block_len)[None, :] + block_len
    angle = ((kk * m) % size) * (2.0 * math.pi / size)
    weight = np.where(kk == 0, 1.0, 2.0)
    inv_real = weight * np.cos(angle) / size
    inv_imag = np.where(kk == 0, (1.0 - 2.0 * (m % 2)) / size, -2.0 * np.sin(angle) / size)
    def slabs(pair):
        return bf16_table(np.stack(pair).reshape(2, block_len, -1, SLAB).transpose(0, 2, 1, 3))

    return slabs([fwd_real, fwd_imag]), slabs([inv_real, inv_imag])


@functools.lru_cache(maxsize=None)
def step_tables(parts, frames, channels):
    half = STEPS // 2
    theta = 2.0 * math.pi * (np.arange(STEPS) + 0.5) / STEPS
    first = (np.arange(STEPS) < half).astype(np.float64)[:, None]

    def forward(steps):
        cos = np.cos(theta[:, None] * steps[None, :])
        sin = np.sin(theta[:, None] * steps[None, :])
        plain = np.block([[cos, sin], [-sin, cos]])
        packed = np.block([[cos * first, cos * (1 - first)], [-sin * first, -sin * (1 - first)]])
        return plain, packed

    spec = np.zeros((2, SEGS, 2, STEPS, 2, frames))
    used = parts - 1 + KEEP
    for kind, table in enumerate(forward(np.arange(used))):
        table = table.reshape(2, STEPS, 2, used)
        for seg in range(SEGS):
            spec[kind, seg, :, :, :, seg * KEEP : seg * KEEP + used] = table
    spec = spec.reshape(2, SEGS * 2 * STEPS, 2 * frames)
    spec = np.concatenate([spec[0], spec[1]], axis=1)

    resp = np.zeros((channels // 2, 2, 2, STEPS, 2, parts, channels, 2))
    for kind, table in enumerate(forward(np.arange(parts))):
        table = table.reshape(2, STEPS, 2, parts).transpose(0, 1, 3, 2)
        for c in range(channels):
            resp[c // 2, :, c % 2, :, kind, :, c] = table
    resp = resp.reshape(channels * 2 * STEPS, 2 * parts * channels * 2)

    back = np.zeros((2, 2, 2, SEGS, KEEP, SEGS, 2, 2, STEPS))
    steps = np.arange(KEEP) + parts - 1
    cos = np.cos(theta[None, :] * steps[:, None]) / STEPS
    sin = np.sin(theta[None, :] * steps[:, None]) / STEPS
    firsts = first[:, 0][None, :]
    for seg in range(SEGS):
        for c in range(2):
            back[0, c, 0, seg, :, seg, 0, c] = cos
            back[0, c, 0, seg, :, seg, 1, c] = -sin
            back[0, c, 1, seg, :, seg, 0, c] = sin
            back[0, c, 1, seg, :, seg, 1, c] = cos
            back[1, c, 0, seg, :, seg, 0, c] = 2 * cos * firsts
            back[1, c, 0, seg, :, seg, 1, c] = -2 * sin * firsts
            back[1, c, 1, seg, :, seg, 0, c] = 2 * cos * (1 - firsts)
            back[1, c, 1, seg, :, seg, 1, c] = -2 * sin * (1 - firsts)
    back = back.reshape(2, 4 * SEGS * KEEP, 4 * SEGS * STEPS)
    return bf16_table(spec), bf16_table(resp), bf16_table(back)


def dot(left, right):
    return jnp.dot(left, right, preferred_element_type=F32)


def lane_masks(start, width):
    lane = lax.broadcasted_iota(jnp.int32, (1, width), 1) + start
    packed = (lane == 0).astype(F32)
    sign = (1 - 2 * (lane % 2)).astype(F32)
    return 1.0 - packed, packed, sign


def two_slabs(ref, step, *index):
    first = step * (LANES // SLAB)
    return jnp.concatenate([ref[(*index, first + i)] for i in range(LANES // SLAB)], axis=-1)


def response_kernel(rows, bins, room_ref, table_ref, hat_ref):
    depth = room_ref.shape[1] * room_ref.shape[2] * 2
    flat = room_ref.reshape(rows, depth, bins)
    plain, packed, _ = lane_masks(0, LANES)
    plain, packed = plain.astype(BF16), packed.astype(BF16)

    def some(outer, carry):
        for inner in range(ROWS):
            r = outer * ROWS + inner
            for step in range(bins // LANES):
                h = flat[r, :, step * LANES : (step + 1) * LANES]
                if step == 0:
                    h = jnp.concatenate([h * plain, h * packed], axis=0)
                    hat = dot(table_ref[...], h)
                else:
                    hat = dot(table_ref[:, :depth], h)
                hat = hat.astype(BF16)
                for i in range(LANES // SLAB):
                    hat_ref[r, step * (LANES // SLAB) + i] = hat[:, i * SLAB : (i + 1) * SLAB]
        return carry

    lax.fori_loop(0, rows // ROWS, some, 0)


def transform_responses(room):
    rows, parts, channels, _, bins = room.shape
    slabs = bins // SLAB
    _, resp, _ = step_tables(parts, parts + SEGS * KEEP, channels)
    vmem = pl.BlockSpec(memory_space=pltpu.VMEM)
    flops = 2 * rows * channels * 2 * STEPS * parts * channels * 2 * bins
    return pl.pallas_call(
        functools.partial(response_kernel, rows, bins),
        in_specs=[vmem, vmem],
        out_specs=vmem,
        out_shape=jax.ShapeDtypeStruct((rows, slabs, channels * 2 * STEPS, SLAB), BF16),
        compiler_params=pltpu.CompilerParams(vmem_limit_bytes=8 * 2**20),
        cost_estimate=pl.CostEstimate(flops=flops, bytes_accessed=16 * 2**20, transcendentals=0),
    )(room, jnp.asarray(resp))


def copy_kernel(x_ref, out_ref):
    out_ref[...] = x_ref[...]


def copy_early(x):
    vmem = pl.BlockSpec(memory_space=pltpu.VMEM)
    return pl.pallas_call(
        copy_kernel,
        in_specs=[vmem],
        out_specs=vmem,
        out_shape=jax.ShapeDtypeStruct(x.shape, x.dtype),
        compiler_params=pltpu.CompilerParams(vmem_limit_bytes=2 * 2**20),
        cost_estimate=pl.CostEstimate(flops=0, bytes_accessed=24 * 2**20, transcendentals=0),
    )(x)


def mix_kernel(flips, own, channels, blocks, shares, has_total, last, me_ref, slot_ref, *refs):
    refs = list(refs)
    x_refs = [refs.pop(0) for _ in flips]
    hat_ref, table_ref, spec_ref = [refs.pop(0) for _ in range(3)]
    total_ref = refs.pop(0) if has_total else None
    if last:
        back_ref, inv_ref = refs.pop(0), refs.pop(0)
        out_refs = [refs.pop(0) for _ in range(shares)]
    else:
        out_ref = refs.pop(0)
    s_ref = refs.pop(0)
    if last:
        y_ref, left_re, left_im, time_ref = refs

    slabs = hat_ref.shape[1]
    bins = slabs * SLAB
    steps = bins // LANES
    rows = own * len(flips)
    half = 2 * STEPS
    x = jnp.concatenate([ref[...] for ref in x_refs], axis=0)
    count = x.shape[0] // rows
    cols = 2 * count
    slots = [
        lax.rem(slot_ref[(me_ref[1] ^ flip) * own + i], hat_ref.shape[0])
        for flip in flips
        for i in range(own)
    ]

    def frame_spectra(step):
        _, _, sign = lane_masks(step * LANES, LANES)
        spectra = []
        for j in range(2):
            one = dot(x, two_slabs(table_ref, step, j))
            spectra.append(one + sign * pltpu.roll(one, one.shape[0] - 1, axis=0))
        return spectra

    def step_spectra(step, r, spectra):
        both = jnp.concatenate([s[r * count : (r + 1) * count] for s in spectra], axis=0)
        if step == 0:
            plain, packed, _ = lane_masks(0, LANES)
            both = jnp.concatenate([both * plain, both * packed], axis=0).astype(BF16)
            hat = dot(spec_ref[...], both)
        else:
            hat = dot(spec_ref[:, :cols], both.astype(BF16))
        for i in range(LANES // SLAB):
            part = hat[:, i * SLAB : (i + 1) * SLAB]
            for k in range(2 * SEGS):
                one = part[k * STEPS : (k + 1) * STEPS]
                both = jnp.concatenate([one, one], axis=0).astype(BF16)
                s_ref[step * (LANES // SLAB) + i, r, k * half : (k + 1) * half] = both

    def product_slab(slab, pair):
        far = slice(slab * SLAB, (slab + 1) * SLAB)
        base = pair * 2 * half
        for seg in range(SEGS):
            re_rows = slice(2 * seg * half, (2 * seg + 1) * half)
            im_rows = slice((2 * seg + 1) * half, (2 * seg + 2) * half)
            re_sum = total_ref[pair, re_rows, far] if has_total else None
            im_sum = total_ref[pair, im_rows, far] if has_total else None
            for start in range(0, rows, GROUP):
                re, im = None, None
                for r in range(start, min(start + GROUP, rows)):
                    h_re = hat_ref[slots[r], slab, base : base + half]
                    h_im = hat_ref[slots[r], slab, base + half : base + 2 * half]
                    s_re, s_im = s_ref[slab, r, re_rows], s_ref[slab, r, im_rows]
                    add_re = s_re * h_re - s_im * h_im
                    add_im = s_re * h_im + s_im * h_re
                    re = add_re if re is None else re + add_re
                    im = add_im if im is None else im + add_im
                re, im = re.astype(F32), im.astype(F32)
                re_sum = re if re_sum is None else re_sum + re
                im_sum = im if im_sum is None else im_sum + im
            if last:
                y_ref[slab, pair, re_rows] = re_sum.astype(BF16)
                y_ref[slab, pair, im_rows] = im_sum.astype(BF16)
            else:
                out_ref[pair, re_rows, far] = re_sum
                out_ref[pair, im_rows, far] = im_sum

    def product_pair(step, pair):
        first = step * (LANES // SLAB)
        for i in range(LANES // SLAB):
            product_slab(first + i, pair)
        if last:
            y = jnp.concatenate([y_ref[first + i, pair] for i in range(LANES // SLAB)], axis=-1)
            if step == 0:
                plain, packed, _ = lane_masks(0, LANES)
                mix = dot(back_ref[0], y * plain.astype(BF16)) + dot(back_ref[1], y * packed.astype(BF16))
            else:
                mix = dot(back_ref[0], y)
            mix = mix.astype(BF16)
            here = slice(step * LANES, (step + 1) * LANES)
            for c in range(2):
                rows_to = slice((2 * pair + c) * blocks, (2 * pair + c + 1) * blocks)
                left_re[rows_to, here] = mix[2 * c * blocks : (2 * c + 1) * blocks]
                left_im[rows_to, here] = mix[(2 * c + 1) * blocks : (2 * c + 2) * blocks]

    pairs = channels // 2
    for step in range(steps + 1):
        spectra = frame_spectra(step) if step < steps else None
        done = 0
        for pair in range(pairs):
            if spectra is not None:
                upto = rows * (pair + 1) // pairs
                for r in range(done, upto):
                    step_spectra(step, r, spectra)
                done = upto
            if step > 0:
                product_pair(step - 1, pair)

    if last:
        each = blocks // shares
        for step in range(steps):
            here = slice(step * LANES, (step + 1) * LANES)
            part = dot(left_re[...], two_slabs(inv_ref, step, 0)) + dot(left_im[...], two_slabs(inv_ref, step, 1))
            for t in range(shares):
                for c in range(channels):
                    row = c * blocks + t * each
                    time_ref[t, c, :, here] = part[row : row + each]
        for d in range(shares):
            out_refs[d][...] = time_ref[me_ref[0] ^ d].astype(BF16)


def add_sources(x_list, flips, me, slots, hat, total, last, shares, channels, parts):
    slabs = hat.shape[1]
    bins = slabs * SLAB
    frames = parts + SEGS * KEEP
    own = x_list[0].shape[0] // frames
    rows = own * len(x_list)
    blocks = frames - parts
    wide = 2 * SEGS * STEPS
    table, inverse = block_tables(bins)
    spec, _, back = step_tables(parts, frames, channels)
    vmem = pl.BlockSpec(memory_space=pltpu.VMEM)
    smem = pl.BlockSpec(memory_space=pltpu.SMEM)

    operands = [me, slots] + list(x_list) + [hat, jnp.asarray(table), jnp.asarray(spec)]
    aliases = {}
    if total is not None:
        if not last:
            aliases = {len(operands): 0}
        operands.append(total)
    scratch = [pltpu.VMEM((slabs, rows, 2 * wide, SLAB), BF16)]
    if last:
        operands += [jnp.asarray(back), jnp.asarray(inverse)]
        each = blocks // shares
        out_shape = [jax.ShapeDtypeStruct((channels, each, bins), BF16)] * shares
        scratch += [
            pltpu.VMEM((slabs, channels // 2, 2 * wide, SLAB), BF16),
            pltpu.VMEM((channels * blocks, bins), BF16),
            pltpu.VMEM((channels * blocks, bins), BF16),
            pltpu.VMEM((shares, channels, each, bins), F32),
        ]
    else:
        out_shape = jax.ShapeDtypeStruct((channels // 2, 2 * wide, bins), F32)
    flops = 2 * bins * (
        rows * frames * 2 * bins + channels * rows * wide * 16 + (channels * blocks * 2 * bins if last else 0)
    )
    body = functools.partial(
        mix_kernel, tuple(flips), own, channels, blocks, shares, total is not None, last
    )
    return pl.pallas_call(
        body,
        in_specs=[smem, smem] + [vmem] * (len(operands) - 2),
        out_specs=[vmem] * shares if last else vmem,
        out_shape=out_shape,
        scratch_shapes=scratch,
        input_output_aliases=aliases,
        compiler_params=pltpu.CompilerParams(vmem_limit_bytes=16 * 2**20),
        cost_estimate=pl.CostEstimate(flops=flops, bytes_accessed=8 * 2**20, transcendentals=0),
    )(*operands)


def sum_kernel(count, each, me_ref, *refs):
    parts, outs, sum_ref = refs[:count], refs[count:-1], refs[-1]
    total = parts[0][...].astype(F32)
    for part in parts[1:]:
        total = total + part[...].astype(F32)
    sum_ref[...] = total
    for d in range(each):
        outs[d][...] = sum_ref[:, pl.ds(me_ref[0] ^ d, 1), :].reshape(outs[d].shape).astype(BF16)


def sum_groups(parts, me):
    channels, each, bins = parts[0].shape
    vmem = pl.BlockSpec(memory_space=pltpu.VMEM)
    return pl.pallas_call(
        functools.partial(sum_kernel, len(parts), each),
        in_specs=[pl.BlockSpec(memory_space=pltpu.SMEM)] + [vmem] * len(parts),
        out_specs=[vmem] * each,
        out_shape=[jax.ShapeDtypeStruct((channels, bins), BF16)] * each,
        scratch_shapes=[pltpu.VMEM(parts[0].shape, F32)],
        compiler_params=pltpu.CompilerParams(vmem_limit_bytes=8 * 2**20),
    )(me[None], *parts)


def per_device(src_count, ch_count, dry_signal, room_spectra, render_slot, decoder):
    rows_total, parts, channels, _, block_len = room_spectra.shape
    own = dry_signal.shape[0]
    frames = dry_signal.shape[1] // block_len
    blocks = frames - parts
    src_me = lax.axis_index("src").astype(jnp.int32)
    ch_me = lax.axis_index("ch").astype(jnp.int32)

    x_own = copy_early(dry_signal.reshape(own * frames, block_len))

    def swap(value, axis, count, flip):
        return lax.ppermute(value, axis, [(i, i ^ flip) for i in range(count)])

    chips = ch_count // 2
    lanes = [x_own] + [swap(x_own, "ch", ch_count, 2 * d) for d in range(1, chips)]
    mates = [swap(x_own, "ch", ch_count, 1)]

    row = jnp.arange(ch_count * channels, dtype=jnp.int32)
    takes = ((row // channels) ^ ch_me) * channels + row % channels
    order = (takes[:, None] == row[None, :]).astype(BF16)
    own_order = dot(order, decoder).astype(BF16)

    hat = transform_responses(room_spectra)
    me = jnp.stack([src_me, ch_me])

    def add(x_list, flips, total, last):
        return add_sources(
            x_list, flips, me, render_slot, hat, total, last, src_count, channels, parts
        )

    total = add([lanes[0], mates[0]], [0, 1], None, False)
    mates.append(swap(lanes[1], "ch", ch_count, 1))
    *late, total = lax.optimization_barrier((*lanes[2:], total))
    lanes[2:] = late
    mates += [swap(x, "ch", ch_count, 1) for x in late]
    x_list, flips = [], []
    for d in range(1, chips):
        x_list += [lanes[d], mates[d]]
        flips += [2 * d, 2 * d + 1]
    total = add(x_list, flips, total, True)

    parts_in = [total[0]] + [swap(total[d], "src", src_count, d) for d in range(1, src_count)]
    each = blocks // src_count
    if each == ch_count:
        pieces = sum_groups(parts_in, ch_me)
        given = swap(jnp.concatenate(pieces[1::2], axis=0), "ch", ch_count, 1)
        both = [
            jnp.concatenate([pieces[2 * d], given[d * channels : (d + 1) * channels]], axis=0)
            for d in range(chips)
        ]
        both[1:] = [swap(both[d], "ch", ch_count, 2 * d) for d in range(1, chips)]
        gathered = jnp.concatenate(both, axis=0)
        matrix = own_order
    else:
        signal = parts_in[0].astype(F32)
        for part in parts_in[1:]:
            signal = signal + part.astype(F32)
        signal = signal.astype(BF16).reshape(channels, -1)
        gathered = lax.all_to_all(signal, "ch", split_axis=1, concat_axis=0, tiled=True)
        matrix = decoder
    decoded = lax.dot_general(
        gathered, matrix, (((0,), (0,)), ((), ())), preferred_element_type=F32
    )
    return decoded.astype(BF16)


def solution(mesh):
    body = functools.partial(per_device, mesh.shape["src"], mesh.shape["ch"])
    return jax.shard_map(
        body,
        mesh=mesh,
        in_specs=(P(("src", "ch"), None), P("src", None, "ch", None, None), P("src"), P()),
        out_specs=P(("src", "ch"), None),
        check_vma=False,
    )
```

```python
import functools
import math

import jax
import jax.numpy as jnp
import ml_dtypes
import numpy as np
from jax import lax
from jax.experimental import pallas as pl
from jax.experimental.pallas import tpu as pltpu
from jax.sharding import PartitionSpec as P

BF16 = jnp.bfloat16
F32 = jnp.float32
LANES = 256
SLAB = 128
GROUP = 4
ROWS = 4
STEPS = 24
SEGS = 2
KEEP = 16


def bf16_table(values):
    return np.asarray(values, dtype=np.float32).astype(ml_dtypes.bfloat16)


@functools.lru_cache(maxsize=None)
def block_tables(block_len):
    size = 2 * block_len
    n = np.arange(block_len)[:, None]
    k = np.arange(block_len)[None, :]
    angle = ((n * k) % size) * (2.0 * math.pi / size)
    fwd_real = np.cos(angle)
    fwd_imag = np.where(k == 0, 1.0 - 2.0 * (n % 2), -np.sin(angle))
    kk = np.arange(block_len)[:, None]
    m = np.arange(block_len)[None, :] + block_len
    angle = ((kk * m) % size) * (2.0 * math.pi / size)
    weight = np.where(kk == 0, 1.0, 2.0)
    inv_real = weight * np.cos(angle) / size
    inv_imag = np.where(kk == 0, (1.0 - 2.0 * (m % 2)) / size, -2.0 * np.sin(angle) / size)
    def slabs(pair):
        return bf16_table(np.stack(pair).reshape(2, block_len, -1, SLAB).transpose(0, 2, 1, 3))

    return slabs([fwd_real, fwd_imag]), slabs([inv_real, inv_imag])


@functools.lru_cache(maxsize=None)
def step_tables(parts, frames, channels):
    half = STEPS // 2
    theta = 2.0 * math.pi * (np.arange(STEPS) + 0.5) / STEPS
    first = (np.arange(STEPS) < half).astype(np.float64)[:, None]

    def forward(steps):
        cos = np.cos(theta[:, None] * steps[None, :])
        sin = np.sin(theta[:, None] * steps[None, :])
        plain = np.block([[cos, sin], [-sin, cos]])
        packed = np.block([[cos * first, cos * (1 - first)], [-sin * first, -sin * (1 - first)]])
        return plain, packed

    spec = np.zeros((2, SEGS, 2, STEPS, 2, frames))
    used = parts - 1 + KEEP
    for kind, table in enumerate(forward(np.arange(used))):
        table = table.reshape(2, STEPS, 2, used)
        for seg in range(SEGS):
            spec[kind, seg, :, :, :, seg * KEEP : seg * KEEP + used] = table
    spec = spec.reshape(2, SEGS * 2 * STEPS, 2 * frames)
    spec = np.stack([np.kron(np.eye(2), one) for one in spec])

    resp = np.zeros((channels // 2, 2, 2, STEPS, 2, parts, channels, 2))
    for kind, table in enumerate(forward(np.arange(parts))):
        table = table.reshape(2, STEPS, 2, parts).transpose(0, 1, 3, 2)
        for c in range(channels):
            resp[c // 2, :, c % 2, :, kind, :, c] = table
    resp = resp.reshape(channels * 2 * STEPS, 2 * parts * channels * 2)

    back = np.zeros((2, 2, 2, SEGS, KEEP, SEGS, 2, 2, STEPS))
    steps = np.arange(KEEP) + parts - 1
    cos = np.cos(theta[None, :] * steps[:, None]) / STEPS
    sin = np.sin(theta[None, :] * steps[:, None]) / STEPS
    firsts = first[:, 0][None, :]
    for seg in range(SEGS):
        for c in range(2):
            back[0, c, 0, seg, :, seg, 0, c] = cos
            back[0, c, 0, seg, :, seg, 1, c] = -sin
            back[0, c, 1, seg, :, seg, 0, c] = sin
            back[0, c, 1, seg, :, seg, 1, c] = cos
            back[1, c, 0, seg, :, seg, 0, c] = 2 * cos * firsts
            back[1, c, 0, seg, :, seg, 1, c] = -2 * sin * firsts
            back[1, c, 1, seg, :, seg, 0, c] = 2 * cos * (1 - firsts)
            back[1, c, 1, seg, :, seg, 1, c] = -2 * sin * (1 - firsts)
    back = back.reshape(2, 4 * SEGS * KEEP, 4 * SEGS * STEPS)
    return bf16_table(spec), bf16_table(resp), bf16_table(back)


def dot(left, right):
    return jnp.dot(left, right, preferred_element_type=F32)


def lane_masks(start, width):
    lane = lax.broadcasted_iota(jnp.int32, (1, width), 1) + start
    packed = (lane == 0).astype(F32)
    sign = (1 - 2 * (lane % 2)).astype(F32)
    return 1.0 - packed, packed, sign


def two_slabs(ref, step, *index):
    first = step * (LANES // SLAB)
    return jnp.concatenate([ref[(*index, first + i)] for i in range(LANES // SLAB)], axis=-1)


def response_kernel(rows, bins, room_hbm, table_hbm, hat_ref, done_ref, room_ref, table_ref, sems):
    depth = room_ref.shape[1] * room_ref.shape[2] * 2
    flat = room_ref.reshape(rows, depth, bins)
    plain, packed, _ = lane_masks(0, LANES)
    plain, packed = plain.astype(BF16), packed.astype(BF16)

    def copy(r):
        return pltpu.make_async_copy(room_hbm.at[r], room_ref.at[r], sems.at[r])

    table_copy = pltpu.make_async_copy(table_hbm, table_ref, sems.at[rows])
    table_copy.start()
    for r in range(rows):
        copy(r).start()
    table_copy.wait()

    def some(outer, carry):
        for inner in range(ROWS):
            copy(outer * ROWS + inner).wait()
        for inner in range(ROWS):
            r = outer * ROWS + inner
            for step in range(bins // LANES):
                h = flat[r, :, step * LANES : (step + 1) * LANES]
                if step == 0:
                    h = jnp.concatenate([h * plain, h * packed], axis=0)
                    hat = dot(table_ref[...], h)
                else:
                    hat = dot(table_ref[:, :depth], h)
                hat = hat.astype(BF16)
                for i in range(LANES // SLAB):
                    hat_ref[r, step * (LANES // SLAB) + i] = hat[:, i * SLAB : (i + 1) * SLAB]
        return carry

    lax.fori_loop(0, rows // ROWS, some, 0)
    done_ref[...] = jnp.zeros_like(done_ref)


def transform_responses(room):
    rows, parts, channels, _, bins = room.shape
    slabs = bins // SLAB
    _, resp, _ = step_tables(parts, parts + SEGS * KEEP, channels)
    flops = 2 * rows * channels * 2 * STEPS * parts * channels * 2 * bins
    hbm = pl.BlockSpec(memory_space=pltpu.HBM)
    return pl.pallas_call(
        functools.partial(response_kernel, rows, bins),
        in_specs=[hbm, hbm],
        out_specs=[pl.BlockSpec(memory_space=pltpu.VMEM)] * 2,
        out_shape=[
            pltpu.VMEM((rows, slabs, channels * 2 * STEPS, SLAB), BF16),
            jax.ShapeDtypeStruct((8, 128), F32),
        ],
        scratch_shapes=[
            pltpu.VMEM(room.shape, BF16),
            pltpu.VMEM(resp.shape, BF16),
            pltpu.SemaphoreType.DMA((rows + 1,)),
        ],
        compiler_params=pltpu.CompilerParams(vmem_limit_bytes=8 * 2**20),
        cost_estimate=pl.CostEstimate(flops=flops, bytes_accessed=16 * 2**20, transcendentals=0),
    )(
        pltpu.with_memory_space_constraint(room, pltpu.HBM),
        pltpu.with_memory_space_constraint(jnp.asarray(resp), pltpu.HBM),
    )


def spectra_kernel(pieces, rows, *refs):
    x_refs, (table_ref, spec_ref) = refs[:pieces], refs[pieces : pieces + 2]
    out_ref = refs[-1]
    slabs = table_ref.shape[1]
    wide = 2 * SEGS * STEPS
    x = jnp.concatenate([ref[...] for ref in x_refs], axis=0)
    count = x.shape[0] // rows
    cols = 2 * count
    for step in range(slabs * SLAB // LANES):
        plain, packed, sign = lane_masks(step * LANES, LANES)
        spectra = []
        for j in range(2):
            one = dot(x, two_slabs(table_ref, step, j))
            spectra.append(one + sign * pltpu.roll(one, one.shape[0] - 1, axis=0))
        for start in range(0, rows, 2):
            some = range(start, min(start + 2, rows))
            n = len(some)
            both = [s[r * count : (r + 1) * count] for r in some for s in spectra]
            both = jnp.concatenate(both, axis=0)
            spec = [spec_ref[kind, : n * wide, : n * cols] for kind in range(2)]
            if step == 0:
                hat = dot(spec[0], (both * plain).astype(BF16)) + dot(spec[1], (both * packed).astype(BF16))
            else:
                hat = dot(spec[0], both.astype(BF16))
            hat = hat.astype(BF16)
            for k, r in enumerate(some):
                for i in range(LANES // SLAB):
                    at = slice(i * SLAB, (i + 1) * SLAB)
                    out_ref[step * (LANES // SLAB) + i, r] = hat[k * wide : (k + 1) * wide, at]


def transform_signals(x_list, own, bins, parts, after=None):
    frames = parts + SEGS * KEEP
    rows = own * len(x_list)
    slabs = bins // SLAB
    table, _ = block_tables(bins)
    spec, _, _ = step_tables(parts, frames, 2)
    vmem = pl.BlockSpec(memory_space=pltpu.VMEM)
    flops = 2 * bins * rows * (frames * 2 * bins + 4 * SEGS * STEPS * frames)
    operands = [*x_list, jnp.asarray(table), jnp.asarray(spec)]
    if after is not None:
        operands.append(after)
    return pl.pallas_call(
        functools.partial(spectra_kernel, len(x_list), rows),
        in_specs=[vmem] * len(operands),
        out_specs=vmem,
        out_shape=jax.ShapeDtypeStruct((slabs, rows, 2 * SEGS * STEPS, SLAB), BF16),
        compiler_params=pltpu.CompilerParams(vmem_limit_bytes=8 * 2**20),
        cost_estimate=pl.CostEstimate(flops=flops, bytes_accessed=4 * 2**20, transcendentals=0),
    )(*operands)


def mix_kernel(flips, own, channels, blocks, shares, has_total, last, me_ref, slot_ref, *refs):
    refs = list(refs)
    s_refs = [refs.pop(0) for _ in flips]
    hat_ref = refs.pop(0)
    total_ref = refs.pop(0) if has_total else None
    if last:
        back_ref, inv_ref = refs.pop(0), refs.pop(0)
        out_refs = [refs.pop(0) for _ in range(shares)]
        y_ref, left_re, left_im, time_ref = refs
    else:
        (out_ref,) = refs

    slabs = hat_ref.shape[1]
    steps = slabs * SLAB // LANES
    half = 2 * STEPS
    pairs = channels // 2
    sources = []
    for ref, some in zip(s_refs, flips):
        for k, flip in enumerate(some):
            for i in range(own):
                slot = lax.rem(slot_ref[(me_ref[1] ^ flip) * own + i], hat_ref.shape[0])
                sources.append((ref, k * own + i, slot))
    groups = -(-len(sources) // GROUP)
    size = -(-len(sources) // groups)

    def twice(rows):
        rows = rows.astype(F32)
        return jnp.concatenate([rows, rows], axis=0).astype(BF16)

    def products(slab, seg):
        re_in = slice(2 * seg * STEPS, (2 * seg + 1) * STEPS)
        im_in = slice((2 * seg + 1) * STEPS, (2 * seg + 2) * STEPS)
        re_rows = slice(2 * seg * half, (2 * seg + 1) * half)
        im_rows = slice((2 * seg + 1) * half, (2 * seg + 2) * half)
        spectra = [(twice(ref[slab, r, re_in]), twice(ref[slab, r, im_in])) for ref, r, _ in sources]
        for pair in range(pairs):
            base = pair * 2 * half
            re_sum = total_ref[slab, pair, re_rows] if has_total else None
            im_sum = total_ref[slab, pair, im_rows] if has_total else None
            for start in range(0, len(sources), size):
                re, im = None, None
                for (s_re, s_im), (_, _, slot) in list(zip(spectra, sources))[start : start + size]:
                    h_re = hat_ref[slot, slab, base : base + half]
                    h_im = hat_ref[slot, slab, base + half : base + 2 * half]
                    add_re = s_re * h_re - s_im * h_im
                    add_im = s_re * h_im + s_im * h_re
                    re = add_re if re is None else re + add_re
                    im = add_im if im is None else im + add_im
                re, im = re.astype(F32), im.astype(F32)
                re_sum = re if re_sum is None else re_sum + re
                im_sum = im if im_sum is None else im_sum + im
            if last:
                y_ref[slab, pair, re_rows] = re_sum.astype(BF16)
                y_ref[slab, pair, im_rows] = im_sum.astype(BF16)
            else:
                out_ref[slab, pair, re_rows] = re_sum
                out_ref[slab, pair, im_rows] = im_sum

    for step in range(steps):
        first = step * (LANES // SLAB)
        for i in range(LANES // SLAB):
            for seg in range(SEGS):
                products(first + i, seg)
        if not last:
            continue
        for pair in range(pairs):
            y = jnp.concatenate([y_ref[first + i, pair] for i in range(LANES // SLAB)], axis=-1)
            if step == 0:
                plain, packed, _ = lane_masks(0, LANES)
                mix = dot(back_ref[0], y * plain.astype(BF16)) + dot(back_ref[1], y * packed.astype(BF16))
            else:
                mix = dot(back_ref[0], y)
            mix = mix.astype(BF16)
            here = slice(step * LANES, (step + 1) * LANES)
            for c in range(2):
                rows_to = slice((2 * pair + c) * blocks, (2 * pair + c + 1) * blocks)
                left_re[rows_to, here] = mix[2 * c * blocks : (2 * c + 1) * blocks]
                left_im[rows_to, here] = mix[(2 * c + 1) * blocks : (2 * c + 2) * blocks]

    if last:
        each = blocks // shares
        for step in range(steps):
            here = slice(step * LANES, (step + 1) * LANES)
            part = dot(left_re[...], two_slabs(inv_ref, step, 0)) + dot(left_im[...], two_slabs(inv_ref, step, 1))
            for t in range(shares):
                for c in range(channels):
                    row = c * blocks + t * each
                    time_ref[t, c, :, here] = part[row : row + each]
        for d in range(shares):
            out_refs[d][...] = time_ref[me_ref[0] ^ d].astype(BF16)


def add_sources(s_list, flips, own, me, slots, hat, total, last, shares, channels, parts):
    slabs = hat.shape[1]
    bins = slabs * SLAB
    frames = parts + SEGS * KEEP
    blocks = frames - parts
    wide = 2 * SEGS * STEPS
    _, inverse = block_tables(bins)
    _, _, back = step_tables(parts, frames, channels)
    vmem = pl.BlockSpec(memory_space=pltpu.VMEM)
    smem = pl.BlockSpec(memory_space=pltpu.SMEM)

    operands = [me, slots] + list(s_list) + [pltpu.with_memory_space_constraint(hat, pltpu.VMEM)]
    aliases = {}
    if total is not None:
        if not last:
            aliases = {len(operands): 0}
        operands.append(total)
    scratch = []
    if last:
        operands += [jnp.asarray(back), jnp.asarray(inverse)]
        each = blocks // shares
        out_shape = [jax.ShapeDtypeStruct((channels, each, bins), BF16)] * shares
        scratch = [
            pltpu.VMEM((slabs, channels // 2, 2 * wide, SLAB), BF16),
            pltpu.VMEM((channels * blocks, bins), BF16),
            pltpu.VMEM((channels * blocks, bins), BF16),
            pltpu.VMEM((shares, channels, each, bins), F32),
        ]
    else:
        out_shape = jax.ShapeDtypeStruct((slabs, channels // 2, 2 * wide, SLAB), F32)
    count = own * sum(len(some) for some in flips)
    flops = 2 * bins * channels * (count * wide * 8 + (blocks * 2 * bins if last else 0))
    body = functools.partial(
        mix_kernel, tuple(flips), own, channels, blocks, shares, total is not None, last
    )
    return pl.pallas_call(
        body,
        in_specs=[smem, smem] + [vmem] * (len(operands) - 2),
        out_specs=[vmem] * shares if last else vmem,
        out_shape=out_shape,
        scratch_shapes=scratch,
        input_output_aliases=aliases,
        compiler_params=pltpu.CompilerParams(vmem_limit_bytes=12 * 2**20),
        cost_estimate=pl.CostEstimate(flops=flops, bytes_accessed=8 * 2**20, transcendentals=0),
    )(*operands)


def sum_kernel(count, each, me_ref, *refs):
    parts, outs, sum_ref = refs[:count], refs[count:-1], refs[-1]
    total = parts[0][...].astype(F32)
    for part in parts[1:]:
        total = total + part[...].astype(F32)
    sum_ref[...] = total
    for d in range(each):
        outs[d][...] = sum_ref[:, pl.ds(me_ref[0] ^ d, 1), :].reshape(outs[d].shape).astype(BF16)


def sum_groups(parts, me):
    channels, each, bins = parts[0].shape
    vmem = pl.BlockSpec(memory_space=pltpu.VMEM)
    return pl.pallas_call(
        functools.partial(sum_kernel, len(parts), each),
        in_specs=[pl.BlockSpec(memory_space=pltpu.SMEM)] + [vmem] * len(parts),
        out_specs=[vmem] * each,
        out_shape=[jax.ShapeDtypeStruct((channels, bins), BF16)] * each,
        scratch_shapes=[pltpu.VMEM(parts[0].shape, F32)],
        compiler_params=pltpu.CompilerParams(vmem_limit_bytes=8 * 2**20),
    )(me[None], *parts)


def per_device(src_count, ch_count, dry_signal, room_spectra, render_slot, decoder):
    rows_total, parts, channels, _, block_len = room_spectra.shape
    own = dry_signal.shape[0]
    frames = dry_signal.shape[1] // block_len
    blocks = frames - parts
    src_me = lax.axis_index("src").astype(jnp.int32)
    ch_me = lax.axis_index("ch").astype(jnp.int32)

    x_own = dry_signal.reshape(own * frames, block_len)

    def swap(value, axis, count, flip):
        return lax.ppermute(value, axis, [(i, i ^ flip) for i in range(count)])

    chips = ch_count // 2
    lanes = [swap(x_own, "ch", ch_count, 2 * d) for d in range(1, chips)]

    row = jnp.arange(ch_count * channels, dtype=jnp.int32)
    takes = ((row // channels) ^ ch_me) * channels + row % channels
    order = (takes[:, None] == row[None, :]).astype(BF16)
    own_order = dot(order, decoder).astype(BF16)

    hat, done = transform_responses(room_spectra)
    me = jnp.stack([src_me, ch_me])

    def add(s_list, flips, total, last):
        return add_sources(
            s_list, flips, own, me, render_slot, hat, total, last, src_count, channels, parts
        )

    early = transform_signals([x_own], own, block_len, parts, done)
    early_mate = swap(early, "ch", ch_count, 1)
    total = add([early, early_mate], [[0], [1]], None, False)
    *lanes, total = lax.optimization_barrier((*lanes, total))
    late = transform_signals(lanes, own, block_len, parts)
    late_mate = swap(late, "ch", ch_count, 1)
    total = add([late], [[2 * d for d in range(1, chips)]], total, False)
    total = add([late_mate], [[2 * d + 1 for d in range(1, chips)]], total, True)

    parts_in = [total[0]] + [swap(total[d], "src", src_count, d) for d in range(1, src_count)]
    each = blocks // src_count
    if each == ch_count:
        pieces = sum_groups(parts_in, ch_me)
        given = swap(jnp.concatenate(pieces[1::2], axis=0), "ch", ch_count, 1)
        both = [
            jnp.concatenate([pieces[2 * d], given[d * channels : (d + 1) * channels]], axis=0)
            for d in range(chips)
        ]
        both[1:] = [swap(both[d], "ch", ch_count, 2 * d) for d in range(1, chips)]
        gathered = jnp.concatenate(both, axis=0)
        matrix = own_order
    else:
        signal = parts_in[0].astype(F32)
        for part in parts_in[1:]:
            signal = signal + part.astype(F32)
        signal = signal.astype(BF16).reshape(channels, -1)
        gathered = lax.all_to_all(signal, "ch", split_axis=1, concat_axis=0, tiled=True)
        matrix = decoder
    decoded = lax.dot_general(
        gathered, matrix, (((0,), (0,)), ((), ())), preferred_element_type=F32
    )
    return decoded.astype(BF16)


def solution(mesh):
    body = functools.partial(per_device, mesh.shape["src"], mesh.shape["ch"])
    return jax.shard_map(
        body,
        mesh=mesh,
        in_specs=(P(("src", "ch"), None), P("src", None, "ch", None, None), P("src"), P()),
        out_specs=P(("src", "ch"), None),
        check_vma=False,
    )
```

```python
import functools
import math

import jax
import jax.numpy as jnp
import ml_dtypes
import numpy as np
from jax import lax
from jax.experimental import pallas as pl
from jax.experimental.pallas import tpu as pltpu
from jax.sharding import PartitionSpec as P

BF16 = jnp.bfloat16
F32 = jnp.float32
LANES = 256
SLAB = 128
GROUP = 4
COST = pl.CostEstimate(flops=2**20, bytes_accessed=2**16, transcendentals=0)
ROWS = 4
STEPS = 24
SEGS = 2
KEEP = 16


def bf16_table(values):
    return np.asarray(values, dtype=np.float32).astype(ml_dtypes.bfloat16)


@functools.lru_cache(maxsize=None)
def block_tables(block_len):
    size = 2 * block_len
    n = np.arange(block_len)[:, None]
    k = np.arange(block_len)[None, :]
    angle = ((n * k) % size) * (2.0 * math.pi / size)
    fwd_real = np.cos(angle)
    fwd_imag = np.where(k == 0, 1.0 - 2.0 * (n % 2), -np.sin(angle))
    kk = np.arange(block_len)[:, None]
    m = np.arange(block_len)[None, :] + block_len
    angle = ((kk * m) % size) * (2.0 * math.pi / size)
    weight = np.where(kk == 0, 1.0, 2.0)
    inv_real = weight * np.cos(angle) / size
    inv_imag = np.where(kk == 0, (1.0 - 2.0 * (m % 2)) / size, -2.0 * np.sin(angle) / size)
    def slabs(pair):
        return bf16_table(np.stack(pair).reshape(2, block_len, -1, SLAB).transpose(0, 2, 1, 3))

    return slabs([fwd_real, fwd_imag]), slabs([inv_real, inv_imag])


@functools.lru_cache(maxsize=None)
def step_tables(parts, frames, channels):
    half = STEPS // 2
    theta = 2.0 * math.pi * (np.arange(STEPS) + 0.5) / STEPS
    first = (np.arange(STEPS) < half).astype(np.float64)[:, None]

    def forward(steps):
        cos = np.cos(theta[:, None] * steps[None, :])
        sin = np.sin(theta[:, None] * steps[None, :])
        plain = np.block([[cos, sin], [-sin, cos]])
        packed = np.block([[cos * first, cos * (1 - first)], [-sin * first, -sin * (1 - first)]])
        return plain, packed

    spec = np.zeros((2, SEGS, 2, STEPS, 2, frames))
    used = parts - 1 + KEEP
    for kind, table in enumerate(forward(np.arange(used))):
        table = table.reshape(2, STEPS, 2, used)
        for seg in range(SEGS):
            spec[kind, seg, :, :, :, seg * KEEP : seg * KEEP + used] = table
    spec = spec.reshape(2, SEGS * 2 * STEPS, 2 * frames)
    spec = np.stack([np.kron(np.eye(2), one) for one in spec])

    resp = np.zeros((channels // 2, 2, 2, STEPS, 2, parts, channels, 2))
    for kind, table in enumerate(forward(np.arange(parts))):
        table = table.reshape(2, STEPS, 2, parts).transpose(0, 1, 3, 2)
        for c in range(channels):
            resp[c // 2, :, c % 2, :, kind, :, c] = table
    resp = resp.reshape(channels * 2 * STEPS, 2 * parts * channels * 2)

    back = np.zeros((2, 2, 2, SEGS, KEEP, SEGS, 2, 2, STEPS))
    steps = np.arange(KEEP) + parts - 1
    cos = np.cos(theta[None, :] * steps[:, None]) / STEPS
    sin = np.sin(theta[None, :] * steps[:, None]) / STEPS
    firsts = first[:, 0][None, :]
    for seg in range(SEGS):
        for c in range(2):
            back[0, c, 0, seg, :, seg, 0, c] = cos
            back[0, c, 0, seg, :, seg, 1, c] = -sin
            back[0, c, 1, seg, :, seg, 0, c] = sin
            back[0, c, 1, seg, :, seg, 1, c] = cos
            back[1, c, 0, seg, :, seg, 0, c] = 2 * cos * firsts
            back[1, c, 0, seg, :, seg, 1, c] = -2 * sin * firsts
            back[1, c, 1, seg, :, seg, 0, c] = 2 * cos * (1 - firsts)
            back[1, c, 1, seg, :, seg, 1, c] = -2 * sin * (1 - firsts)
    back = back.reshape(2, 4 * SEGS * KEEP, 4 * SEGS * STEPS)
    return bf16_table(spec), bf16_table(resp), bf16_table(back)


def dot(left, right):
    return jnp.dot(left, right, preferred_element_type=F32)


def lane_masks(start, width):
    lane = lax.broadcasted_iota(jnp.int32, (1, width), 1) + start
    packed = (lane == 0).astype(F32)
    sign = (1 - 2 * (lane % 2)).astype(F32)
    return 1.0 - packed, packed, sign


def two_slabs(ref, step, *index):
    first = step * (LANES // SLAB)
    return jnp.concatenate([ref[(*index, first + i)] for i in range(LANES // SLAB)], axis=-1)


def response_kernel(rows, bins, me_ref, room_hbm, table_hbm, hat_ref, done_ref, room_ref, table_ref, sems):
    depth = room_ref.shape[1] * room_ref.shape[2] * 2
    flat = room_ref.reshape(rows, depth, bins)
    plain, packed, _ = lane_masks(0, LANES)
    plain, packed = plain.astype(BF16), packed.astype(BF16)

    def copy(r):
        return pltpu.make_async_copy(room_hbm.at[r], room_ref.at[r], sems.at[r])

    table_copy = pltpu.make_async_copy(table_hbm, table_ref, sems.at[rows])
    table_copy.start()
    for r in range(rows):
        copy(r).start()
    table_copy.wait()

    def some(outer, carry):
        for inner in range(ROWS):
            copy(outer * ROWS + inner).wait()
        for inner in range(ROWS):
            r = outer * ROWS + inner
            for step in range(bins // LANES):
                h = flat[r, :, step * LANES : (step + 1) * LANES]
                if step == 0:
                    h = jnp.concatenate([h * plain, h * packed], axis=0)
                    hat = dot(table_ref[...], h)
                else:
                    hat = dot(table_ref[:, :depth], h)
                hat = hat.astype(BF16)
                for i in range(LANES // SLAB):
                    hat_ref[r, step * (LANES // SLAB) + i] = hat[:, i * SLAB : (i + 1) * SLAB]
        return carry

    lax.fori_loop(0, rows // ROWS, some, 0)
    done_ref[...] = jnp.zeros_like(done_ref)


def transform_responses(room, me):
    rows, parts, channels, _, bins = room.shape
    slabs = bins // SLAB
    _, resp, _ = step_tables(parts, parts + SEGS * KEEP, channels)
    hbm = pl.BlockSpec(memory_space=pltpu.HBM)
    return pl.pallas_call(
        functools.partial(response_kernel, rows, bins),
        in_specs=[pl.BlockSpec(memory_space=pltpu.SMEM), hbm, hbm],
        out_specs=[pl.BlockSpec(memory_space=pltpu.VMEM)] * 2,
        out_shape=[
            pltpu.VMEM((rows, slabs, channels * 2 * STEPS, SLAB), BF16),
            jax.ShapeDtypeStruct((8, 128), F32),
        ],
        scratch_shapes=[
            pltpu.VMEM(room.shape, BF16),
            pltpu.VMEM(resp.shape, BF16),
            pltpu.SemaphoreType.DMA((rows + 1,)),
        ],
        compiler_params=pltpu.CompilerParams(vmem_limit_bytes=8 * 2**20),
        cost_estimate=COST,
    )(
        me,
        pltpu.with_memory_space_constraint(room, pltpu.HBM),
        pltpu.with_memory_space_constraint(jnp.asarray(resp), pltpu.HBM),
    )


def spectra_kernel(pieces, rows, *refs):
    x_refs, (table_ref, spec_ref) = refs[:pieces], refs[pieces : pieces + 2]
    out_ref = refs[-1]
    slabs = table_ref.shape[1]
    wide = 2 * SEGS * STEPS
    x = jnp.concatenate([ref[...] for ref in x_refs], axis=0)
    count = x.shape[0] // rows
    cols = 2 * count
    for step in range(slabs * SLAB // LANES):
        plain, packed, sign = lane_masks(step * LANES, LANES)
        spectra = []
        for j in range(2):
            one = dot(x, two_slabs(table_ref, step, j))
            spectra.append(one + sign * pltpu.roll(one, one.shape[0] - 1, axis=0))
        for start in range(0, rows, 2):
            some = range(start, min(start + 2, rows))
            n = len(some)
            both = [s[r * count : (r + 1) * count] for r in some for s in spectra]
            both = jnp.concatenate(both, axis=0)
            spec = [spec_ref[kind, : n * wide, : n * cols] for kind in range(2)]
            if step == 0:
                hat = dot(spec[0], (both * plain).astype(BF16)) + dot(spec[1], (both * packed).astype(BF16))
            else:
                hat = dot(spec[0], both.astype(BF16))
            hat = hat.astype(BF16)
            for k, r in enumerate(some):
                for i in range(LANES // SLAB):
                    at = slice(i * SLAB, (i + 1) * SLAB)
                    out_ref[step * (LANES // SLAB) + i, r] = hat[k * wide : (k + 1) * wide, at]


def transform_signals(x_list, own, bins, parts, after=None):
    frames = parts + SEGS * KEEP
    rows = own * len(x_list)
    slabs = bins // SLAB
    table, _ = block_tables(bins)
    spec, _, _ = step_tables(parts, frames, 2)
    vmem = pl.BlockSpec(memory_space=pltpu.VMEM)
    operands = [*x_list, jnp.asarray(table), jnp.asarray(spec)]
    if after is not None:
        operands.append(after)
    return pl.pallas_call(
        functools.partial(spectra_kernel, len(x_list), rows),
        in_specs=[vmem] * len(operands),
        out_specs=vmem,
        out_shape=jax.ShapeDtypeStruct((slabs, rows, 2 * SEGS * STEPS, SLAB), BF16),
        compiler_params=pltpu.CompilerParams(vmem_limit_bytes=8 * 2**20),
        cost_estimate=COST,
    )(*operands)


def mix_kernel(flips, own, channels, blocks, shares, has_total, last, me_ref, slot_ref, *refs):
    refs = list(refs)
    s_refs = [refs.pop(0) for _ in flips]
    hat_ref = refs.pop(0)
    total_ref = refs.pop(0) if has_total else None
    if last:
        back_ref, inv_ref = refs.pop(0), refs.pop(0)
        out_refs = [refs.pop(0) for _ in range(shares)]
        y_ref, left_re, left_im, time_ref = refs
    else:
        (out_ref,) = refs

    slabs = hat_ref.shape[1]
    steps = slabs * SLAB // LANES
    half = 2 * STEPS
    pairs = channels // 2
    sources = []
    for ref, some in zip(s_refs, flips):
        for k, flip in enumerate(some):
            for i in range(own):
                slot = lax.rem(slot_ref[(me_ref[1] ^ flip) * own + i], hat_ref.shape[0])
                sources.append((ref, k * own + i, slot))
    groups = -(-len(sources) // GROUP)
    size = -(-len(sources) // groups)

    def twice(rows):
        rows = rows.astype(F32)
        return jnp.concatenate([rows, rows], axis=0).astype(BF16)

    def products(slab, seg):
        re_in = slice(2 * seg * STEPS, (2 * seg + 1) * STEPS)
        im_in = slice((2 * seg + 1) * STEPS, (2 * seg + 2) * STEPS)
        re_rows = slice(2 * seg * half, (2 * seg + 1) * half)
        im_rows = slice((2 * seg + 1) * half, (2 * seg + 2) * half)
        spectra = [(twice(ref[slab, r, re_in]), twice(ref[slab, r, im_in])) for ref, r, _ in sources]
        for pair in range(pairs):
            base = pair * 2 * half
            re_sum = total_ref[slab, pair, re_rows] if has_total else None
            im_sum = total_ref[slab, pair, im_rows] if has_total else None
            for start in range(0, len(sources), size):
                re, im = None, None
                for (s_re, s_im), (_, _, slot) in list(zip(spectra, sources))[start : start + size]:
                    h_re = hat_ref[slot, slab, base : base + half]
                    h_im = hat_ref[slot, slab, base + half : base + 2 * half]
                    add_re = s_re * h_re - s_im * h_im
                    add_im = s_re * h_im + s_im * h_re
                    re = add_re if re is None else re + add_re
                    im = add_im if im is None else im + add_im
                re, im = re.astype(F32), im.astype(F32)
                re_sum = re if re_sum is None else re_sum + re
                im_sum = im if im_sum is None else im_sum + im
            if last:
                y_ref[slab, pair, re_rows] = re_sum.astype(BF16)
                y_ref[slab, pair, im_rows] = im_sum.astype(BF16)
            else:
                out_ref[slab, pair, re_rows] = re_sum
                out_ref[slab, pair, im_rows] = im_sum

    for step in range(steps):
        first = step * (LANES // SLAB)
        for i in range(LANES // SLAB):
            for seg in range(SEGS):
                products(first + i, seg)
        if not last:
            continue
        for pair in range(pairs):
            y = jnp.concatenate([y_ref[first + i, pair] for i in range(LANES // SLAB)], axis=-1)
            if step == 0:
                plain, packed, _ = lane_masks(0, LANES)
                mix = dot(back_ref[0], y * plain.astype(BF16)) + dot(back_ref[1], y * packed.astype(BF16))
            else:
                mix = dot(back_ref[0], y)
            mix = mix.astype(BF16)
            here = slice(step * LANES, (step + 1) * LANES)
            for c in range(2):
                rows_to = slice((2 * pair + c) * blocks, (2 * pair + c + 1) * blocks)
                left_re[rows_to, here] = mix[2 * c * blocks : (2 * c + 1) * blocks]
                left_im[rows_to, here] = mix[(2 * c + 1) * blocks : (2 * c + 2) * blocks]

    if last:
        each = blocks // shares
        for step in range(steps):
            here = slice(step * LANES, (step + 1) * LANES)
            part = dot(left_re[...], two_slabs(inv_ref, step, 0)) + dot(left_im[...], two_slabs(inv_ref, step, 1))
            for t in range(shares):
                for c in range(channels):
                    row = c * blocks + t * each
                    time_ref[t, c, :, here] = part[row : row + each]
        for d in range(shares):
            out_refs[d][...] = time_ref[me_ref[0] ^ d].astype(BF16)


def add_sources(s_list, flips, own, me, slots, hat, total, last, shares, channels, parts):
    slabs = hat.shape[1]
    bins = slabs * SLAB
    frames = parts + SEGS * KEEP
    blocks = frames - parts
    wide = 2 * SEGS * STEPS
    _, inverse = block_tables(bins)
    _, _, back = step_tables(parts, frames, channels)
    vmem = pl.BlockSpec(memory_space=pltpu.VMEM)
    smem = pl.BlockSpec(memory_space=pltpu.SMEM)

    operands = [me, slots] + list(s_list) + [pltpu.with_memory_space_constraint(hat, pltpu.VMEM)]
    aliases = {}
    if total is not None:
        if not last:
            aliases = {len(operands): 0}
        operands.append(total)
    scratch = []
    if last:
        operands += [jnp.asarray(back), jnp.asarray(inverse)]
        each = blocks // shares
        out_shape = [jax.ShapeDtypeStruct((channels, each, bins), BF16)] * shares
        scratch = [
            pltpu.VMEM((slabs, channels // 2, 2 * wide, SLAB), BF16),
            pltpu.VMEM((channels * blocks, bins), BF16),
            pltpu.VMEM((channels * blocks, bins), BF16),
            pltpu.VMEM((shares, channels, each, bins), F32),
        ]
    else:
        out_shape = jax.ShapeDtypeStruct((slabs, channels // 2, 2 * wide, SLAB), F32)
    body = functools.partial(
        mix_kernel, tuple(flips), own, channels, blocks, shares, total is not None, last
    )
    return pl.pallas_call(
        body,
        in_specs=[smem, smem] + [vmem] * (len(operands) - 2),
        out_specs=[vmem] * shares if last else vmem,
        out_shape=out_shape,
        scratch_shapes=scratch,
        input_output_aliases=aliases,
        compiler_params=pltpu.CompilerParams(vmem_limit_bytes=12 * 2**20),
        cost_estimate=COST,
    )(*operands)


def sum_kernel(count, each, me_ref, *refs):
    parts, outs, sum_ref = refs[:count], refs[count:-1], refs[-1]
    total = parts[0][...].astype(F32)
    for part in parts[1:]:
        total = total + part[...].astype(F32)
    sum_ref[...] = total
    for d in range(each):
        outs[d][...] = sum_ref[:, pl.ds(me_ref[0] ^ d, 1), :].reshape(outs[d].shape).astype(BF16)


def sum_groups(parts, me):
    channels, each, bins = parts[0].shape
    vmem = pl.BlockSpec(memory_space=pltpu.VMEM)
    return pl.pallas_call(
        functools.partial(sum_kernel, len(parts), each),
        in_specs=[pl.BlockSpec(memory_space=pltpu.SMEM)] + [vmem] * len(parts),
        out_specs=[vmem] * each,
        out_shape=[jax.ShapeDtypeStruct((channels, bins), BF16)] * each,
        scratch_shapes=[pltpu.VMEM(parts[0].shape, F32)],
        compiler_params=pltpu.CompilerParams(vmem_limit_bytes=8 * 2**20),
    )(me[None], *parts)


def per_device(src_count, ch_count, dry_signal, room_spectra, render_slot, decoder):
    rows_total, parts, channels, _, block_len = room_spectra.shape
    own = dry_signal.shape[0]
    frames = dry_signal.shape[1] // block_len
    blocks = frames - parts
    src_me = lax.axis_index("src").astype(jnp.int32)
    ch_me = lax.axis_index("ch").astype(jnp.int32)

    x_own = dry_signal.reshape(own * frames, block_len)

    def swap(value, axis, count, flip):
        return lax.ppermute(value, axis, [(i, i ^ flip) for i in range(count)])

    chips = ch_count // 2
    lanes = [swap(x_own, "ch", ch_count, 2 * d) for d in range(1, chips)]

    row = jnp.arange(ch_count * channels, dtype=jnp.int32)
    takes = ((row // channels) ^ ch_me) * channels + row % channels
    order = (takes[:, None] == row[None, :]).astype(BF16)
    own_order = dot(order, decoder).astype(BF16)

    me = jnp.stack([src_me, ch_me])
    hat, done = transform_responses(room_spectra, me)

    def add(s_list, flips, total, last):
        return add_sources(
            s_list, flips, own, me, render_slot, hat, total, last, src_count, channels, parts
        )

    def transform(x_list, after=None):
        mine = transform_signals(x_list, own, block_len, parts, after)
        return mine, swap(mine, "ch", ch_count, 1)

    near, far = range(0, 2), range(2, chips)
    near_mine, near_given = transform([x_own, lanes[0]], done)
    total = add([near_mine], [[2 * d for d in near]], None, False)
    *late, total = lax.optimization_barrier((*lanes[1:], total))
    far_mine, far_given = transform(late)
    flips = [[2 * d + 1 for d in near], [2 * d for d in far]]
    total = add([near_given, far_mine], flips, total, False)
    total = add([far_given], [[2 * d + 1 for d in far]], total, True)

    parts_in = [total[0]] + [swap(total[d], "src", src_count, d) for d in range(1, src_count)]
    each = blocks // src_count
    if each == ch_count:
        pieces = sum_groups(parts_in, ch_me)
        given = swap(jnp.concatenate(pieces[1::2], axis=0), "ch", ch_count, 1)
        both = [
            jnp.concatenate([pieces[2 * d], given[d * channels : (d + 1) * channels]], axis=0)
            for d in range(chips)
        ]
        both[1:] = [swap(both[d], "ch", ch_count, 2 * d) for d in range(1, chips)]
        gathered = jnp.concatenate(both, axis=0)
        matrix = own_order
    else:
        signal = parts_in[0].astype(F32)
        for part in parts_in[1:]:
            signal = signal + part.astype(F32)
        signal = signal.astype(BF16).reshape(channels, -1)
        gathered = lax.all_to_all(signal, "ch", split_axis=1, concat_axis=0, tiled=True)
        matrix = decoder
    decoded = lax.dot_general(
        gathered, matrix, (((0,), (0,)), ((), ())), preferred_element_type=F32
    )
    return decoded.astype(BF16)


def solution(mesh):
    body = functools.partial(per_device, mesh.shape["src"], mesh.shape["ch"])
    return jax.shard_map(
        body,
        mesh=mesh,
        in_specs=(P(("src", "ch"), None), P("src", None, "ch", None, None), P("src"), P()),
        out_specs=P(("src", "ch"), None),
        check_vma=False,
    )
```

```python
import functools
import math

import jax
import jax.numpy as jnp
import ml_dtypes
import numpy as np
from jax import lax
from jax.experimental import pallas as pl
from jax.experimental.pallas import tpu as pltpu
from jax.sharding import PartitionSpec as P

BF16 = jnp.bfloat16
F32 = jnp.float32
LANES = 256
SLAB = 128
GROUP = 4
COST = pl.CostEstimate(flops=2**20, bytes_accessed=2**16, transcendentals=0)
ROWS = 4
STEPS = 24
SEGS = 2
KEEP = 16


def bf16_table(values):
    return np.asarray(values, dtype=np.float32).astype(ml_dtypes.bfloat16)


@functools.lru_cache(maxsize=None)
def block_tables(block_len):
    size = 2 * block_len
    n = np.arange(block_len)[:, None]
    k = np.arange(block_len)[None, :]
    angle = ((n * k) % size) * (2.0 * math.pi / size)
    fwd_real = np.cos(angle)
    fwd_imag = np.where(k == 0, 1.0 - 2.0 * (n % 2), -np.sin(angle))
    kk = np.arange(block_len)[:, None]
    m = np.arange(block_len)[None, :] + block_len
    angle = ((kk * m) % size) * (2.0 * math.pi / size)
    weight = np.where(kk == 0, 1.0, 2.0)
    inv_real = weight * np.cos(angle) / size
    inv_imag = np.where(kk == 0, (1.0 - 2.0 * (m % 2)) / size, -2.0 * np.sin(angle) / size)
    def slabs(pair):
        return bf16_table(np.stack(pair).reshape(2, block_len, -1, SLAB).transpose(0, 2, 1, 3))

    return slabs([fwd_real, fwd_imag]), slabs([inv_real, inv_imag])


@functools.lru_cache(maxsize=None)
def step_tables(parts, frames, channels, own=1):
    half = STEPS // 2
    theta = 2.0 * math.pi * (np.arange(STEPS) + 0.5) / STEPS
    first = (np.arange(STEPS) < half).astype(np.float64)[:, None]

    def forward(steps):
        cos = np.cos(theta[:, None] * steps[None, :])
        sin = np.sin(theta[:, None] * steps[None, :])
        plain = np.block([[cos, sin], [-sin, cos]])
        packed = np.block([[cos * first, cos * (1 - first)], [-sin * first, -sin * (1 - first)]])
        return plain, packed

    spec = np.zeros((2, SEGS, 2, STEPS, 2, frames))
    used = parts - 1 + KEEP
    for kind, table in enumerate(forward(np.arange(used))):
        table = table.reshape(2, STEPS, 2, used)
        for seg in range(SEGS):
            spec[kind, seg, :, :, :, seg * KEEP : seg * KEEP + used] = table
    spec = spec.reshape(2, 1, SEGS * 2 * STEPS, 2 * frames, 1) * np.eye(own)[None, :, None, None, :]
    spec = spec.reshape(2, own * SEGS * 2 * STEPS, 2 * frames * own)

    resp = np.zeros((channels // 2, 2, 2, STEPS, 2, parts, channels, 2))
    for kind, table in enumerate(forward(np.arange(parts))):
        table = table.reshape(2, STEPS, 2, parts).transpose(0, 1, 3, 2)
        for c in range(channels):
            resp[c // 2, :, c % 2, :, kind, :, c] = table
    resp = resp.reshape(channels * 2 * STEPS, 2 * parts * channels * 2)

    back = np.zeros((2, 2, 2, SEGS, KEEP, SEGS, 2, 2, STEPS))
    steps = np.arange(KEEP) + parts - 1
    cos = np.cos(theta[None, :] * steps[:, None]) / STEPS
    sin = np.sin(theta[None, :] * steps[:, None]) / STEPS
    firsts = first[:, 0][None, :]
    for seg in range(SEGS):
        for c in range(2):
            back[0, c, 0, seg, :, seg, 0, c] = cos
            back[0, c, 0, seg, :, seg, 1, c] = -sin
            back[0, c, 1, seg, :, seg, 0, c] = sin
            back[0, c, 1, seg, :, seg, 1, c] = cos
            back[1, c, 0, seg, :, seg, 0, c] = 2 * cos * firsts
            back[1, c, 0, seg, :, seg, 1, c] = -2 * sin * firsts
            back[1, c, 1, seg, :, seg, 0, c] = 2 * cos * (1 - firsts)
            back[1, c, 1, seg, :, seg, 1, c] = -2 * sin * (1 - firsts)
    back = back.reshape(2, 4 * SEGS * KEEP, 4 * SEGS * STEPS)
    return bf16_table(spec), bf16_table(resp), bf16_table(back)


def dot(left, right):
    return jnp.dot(left, right, preferred_element_type=F32)


def lane_masks(start, width):
    lane = lax.broadcasted_iota(jnp.int32, (1, width), 1) + start
    packed = (lane == 0).astype(F32)
    sign = (1 - 2 * (lane % 2)).astype(F32)
    return 1.0 - packed, packed, sign


def two_slabs(ref, step, *index):
    first = step * (LANES // SLAB)
    return jnp.concatenate([ref[(*index, first + i)] for i in range(LANES // SLAB)], axis=-1)


def response_kernel(rows, bins, me_ref, room_hbm, table_hbm, hat_ref, room_ref, table_ref, sems):
    depth = room_ref.shape[1] * room_ref.shape[2] * 2
    flat = room_ref.reshape(rows, depth, bins)
    plain, packed, _ = lane_masks(0, LANES)
    plain, packed = plain.astype(BF16), packed.astype(BF16)

    def copy(r):
        return pltpu.make_async_copy(room_hbm.at[r], room_ref.at[r], sems.at[r])

    table_copy = pltpu.make_async_copy(table_hbm, table_ref, sems.at[rows])
    table_copy.start()
    for r in range(rows):
        copy(r).start()
    table_copy.wait()

    def some(outer, carry):
        for inner in range(ROWS):
            copy(outer * ROWS + inner).wait()
        for inner in range(ROWS):
            r = outer * ROWS + inner
            for step in range(bins // LANES):
                h = flat[r, :, step * LANES : (step + 1) * LANES]
                if step == 0:
                    h = jnp.concatenate([h * plain, h * packed], axis=0)
                    hat = dot(table_ref[...], h)
                else:
                    hat = dot(table_ref[:, :depth], h)
                hat = hat.astype(BF16)
                for i in range(LANES // SLAB):
                    hat_ref[r, step * (LANES // SLAB) + i] = hat[:, i * SLAB : (i + 1) * SLAB]
        return carry

    lax.fori_loop(0, rows // ROWS, some, 0)


def transform_responses(room, me):
    rows, parts, channels, _, bins = room.shape
    slabs = bins // SLAB
    _, resp, _ = step_tables(parts, parts + SEGS * KEEP, channels)
    hbm = pl.BlockSpec(memory_space=pltpu.HBM)
    return pl.pallas_call(
        functools.partial(response_kernel, rows, bins),
        in_specs=[pl.BlockSpec(memory_space=pltpu.SMEM), hbm, hbm],
        out_specs=pl.BlockSpec(memory_space=pltpu.VMEM),
        out_shape=pltpu.VMEM((rows, slabs, channels * 2 * STEPS, SLAB), BF16),
        scratch_shapes=[
            pltpu.VMEM(room.shape, BF16),
            pltpu.VMEM(resp.shape, BF16),
            pltpu.SemaphoreType.DMA((rows + 1,)),
        ],
        compiler_params=pltpu.CompilerParams(vmem_limit_bytes=8 * 2**20),
        cost_estimate=COST,
    )(
        me,
        pltpu.with_memory_space_constraint(room, pltpu.HBM),
        pltpu.with_memory_space_constraint(jnp.asarray(resp), pltpu.HBM),
    )


def spectra_kernel(pieces, rows, *refs):
    x_refs, (table_ref, spec_ref, out_ref) = refs[:pieces], refs[pieces:]
    slabs = table_ref.shape[1]
    wide = 2 * SEGS * STEPS
    own = rows // pieces
    span = x_refs[0].shape[0] * own
    flat = x_refs if own == 1 else [ref.reshape(span, slabs * SLAB) for ref in x_refs]
    x = jnp.concatenate([ref[...] for ref in flat], axis=0)
    for step in range(slabs * SLAB // LANES):
        plain, packed, sign = lane_masks(step * LANES, LANES)
        spectra = []
        for j in range(2):
            one = dot(x, two_slabs(table_ref, step, j))
            spectra.append(one + sign * pltpu.roll(one, one.shape[0] - own, axis=0))
        for piece in range(pieces):
            both = [s[piece * span : (piece + 1) * span] for s in spectra]
            both = jnp.concatenate(both, axis=0)
            if step == 0:
                hat = dot(spec_ref[0], (both * plain).astype(BF16)) + dot(spec_ref[1], (both * packed).astype(BF16))
            else:
                hat = dot(spec_ref[0], both.astype(BF16))
            hat = hat.astype(BF16)
            for k in range(own):
                for i in range(LANES // SLAB):
                    at = slice(i * SLAB, (i + 1) * SLAB)
                    out_ref[step * (LANES // SLAB) + i, piece * own + k] = hat[k * wide : (k + 1) * wide, at]


def transform_signals(x_list, own, bins, parts):
    frames = parts + SEGS * KEEP
    rows = own * len(x_list)
    slabs = bins // SLAB
    table, _ = block_tables(bins)
    spec, _, _ = step_tables(parts, frames, 2, own)
    vmem = pl.BlockSpec(memory_space=pltpu.VMEM)
    operands = [*x_list, jnp.asarray(table), jnp.asarray(spec)]
    return pl.pallas_call(
        functools.partial(spectra_kernel, len(x_list), rows),
        in_specs=[vmem] * len(operands),
        out_specs=vmem,
        out_shape=jax.ShapeDtypeStruct((slabs, rows, 2 * SEGS * STEPS, SLAB), BF16),
        compiler_params=pltpu.CompilerParams(vmem_limit_bytes=8 * 2**20),
        cost_estimate=COST,
    )(*operands)


def mix_kernel(flips, own, channels, blocks, shares, has_total, last, me_ref, slot_ref, *refs):
    refs = list(refs)
    s_refs = [refs.pop(0) for _ in flips]
    hat_ref = refs.pop(0)
    total_ref = refs.pop(0) if has_total else None
    if last:
        back_ref, inv_ref = refs.pop(0), refs.pop(0)
        out_refs = [refs.pop(0) for _ in range(shares)]
        y_ref, left_re, left_im, time_ref = refs
    else:
        (out_ref,) = refs

    slabs = hat_ref.shape[1]
    steps = slabs * SLAB // LANES
    half = 2 * STEPS
    pairs = channels // 2
    sources = []
    for ref, some in zip(s_refs, flips):
        for k, flip in enumerate(some):
            for i in range(own):
                slot = lax.rem(slot_ref[(me_ref[1] ^ flip) * own + i], hat_ref.shape[0])
                sources.append((ref, k * own + i, slot))
    groups = -(-len(sources) // GROUP)
    size = -(-len(sources) // groups)

    def twice(rows):
        rows = rows.astype(F32)
        return jnp.concatenate([rows, rows], axis=0).astype(BF16)

    def products(slab, seg):
        re_in = slice(2 * seg * STEPS, (2 * seg + 1) * STEPS)
        im_in = slice((2 * seg + 1) * STEPS, (2 * seg + 2) * STEPS)
        re_rows = slice(2 * seg * half, (2 * seg + 1) * half)
        im_rows = slice((2 * seg + 1) * half, (2 * seg + 2) * half)
        spectra = [(twice(ref[slab, r, re_in]), twice(ref[slab, r, im_in])) for ref, r, _ in sources]
        for pair in range(pairs):
            base = pair * 2 * half
            re_sum = total_ref[slab, pair, re_rows] if has_total else None
            im_sum = total_ref[slab, pair, im_rows] if has_total else None
            for start in range(0, len(sources), size):
                re, im = None, None
                for (s_re, s_im), (_, _, slot) in list(zip(spectra, sources))[start : start + size]:
                    h_re = hat_ref[slot, slab, base : base + half]
                    h_im = hat_ref[slot, slab, base + half : base + 2 * half]
                    add_re = s_re * h_re - s_im * h_im
                    add_im = s_re * h_im + s_im * h_re
                    re = add_re if re is None else re + add_re
                    im = add_im if im is None else im + add_im
                re, im = re.astype(F32), im.astype(F32)
                re_sum = re if re_sum is None else re_sum + re
                im_sum = im if im_sum is None else im_sum + im
            if last:
                y_ref[slab, pair, re_rows] = re_sum.astype(BF16)
                y_ref[slab, pair, im_rows] = im_sum.astype(BF16)
            else:
                out_ref[slab, pair, re_rows] = re_sum
                out_ref[slab, pair, im_rows] = im_sum

    for step in range(steps):
        first = step * (LANES // SLAB)
        for i in range(LANES // SLAB):
            for seg in range(SEGS):
                products(first + i, seg)
        if not last:
            continue
        for pair in range(pairs):
            y = jnp.concatenate([y_ref[first + i, pair] for i in range(LANES // SLAB)], axis=-1)
            if step == 0:
                plain, packed, _ = lane_masks(0, LANES)
                mix = dot(back_ref[0], y * plain.astype(BF16)) + dot(back_ref[1], y * packed.astype(BF16))
            else:
                mix = dot(back_ref[0], y)
            mix = mix.astype(BF16)
            here = slice(step * LANES, (step + 1) * LANES)
            for c in range(2):
                rows_to = slice((2 * pair + c) * blocks, (2 * pair + c + 1) * blocks)
                left_re[rows_to, here] = mix[2 * c * blocks : (2 * c + 1) * blocks]
                left_im[rows_to, here] = mix[(2 * c + 1) * blocks : (2 * c + 2) * blocks]

    if last:
        each = blocks // shares
        for step in range(steps):
            here = slice(step * LANES, (step + 1) * LANES)
            part = dot(left_re[...], two_slabs(inv_ref, step, 0)) + dot(left_im[...], two_slabs(inv_ref, step, 1))
            for t in range(shares):
                for c in range(channels):
                    row = c * blocks + t * each
                    time_ref[t, c, :, here] = part[row : row + each]
        for d in range(shares):
            out_refs[d][...] = time_ref[me_ref[0] ^ d].astype(BF16)


def add_sources(s_list, flips, own, me, slots, hat, total, last, shares, channels, parts):
    slabs = hat.shape[1]
    bins = slabs * SLAB
    frames = parts + SEGS * KEEP
    blocks = frames - parts
    wide = 2 * SEGS * STEPS
    _, inverse = block_tables(bins)
    _, _, back = step_tables(parts, frames, channels)
    vmem = pl.BlockSpec(memory_space=pltpu.VMEM)
    smem = pl.BlockSpec(memory_space=pltpu.SMEM)

    operands = [me, slots] + list(s_list) + [pltpu.with_memory_space_constraint(hat, pltpu.VMEM)]
    aliases = {}
    if total is not None:
        if not last:
            aliases = {len(operands): 0}
        operands.append(total)
    scratch = []
    if last:
        operands += [jnp.asarray(back), jnp.asarray(inverse)]
        each = blocks // shares
        out_shape = [jax.ShapeDtypeStruct((channels, each, bins), BF16)] * shares
        scratch = [
            pltpu.VMEM((slabs, channels // 2, 2 * wide, SLAB), BF16),
            pltpu.VMEM((channels * blocks, bins), BF16),
            pltpu.VMEM((channels * blocks, bins), BF16),
            pltpu.VMEM((shares, channels, each, bins), F32),
        ]
    else:
        out_shape = jax.ShapeDtypeStruct((slabs, channels // 2, 2 * wide, SLAB), F32)
    body = functools.partial(
        mix_kernel, tuple(flips), own, channels, blocks, shares, total is not None, last
    )
    return pl.pallas_call(
        body,
        in_specs=[smem, smem] + [vmem] * (len(operands) - 2),
        out_specs=[vmem] * shares if last else vmem,
        out_shape=out_shape,
        scratch_shapes=scratch,
        input_output_aliases=aliases,
        compiler_params=pltpu.CompilerParams(vmem_limit_bytes=12 * 2**20),
        cost_estimate=COST,
    )(*operands)


def sum_kernel(count, each, me_ref, *refs):
    parts, outs, sum_ref = refs[:count], refs[count:-1], refs[-1]
    total = parts[0][...].astype(F32)
    for part in parts[1:]:
        total = total + part[...].astype(F32)
    sum_ref[...] = total
    for d in range(each):
        outs[d][...] = sum_ref[:, pl.ds(me_ref[0] ^ d, 1), :].reshape(outs[d].shape).astype(BF16)


def sum_groups(parts, me):
    channels, each, bins = parts[0].shape
    vmem = pl.BlockSpec(memory_space=pltpu.VMEM)
    return pl.pallas_call(
        functools.partial(sum_kernel, len(parts), each),
        in_specs=[pl.BlockSpec(memory_space=pltpu.SMEM)] + [vmem] * len(parts),
        out_specs=[vmem] * each,
        out_shape=[jax.ShapeDtypeStruct((channels, bins), BF16)] * each,
        scratch_shapes=[pltpu.VMEM(parts[0].shape, F32)],
        compiler_params=pltpu.CompilerParams(vmem_limit_bytes=8 * 2**20),
    )(me[None], *parts)


def per_device(src_count, ch_count, dry_signal, room_spectra, render_slot, decoder):
    rows_total, parts, channels, _, block_len = room_spectra.shape
    own = dry_signal.shape[0]
    frames = dry_signal.shape[1] // block_len
    blocks = frames - parts
    src_me = lax.axis_index("src").astype(jnp.int32)
    ch_me = lax.axis_index("ch").astype(jnp.int32)

    if own == 1:
        x_own = dry_signal.reshape(frames, block_len)
    else:
        x_own = dry_signal.reshape(own, frames, block_len).transpose(1, 0, 2)

    def swap(value, axis, count, flip):
        return lax.ppermute(value, axis, [(i, i ^ flip) for i in range(count)])

    chips = ch_count // 2
    first = chips // 2
    lanes = {first: swap(x_own, "ch", ch_count, 2 * first)}
    me = jnp.stack([src_me, ch_me])
    hat = transform_responses(room_spectra, me)
    x_own, hat = lax.optimization_barrier((x_own, hat))
    rest = [d for d in range(chips - 1, 0, -1) if d != first]
    lanes.update({d: swap(x_own, "ch", ch_count, 2 * d) for d in rest})

    row = jnp.arange(ch_count * channels, dtype=jnp.int32)
    takes = ((row // channels) ^ ch_me) * channels + row % channels
    order = (takes[:, None] == row[None, :]).astype(BF16)
    own_order = dot(order, decoder).astype(BF16)

    def add(s_list, flips, total, last):
        return add_sources(
            s_list, flips, own, me, render_slot, hat, total, last, src_count, channels, parts
        )

    def transform(x_list):
        mine = transform_signals(x_list, own, block_len, parts)
        return mine, swap(mine, "ch", ch_count, 1)

    near_mine, near_given = transform([x_own, lanes[first]])
    total = add([near_mine], [[0, 2 * first]], None, False)
    *late, total = lax.optimization_barrier((*[lanes[d] for d in rest], total))
    far_mine, far_given = transform(late)
    total = add([near_given, far_mine], [[1, 2 * first + 1], [2 * d for d in rest]], total, False)
    total = add([far_given], [[2 * d + 1 for d in rest]], total, True)

    parts_in = [total[0]] + [swap(total[d], "src", src_count, d) for d in range(1, src_count)]
    each = blocks // src_count
    if each == ch_count:
        pieces = sum_groups(parts_in, ch_me)
        given = swap(jnp.concatenate(pieces[1::2], axis=0), "ch", ch_count, 1)
        both = [
            jnp.concatenate([pieces[2 * d], given[d * channels : (d + 1) * channels]], axis=0)
            for d in range(chips)
        ]
        both[1:] = [swap(both[d], "ch", ch_count, 2 * d) for d in range(1, chips)]
        gathered = jnp.concatenate(both, axis=0)
        matrix = own_order
    else:
        signal = parts_in[0].astype(F32)
        for part in parts_in[1:]:
            signal = signal + part.astype(F32)
        signal = signal.astype(BF16).reshape(channels, -1)
        gathered = lax.all_to_all(signal, "ch", split_axis=1, concat_axis=0, tiled=True)
        matrix = decoder
    decoded = lax.dot_general(
        gathered, matrix, (((0,), (0,)), ((), ())), preferred_element_type=F32
    )
    return decoded.astype(BF16)


def solution(mesh):
    body = functools.partial(per_device, mesh.shape["src"], mesh.shape["ch"])
    return jax.shard_map(
        body,
        mesh=mesh,
        in_specs=(P(("src", "ch"), None), P("src", None, "ch", None, None), P("src"), P()),
        out_specs=P(("src", "ch"), None),
        check_vma=False,
    )
```

```python
import functools
import math

import jax
import jax.numpy as jnp
import ml_dtypes
import numpy as np
from jax import lax
from jax.experimental import pallas as pl
from jax.experimental.pallas import tpu as pltpu
from jax.sharding import PartitionSpec as P

BF16 = jnp.bfloat16
F32 = jnp.float32
LANES = 256
SLAB = 128
GROUP = 4
COST = pl.CostEstimate(flops=2**20, bytes_accessed=2**16, transcendentals=0)
ROWS = 4
STEPS = 24
SEGS = 2
KEEP = 16


def bf16_table(values):
    return np.asarray(values, dtype=np.float32).astype(ml_dtypes.bfloat16)


@functools.lru_cache(maxsize=None)
def block_tables(block_len):
    size = 2 * block_len
    n = np.arange(block_len)[:, None]
    k = np.arange(block_len)[None, :]
    angle = ((n * k) % size) * (2.0 * math.pi / size)
    fwd_real = np.cos(angle)
    fwd_imag = np.where(k == 0, 1.0 - 2.0 * (n % 2), -np.sin(angle))
    kk = np.arange(block_len)[:, None]
    m = np.arange(block_len)[None, :] + block_len
    angle = ((kk * m) % size) * (2.0 * math.pi / size)
    weight = np.where(kk == 0, 1.0, 2.0)
    inv_real = weight * np.cos(angle) / size
    inv_imag = np.where(kk == 0, (1.0 - 2.0 * (m % 2)) / size, -2.0 * np.sin(angle) / size)
    def slabs(pair):
        return bf16_table(np.stack(pair).reshape(2, block_len, -1, SLAB).transpose(0, 2, 1, 3))

    return slabs([fwd_real, fwd_imag]), slabs([inv_real, inv_imag])


@functools.lru_cache(maxsize=None)
def step_tables(parts, frames, channels, own=1):
    half = STEPS // 2
    theta = 2.0 * math.pi * (np.arange(STEPS) + 0.5) / STEPS
    first = (np.arange(STEPS) < half).astype(np.float64)[:, None]

    def forward(steps):
        cos = np.cos(theta[:, None] * steps[None, :])
        sin = np.sin(theta[:, None] * steps[None, :])
        plain = np.block([[cos, sin], [-sin, cos]])
        packed = np.block([[cos * first, cos * (1 - first)], [-sin * first, -sin * (1 - first)]])
        return plain, packed

    spec = np.zeros((2, SEGS, 2, STEPS, 2, frames))
    used = parts - 1 + KEEP
    for kind, table in enumerate(forward(np.arange(used))):
        table = table.reshape(2, STEPS, 2, used)
        for seg in range(SEGS):
            spec[kind, seg, :, :, :, seg * KEEP : seg * KEEP + used] = table
    spec = spec.reshape(2, 1, SEGS * 2 * STEPS, 2 * frames, 1) * np.eye(own)[None, :, None, None, :]
    spec = spec.reshape(2, own * SEGS * 2 * STEPS, 2 * frames * own)

    resp = np.zeros((channels // 2, 2, 2, STEPS, 2, parts, channels, 2))
    for kind, table in enumerate(forward(np.arange(parts))):
        table = table.reshape(2, STEPS, 2, parts).transpose(0, 1, 3, 2)
        for c in range(channels):
            resp[c // 2, :, c % 2, :, kind, :, c] = table
    resp = resp.reshape(channels * 2 * STEPS, 2 * parts * channels * 2)

    back = np.zeros((2, 2, 2, SEGS, KEEP, SEGS, 2, 2, STEPS))
    steps = np.arange(KEEP) + parts - 1
    cos = np.cos(theta[None, :] * steps[:, None]) / STEPS
    sin = np.sin(theta[None, :] * steps[:, None]) / STEPS
    firsts = first[:, 0][None, :]
    for seg in range(SEGS):
        for c in range(2):
            back[0, c, 0, seg, :, seg, 0, c] = cos
            back[0, c, 0, seg, :, seg, 1, c] = -sin
            back[0, c, 1, seg, :, seg, 0, c] = sin
            back[0, c, 1, seg, :, seg, 1, c] = cos
            back[1, c, 0, seg, :, seg, 0, c] = 2 * cos * firsts
            back[1, c, 0, seg, :, seg, 1, c] = -2 * sin * firsts
            back[1, c, 1, seg, :, seg, 0, c] = 2 * cos * (1 - firsts)
            back[1, c, 1, seg, :, seg, 1, c] = -2 * sin * (1 - firsts)
    back = back.reshape(2, 4 * SEGS * KEEP, 4 * SEGS * STEPS)
    return bf16_table(spec), bf16_table(resp), bf16_table(back)


def dot(left, right):
    return jnp.dot(left, right, preferred_element_type=F32)


def lane_masks(start, width):
    lane = lax.broadcasted_iota(jnp.int32, (1, width), 1) + start
    packed = (lane == 0).astype(F32)
    sign = (1 - 2 * (lane % 2)).astype(F32)
    return 1.0 - packed, packed, sign


def two_slabs(ref, step, *index):
    first = step * (LANES // SLAB)
    return jnp.concatenate([ref[(*index, first + i)] for i in range(LANES // SLAB)], axis=-1)


def response_kernel(rows, bins, me_ref, room_hbm, table_hbm, hat_ref, room_ref, table_ref, sems):
    depth = room_ref.shape[1] * room_ref.shape[2] * 2
    flat = room_ref.reshape(rows, depth, bins)
    plain, packed, _ = lane_masks(0, LANES)
    plain, packed = plain.astype(BF16), packed.astype(BF16)

    def copy(r):
        return pltpu.make_async_copy(room_hbm.at[r], room_ref.at[r], sems.at[r])

    table_copy = pltpu.make_async_copy(table_hbm, table_ref, sems.at[rows])
    table_copy.start()
    for r in range(rows):
        copy(r).start()
    table_copy.wait()

    def some(outer, carry):
        for inner in range(ROWS):
            copy(outer * ROWS + inner).wait()
        for inner in range(ROWS):
            r = outer * ROWS + inner
            for step in range(bins // LANES):
                h = flat[r, :, step * LANES : (step + 1) * LANES]
                if step == 0:
                    h = jnp.concatenate([h * plain, h * packed], axis=0)
                    hat = dot(table_ref[...], h)
                else:
                    hat = dot(table_ref[:, :depth], h)
                hat = hat.astype(BF16)
                for i in range(LANES // SLAB):
                    hat_ref[r, step * (LANES // SLAB) + i] = hat[:, i * SLAB : (i + 1) * SLAB]
        return carry

    lax.fori_loop(0, rows // ROWS, some, 0)


def transform_responses(room, me):
    rows, parts, channels, _, bins = room.shape
    slabs = bins // SLAB
    _, resp, _ = step_tables(parts, parts + SEGS * KEEP, channels)
    hbm = pl.BlockSpec(memory_space=pltpu.HBM)
    return pl.pallas_call(
        functools.partial(response_kernel, rows, bins),
        in_specs=[pl.BlockSpec(memory_space=pltpu.SMEM), hbm, hbm],
        out_specs=pl.BlockSpec(memory_space=pltpu.VMEM),
        out_shape=pltpu.VMEM((rows, slabs, channels * 2 * STEPS, SLAB), BF16),
        scratch_shapes=[
            pltpu.VMEM(room.shape, BF16),
            pltpu.VMEM(resp.shape, BF16),
            pltpu.SemaphoreType.DMA((rows + 1,)),
        ],
        compiler_params=pltpu.CompilerParams(vmem_limit_bytes=8 * 2**20),
        cost_estimate=COST,
    )(
        me,
        pltpu.with_memory_space_constraint(room, pltpu.HBM),
        pltpu.with_memory_space_constraint(jnp.asarray(resp), pltpu.HBM),
    )


def spectra_kernel(pieces, rows, *refs):
    x_refs, (table_ref, spec_ref, out_ref) = refs[:pieces], refs[pieces:]
    slabs = table_ref.shape[1]
    wide = 2 * SEGS * STEPS
    own = rows // pieces
    span = x_refs[0].shape[0] * own
    flat = x_refs if own == 1 else [ref.reshape(span, slabs * SLAB) for ref in x_refs]
    x = jnp.concatenate([ref[...] for ref in flat], axis=0)
    for step in range(slabs * SLAB // LANES):
        plain, packed, sign = lane_masks(step * LANES, LANES)
        spectra = []
        for j in range(2):
            one = dot(x, two_slabs(table_ref, step, j))
            spectra.append(one + sign * pltpu.roll(one, one.shape[0] - own, axis=0))
        for piece in range(pieces):
            both = [s[piece * span : (piece + 1) * span] for s in spectra]
            both = jnp.concatenate(both, axis=0)
            if step == 0:
                hat = dot(spec_ref[0], (both * plain).astype(BF16)) + dot(spec_ref[1], (both * packed).astype(BF16))
            else:
                hat = dot(spec_ref[0], both.astype(BF16))
            hat = hat.astype(BF16)
            for k in range(own):
                for i in range(LANES // SLAB):
                    at = slice(i * SLAB, (i + 1) * SLAB)
                    out_ref[step * (LANES // SLAB) + i, piece * own + k] = hat[k * wide : (k + 1) * wide, at]


def transform_signals(x_list, own, bins, parts):
    frames = parts + SEGS * KEEP
    rows = own * len(x_list)
    slabs = bins // SLAB
    table, _ = block_tables(bins)
    spec, _, _ = step_tables(parts, frames, 2, own)
    vmem = pl.BlockSpec(memory_space=pltpu.VMEM)
    operands = [*x_list, jnp.asarray(table), jnp.asarray(spec)]
    return pl.pallas_call(
        functools.partial(spectra_kernel, len(x_list), rows),
        in_specs=[vmem] * len(operands),
        out_specs=vmem,
        out_shape=jax.ShapeDtypeStruct((slabs, rows, 2 * SEGS * STEPS, SLAB), BF16),
        compiler_params=pltpu.CompilerParams(vmem_limit_bytes=8 * 2**20),
        cost_estimate=COST,
    )(*operands)


def first_axis(ch):
    return 1 + ch % 2


def second_axis(ch):
    return 2 - ch % 2


def mix_kernel(flips, own, channels, blocks, shares, staged, has_total, last, me_ref, slot_ref, *refs):
    refs = list(refs)
    s_refs = [refs.pop(0) for _ in flips]
    hat_ref = refs.pop(0)
    total_ref = refs.pop(0) if has_total else None
    if last:
        back_ref, inv_ref = refs.pop(0), refs.pop(0)
        out_refs = [refs.pop(0) for _ in range(3 if staged else shares)]
        y_ref, left_re, left_im, time_ref = refs
    else:
        (out_ref,) = refs

    slabs = hat_ref.shape[1]
    steps = slabs * SLAB // LANES
    half = 2 * STEPS
    pairs = channels // 2
    sources = []
    for ref, some in zip(s_refs, flips):
        for k, flip in enumerate(some):
            for i in range(own):
                slot = lax.rem(slot_ref[(me_ref[1] ^ flip) * own + i], hat_ref.shape[0])
                sources.append((ref, k * own + i, slot))
    groups = -(-len(sources) // GROUP)
    size = -(-len(sources) // groups)

    def twice(rows):
        rows = rows.astype(F32)
        return jnp.concatenate([rows, rows], axis=0).astype(BF16)

    def products(slab, seg):
        re_in = slice(2 * seg * STEPS, (2 * seg + 1) * STEPS)
        im_in = slice((2 * seg + 1) * STEPS, (2 * seg + 2) * STEPS)
        re_rows = slice(2 * seg * half, (2 * seg + 1) * half)
        im_rows = slice((2 * seg + 1) * half, (2 * seg + 2) * half)
        spectra = [(twice(ref[slab, r, re_in]), twice(ref[slab, r, im_in])) for ref, r, _ in sources]
        for pair in range(pairs):
            base = pair * 2 * half
            re_sum = total_ref[slab, pair, re_rows] if has_total else None
            im_sum = total_ref[slab, pair, im_rows] if has_total else None
            for start in range(0, len(sources), size):
                re, im = None, None
                for (s_re, s_im), (_, _, slot) in list(zip(spectra, sources))[start : start + size]:
                    h_re = hat_ref[slot, slab, base : base + half]
                    h_im = hat_ref[slot, slab, base + half : base + 2 * half]
                    add_re = s_re * h_re - s_im * h_im
                    add_im = s_re * h_im + s_im * h_re
                    re = add_re if re is None else re + add_re
                    im = add_im if im is None else im + add_im
                re, im = re.astype(F32), im.astype(F32)
                re_sum = re if re_sum is None else re_sum + re
                im_sum = im if im_sum is None else im_sum + im
            if last:
                y_ref[slab, pair, re_rows] = re_sum.astype(BF16)
                y_ref[slab, pair, im_rows] = im_sum.astype(BF16)
            else:
                out_ref[slab, pair, re_rows] = re_sum
                out_ref[slab, pair, im_rows] = im_sum

    for step in range(steps):
        first = step * (LANES // SLAB)
        for i in range(LANES // SLAB):
            for seg in range(SEGS):
                products(first + i, seg)
        if not last:
            continue
        for pair in range(pairs):
            y = jnp.concatenate([y_ref[first + i, pair] for i in range(LANES // SLAB)], axis=-1)
            if step == 0:
                plain, packed, _ = lane_masks(0, LANES)
                mix = dot(back_ref[0], y * plain.astype(BF16)) + dot(back_ref[1], y * packed.astype(BF16))
            else:
                mix = dot(back_ref[0], y)
            mix = mix.astype(BF16)
            here = slice(step * LANES, (step + 1) * LANES)
            for c in range(2):
                rows_to = slice((2 * pair + c) * blocks, (2 * pair + c + 1) * blocks)
                left_re[rows_to, here] = mix[2 * c * blocks : (2 * c + 1) * blocks]
                left_im[rows_to, here] = mix[(2 * c + 1) * blocks : (2 * c + 2) * blocks]

    if last:
        each = blocks // shares
        for step in range(steps):
            here = slice(step * LANES, (step + 1) * LANES)
            part = dot(left_re[...], two_slabs(inv_ref, step, 0)) + dot(left_im[...], two_slabs(inv_ref, step, 1))
            for t in range(shares):
                for c in range(channels):
                    row = c * blocks + t * each
                    time_ref[t, c, :, here] = part[row : row + each]
        if staged:
            near, other = first_axis(me_ref[1]), second_axis(me_ref[1])
            out_refs[0][0] = time_ref[me_ref[0] ^ near].astype(BF16)
            out_refs[0][1] = time_ref[me_ref[0] ^ 3].astype(BF16)
            out_refs[1][...] = time_ref[me_ref[0] ^ other].astype(BF16)
            out_refs[2][...] = time_ref[me_ref[0]].astype(BF16)
        else:
            for d in range(shares):
                out_refs[d][...] = time_ref[me_ref[0] ^ d].astype(BF16)


def add_sources(s_list, flips, own, me, slots, hat, total, last, shares, staged, channels, parts):
    slabs = hat.shape[1]
    bins = slabs * SLAB
    frames = parts + SEGS * KEEP
    blocks = frames - parts
    wide = 2 * SEGS * STEPS
    _, inverse = block_tables(bins)
    _, _, back = step_tables(parts, frames, channels)
    vmem = pl.BlockSpec(memory_space=pltpu.VMEM)
    smem = pl.BlockSpec(memory_space=pltpu.SMEM)

    operands = [me, slots] + list(s_list) + [pltpu.with_memory_space_constraint(hat, pltpu.VMEM)]
    aliases = {}
    if total is not None:
        if not last:
            aliases = {len(operands): 0}
        operands.append(total)
    scratch = []
    if last:
        operands += [jnp.asarray(back), jnp.asarray(inverse)]
        each = blocks // shares
        share = (channels, each, bins)
        shapes = [(2, *share), share, share] if staged else [share] * shares
        out_shape = [jax.ShapeDtypeStruct(shape, BF16) for shape in shapes]
        scratch = [
            pltpu.VMEM((slabs, channels // 2, 2 * wide, SLAB), BF16),
            pltpu.VMEM((channels * blocks, bins), BF16),
            pltpu.VMEM((channels * blocks, bins), BF16),
            pltpu.VMEM((shares, channels, each, bins), F32),
        ]
    else:
        out_shape = jax.ShapeDtypeStruct((slabs, channels // 2, 2 * wide, SLAB), F32)
    body = functools.partial(
        mix_kernel, tuple(flips), own, channels, blocks, shares, staged, total is not None, last
    )
    return pl.pallas_call(
        body,
        in_specs=[smem, smem] + [vmem] * (len(operands) - 2),
        out_specs=[vmem] * len(out_shape) if last else vmem,
        out_shape=out_shape,
        scratch_shapes=scratch,
        input_output_aliases=aliases,
        compiler_params=pltpu.CompilerParams(vmem_limit_bytes=12 * 2**20),
        cost_estimate=COST,
    )(*operands)


def sum_kernel(chips, me_ref, own_ref, first_ref, second_ref, mate_ref, *refs):
    outs, sum_ref = refs[:-1], refs[-1]
    total = own_ref[...].astype(F32) + first_ref[0].astype(F32) + second_ref[...].astype(F32)
    sum_ref[...] = total

    def piece(d):
        return sum_ref[:, pl.ds(me_ref[0] ^ d, 1), :].reshape(outs[0].shape)

    mate_ref[...] = jnp.concatenate([piece(2 * d + 1) for d in range(chips)], axis=0).astype(BF16)
    for d in range(chips):
        outs[d][...] = piece(2 * d).astype(BF16)


def sum_groups(own, first, second, me, chips):
    channels, _, bins = own.shape
    vmem = pl.BlockSpec(memory_space=pltpu.VMEM)
    return pl.pallas_call(
        functools.partial(sum_kernel, chips),
        in_specs=[pl.BlockSpec(memory_space=pltpu.SMEM)] + [vmem] * 3,
        out_specs=[vmem] * (chips + 1),
        out_shape=[jax.ShapeDtypeStruct((chips * channels, bins), BF16)]
        + [jax.ShapeDtypeStruct((channels, bins), BF16)] * chips,
        scratch_shapes=[pltpu.VMEM(own.shape, F32)],
        compiler_params=pltpu.CompilerParams(vmem_limit_bytes=8 * 2**20),
    )(me[None], own, first, second)


def per_device(src_count, ch_count, dry_signal, room_spectra, render_slot, decoder):
    rows_total, parts, channels, _, block_len = room_spectra.shape
    own = dry_signal.shape[0]
    frames = dry_signal.shape[1] // block_len
    blocks = frames - parts
    src_me = lax.axis_index("src").astype(jnp.int32)
    ch_me = lax.axis_index("ch").astype(jnp.int32)

    staged = src_count == 4 and blocks == src_count * ch_count

    if own == 1:
        x_own = dry_signal.reshape(frames, block_len)
    else:
        x_own = dry_signal.reshape(own, frames, block_len).transpose(1, 0, 2)

    def swap(value, axis, count, flip):
        return lax.ppermute(value, axis, [(i, i ^ flip) for i in range(count)])

    chips = ch_count // 2
    first = chips // 2
    lanes = {d: swap(x_own, "ch", ch_count, 2 * d) for d in (first, *range(1, first))}
    me = jnp.stack([src_me, ch_me])
    hat = transform_responses(room_spectra, me)
    lanes[first], hat = lax.optimization_barrier((lanes[first], hat))
    lanes.update({first ^ d: swap(lanes[first], "ch", ch_count, 2 * d) for d in range(1, first)})
    rest = [d for d in range(1, chips) if d not in (1, first)]

    row = jnp.arange(ch_count * channels, dtype=jnp.int32)
    takes = ((row // channels) ^ ch_me) * channels + row % channels
    order = (takes[:, None] == row[None, :]).astype(BF16)
    own_order = dot(order, decoder).astype(BF16)

    def add(s_list, flips, total, last):
        return add_sources(
            s_list, flips, own, me, render_slot, hat, total, last, src_count, staged, channels, parts
        )

    def transform(x_list):
        mine = transform_signals(x_list, own, block_len, parts)
        return mine, swap(mine, "ch", ch_count, 1)

    near = [0, first, 1]
    near_mine, near_given = transform([x_own, lanes[first], lanes[1]])
    total = add([near_mine], [[2 * d for d in near]], None, False)
    *late, total = lax.optimization_barrier((*[lanes[d] for d in rest], total))
    far_mine, far_given = transform(late)
    flips = [[2 * d + 1 for d in near], [2 * d for d in rest]]
    total = add([near_given, far_mine], flips, total, False)
    total = add([far_given], [[2 * d + 1 for d in rest]], total, True)

    if staged:

        def along(value, axis_of):
            pairs = [
                (src * ch_count + ch, (src ^ axis_of(ch)) * ch_count + ch)
                for src in range(src_count)
                for ch in range(ch_count)
            ]
            return lax.ppermute(value, ("src", "ch"), pairs)

        goes_first, goes_second, stays = total
        came_first = along(goes_first, first_axis)
        goes_second = goes_second.astype(F32) + came_first[1].astype(F32)
        came_second = along(goes_second.astype(BF16), second_axis)
        to_mate, *pieces = sum_groups(stays, came_first, came_second, ch_me, chips)
        given = swap(to_mate, "ch", ch_count, 1)
        both = [
            jnp.concatenate([pieces[d], given[d * channels : (d + 1) * channels]], axis=0)
            for d in range(chips)
        ]
        both[1:] = [swap(both[d], "ch", ch_count, 2 * d) for d in range(1, chips)]
        gathered = jnp.concatenate(both, axis=0)
        matrix = own_order
    else:
        signal = total[0].astype(F32)
        for d in range(1, src_count):
            signal = signal + swap(total[d], "src", src_count, d).astype(F32)
        signal = signal.astype(BF16).reshape(channels, -1)
        gathered = lax.all_to_all(signal, "ch", split_axis=1, concat_axis=0, tiled=True)
        matrix = decoder
    decoded = lax.dot_general(
        gathered, matrix, (((0,), (0,)), ((), ())), preferred_element_type=F32
    )
    return decoded.astype(BF16)


def solution(mesh):
    body = functools.partial(per_device, mesh.shape["src"], mesh.shape["ch"])
    return jax.shard_map(
        body,
        mesh=mesh,
        in_specs=(P(("src", "ch"), None), P("src", None, "ch", None, None), P("src"), P()),
        out_specs=P(("src", "ch"), None),
        check_vma=False,
    )
```

```python
import functools
import math

import jax
import jax.numpy as jnp
import ml_dtypes
import numpy as np
from jax import lax
from jax.experimental import pallas as pl
from jax.experimental.pallas import tpu as pltpu
from jax.sharding import PartitionSpec as P

BF16 = jnp.bfloat16
F32 = jnp.float32
LANES = 256
SLAB = 128
GROUP = 4
COST = pl.CostEstimate(flops=2**20, bytes_accessed=2**16, transcendentals=0)
ROWS = 4
STEPS = 24
SEGS = 2
KEEP = 16


def bf16_table(values):
    return np.asarray(values, dtype=np.float32).astype(ml_dtypes.bfloat16)


@functools.lru_cache(maxsize=None)
def block_tables(block_len):
    size = 2 * block_len
    n = np.arange(block_len)[:, None]
    k = np.arange(block_len)[None, :]
    angle = ((n * k) % size) * (2.0 * math.pi / size)
    fwd_real = np.cos(angle)
    fwd_imag = np.where(k == 0, 1.0 - 2.0 * (n % 2), -np.sin(angle))
    kk = np.arange(block_len)[:, None]
    m = np.arange(block_len)[None, :] + block_len
    angle = ((kk * m) % size) * (2.0 * math.pi / size)
    weight = np.where(kk == 0, 1.0, 2.0)
    inv_real = weight * np.cos(angle) / size
    inv_imag = np.where(kk == 0, (1.0 - 2.0 * (m % 2)) / size, -2.0 * np.sin(angle) / size)
    def slabs(pair):
        return bf16_table(np.stack(pair).reshape(2, block_len, -1, SLAB).transpose(0, 2, 1, 3))

    return slabs([fwd_real, fwd_imag]), slabs([inv_real, inv_imag])


@functools.lru_cache(maxsize=None)
def step_tables(parts, frames, channels, own=1):
    half = STEPS // 2
    theta = 2.0 * math.pi * (np.arange(STEPS) + 0.5) / STEPS
    first = (np.arange(STEPS) < half).astype(np.float64)[:, None]

    def forward(steps):
        cos = np.cos(theta[:, None] * steps[None, :])
        sin = np.sin(theta[:, None] * steps[None, :])
        plain = np.block([[cos, sin], [-sin, cos]])
        packed = np.block([[cos * first, cos * (1 - first)], [-sin * first, -sin * (1 - first)]])
        return plain, packed

    spec = np.zeros((2, SEGS, 2, STEPS, 2, frames))
    used = parts - 1 + KEEP
    for kind, table in enumerate(forward(np.arange(used))):
        table = table.reshape(2, STEPS, 2, used)
        for seg in range(SEGS):
            spec[kind, seg, :, :, :, seg * KEEP : seg * KEEP + used] = table
    spec = spec.reshape(2, 1, SEGS * 2 * STEPS, 2 * frames, 1) * np.eye(own)[None, :, None, None, :]
    spec = spec.reshape(2, own * SEGS * 2 * STEPS, 2 * frames * own)

    resp = np.zeros((channels // 2, 2, 2, STEPS, 2, parts, channels, 2))
    for kind, table in enumerate(forward(np.arange(parts))):
        table = table.reshape(2, STEPS, 2, parts).transpose(0, 1, 3, 2)
        for c in range(channels):
            resp[c // 2, :, c % 2, :, kind, :, c] = table
    resp = resp.reshape(channels * 2 * STEPS, 2 * parts * channels * 2)

    back = np.zeros((2, 2, 2, SEGS, KEEP, SEGS, 2, 2, STEPS))
    steps = np.arange(KEEP) + parts - 1
    cos = np.cos(theta[None, :] * steps[:, None]) / STEPS
    sin = np.sin(theta[None, :] * steps[:, None]) / STEPS
    firsts = first[:, 0][None, :]
    for seg in range(SEGS):
        for c in range(2):
            back[0, c, 0, seg, :, seg, 0, c] = cos
            back[0, c, 0, seg, :, seg, 1, c] = -sin
            back[0, c, 1, seg, :, seg, 0, c] = sin
            back[0, c, 1, seg, :, seg, 1, c] = cos
            back[1, c, 0, seg, :, seg, 0, c] = 2 * cos * firsts
            back[1, c, 0, seg, :, seg, 1, c] = -2 * sin * firsts
            back[1, c, 1, seg, :, seg, 0, c] = 2 * cos * (1 - firsts)
            back[1, c, 1, seg, :, seg, 1, c] = -2 * sin * (1 - firsts)
    back = back.reshape(2, 4 * SEGS * KEEP, 4 * SEGS * STEPS)
    return bf16_table(spec), bf16_table(resp), bf16_table(back)


def dot(left, right):
    return jnp.dot(left, right, preferred_element_type=F32)


def lane_masks(start, width):
    lane = lax.broadcasted_iota(jnp.int32, (1, width), 1) + start
    packed = (lane == 0).astype(F32)
    sign = (1 - 2 * (lane % 2)).astype(F32)
    return 1.0 - packed, packed, sign


def two_slabs(ref, step, *index):
    first = step * (LANES // SLAB)
    return jnp.concatenate([ref[(*index, first + i)] for i in range(LANES // SLAB)], axis=-1)


def response_kernel(rows, bins, me_ref, room_hbm, table_hbm, hat_ref, room_ref, table_ref, sems):
    depth = room_ref.shape[1] * room_ref.shape[2] * 2
    flat = room_ref.reshape(rows, depth, bins)
    plain, packed, _ = lane_masks(0, LANES)
    plain, packed = plain.astype(BF16), packed.astype(BF16)

    def copy(r):
        return pltpu.make_async_copy(room_hbm.at[r], room_ref.at[r], sems.at[r])

    table_copy = pltpu.make_async_copy(table_hbm, table_ref, sems.at[rows])
    table_copy.start()
    for r in range(rows):
        copy(r).start()
    table_copy.wait()

    def some(outer, carry):
        for inner in range(ROWS):
            copy(outer * ROWS + inner).wait()
        for inner in range(ROWS):
            r = outer * ROWS + inner
            for step in range(bins // LANES):
                h = flat[r, :, step * LANES : (step + 1) * LANES]
                if step == 0:
                    h = jnp.concatenate([h * plain, h * packed], axis=0)
                    hat = dot(table_ref[...], h)
                else:
                    hat = dot(table_ref[:, :depth], h)
                hat = hat.astype(BF16)
                for i in range(LANES // SLAB):
                    hat_ref[r, step * (LANES // SLAB) + i] = hat[:, i * SLAB : (i + 1) * SLAB]
        return carry

    lax.fori_loop(0, rows // ROWS, some, 0)


def transform_responses(room, me):
    rows, parts, channels, _, bins = room.shape
    slabs = bins // SLAB
    _, resp, _ = step_tables(parts, parts + SEGS * KEEP, channels)
    hbm = pl.BlockSpec(memory_space=pltpu.HBM)
    return pl.pallas_call(
        functools.partial(response_kernel, rows, bins),
        in_specs=[pl.BlockSpec(memory_space=pltpu.SMEM), hbm, hbm],
        out_specs=pl.BlockSpec(memory_space=pltpu.VMEM),
        out_shape=pltpu.VMEM((rows, slabs, channels * 2 * STEPS, SLAB), BF16),
        scratch_shapes=[
            pltpu.VMEM(room.shape, BF16),
            pltpu.VMEM(resp.shape, BF16),
            pltpu.SemaphoreType.DMA((rows + 1,)),
        ],
        compiler_params=pltpu.CompilerParams(vmem_limit_bytes=8 * 2**20),
        cost_estimate=COST,
    )(
        me,
        pltpu.with_memory_space_constraint(room, pltpu.HBM),
        pltpu.with_memory_space_constraint(jnp.asarray(resp), pltpu.HBM),
    )


def spectra_kernel(pieces, rows, *refs):
    x_refs, (table_ref, spec_ref, out_ref) = refs[:pieces], refs[pieces:]
    slabs = table_ref.shape[1]
    wide = 2 * SEGS * STEPS
    own = rows // pieces
    span = x_refs[0].shape[0] * own
    flat = x_refs if own == 1 else [ref.reshape(span, slabs * SLAB) for ref in x_refs]
    x = jnp.concatenate([ref[...] for ref in flat], axis=0)
    for step in range(slabs * SLAB // LANES):
        plain, packed, sign = lane_masks(step * LANES, LANES)
        spectra = []
        for j in range(2):
            one = dot(x, two_slabs(table_ref, step, j))
            spectra.append(one + sign * pltpu.roll(one, one.shape[0] - own, axis=0))
        for piece in range(pieces):
            both = [s[piece * span : (piece + 1) * span] for s in spectra]
            both = jnp.concatenate(both, axis=0)
            if step == 0:
                hat = dot(spec_ref[0], (both * plain).astype(BF16)) + dot(spec_ref[1], (both * packed).astype(BF16))
            else:
                hat = dot(spec_ref[0], both.astype(BF16))
            hat = hat.astype(BF16)
            for k in range(own):
                for i in range(LANES // SLAB):
                    at = slice(i * SLAB, (i + 1) * SLAB)
                    out_ref[step * (LANES // SLAB) + i, piece * own + k] = hat[k * wide : (k + 1) * wide, at]


def transform_signals(x_list, own, bins, parts):
    frames = parts + SEGS * KEEP
    rows = own * len(x_list)
    slabs = bins // SLAB
    table, _ = block_tables(bins)
    spec, _, _ = step_tables(parts, frames, 2, own)
    vmem = pl.BlockSpec(memory_space=pltpu.VMEM)
    operands = [*x_list, jnp.asarray(table), jnp.asarray(spec)]
    return pl.pallas_call(
        functools.partial(spectra_kernel, len(x_list), rows),
        in_specs=[vmem] * len(operands),
        out_specs=vmem,
        out_shape=jax.ShapeDtypeStruct((slabs, rows, 2 * SEGS * STEPS, SLAB), BF16),
        compiler_params=pltpu.CompilerParams(vmem_limit_bytes=8 * 2**20),
        cost_estimate=COST,
    )(*operands)


def mix_kernel(flips, own, channels, blocks, shares, has_total, last, me_ref, slot_ref, *refs):
    refs = list(refs)
    s_refs = [refs.pop(0) for _ in flips]
    hat_ref = refs.pop(0)
    total_ref = refs.pop(0) if has_total else None
    if last:
        back_ref, inv_ref = refs.pop(0), refs.pop(0)
        out_refs = [refs.pop(0) for _ in range(shares)]
        y_ref, left_re, left_im, time_ref = refs
    else:
        (out_ref,) = refs

    slabs = hat_ref.shape[1]
    steps = slabs * SLAB // LANES
    half = 2 * STEPS
    pairs = channels // 2
    sources = []
    for ref, some in zip(s_refs, flips):
        for k, flip in enumerate(some):
            for i in range(own):
                slot = lax.rem(slot_ref[(me_ref[1] ^ flip) * own + i], hat_ref.shape[0])
                sources.append((ref, k * own + i, slot))
    groups = -(-len(sources) // GROUP)
    size = -(-len(sources) // groups)

    def twice(rows):
        rows = rows.astype(F32)
        return jnp.concatenate([rows, rows], axis=0).astype(BF16)

    def products(slab, seg):
        re_in = slice(2 * seg * STEPS, (2 * seg + 1) * STEPS)
        im_in = slice((2 * seg + 1) * STEPS, (2 * seg + 2) * STEPS)
        re_rows = slice(2 * seg * half, (2 * seg + 1) * half)
        im_rows = slice((2 * seg + 1) * half, (2 * seg + 2) * half)
        spectra = [(twice(ref[slab, r, re_in]), twice(ref[slab, r, im_in])) for ref, r, _ in sources]
        for pair in range(pairs):
            base = pair * 2 * half
            re_sum = total_ref[slab, pair, re_rows] if has_total else None
            im_sum = total_ref[slab, pair, im_rows] if has_total else None
            for start in range(0, len(sources), size):
                re, im = None, None
                for (s_re, s_im), (_, _, slot) in list(zip(spectra, sources))[start : start + size]:
                    h_re = hat_ref[slot, slab, base : base + half]
                    h_im = hat_ref[slot, slab, base + half : base + 2 * half]
                    add_re = s_re * h_re - s_im * h_im
                    add_im = s_re * h_im + s_im * h_re
                    re = add_re if re is None else re + add_re
                    im = add_im if im is None else im + add_im
                re, im = re.astype(F32), im.astype(F32)
                re_sum = re if re_sum is None else re_sum + re
                im_sum = im if im_sum is None else im_sum + im
            if last:
                y_ref[slab, pair, re_rows] = re_sum.astype(BF16)
                y_ref[slab, pair, im_rows] = im_sum.astype(BF16)
            else:
                out_ref[slab, pair, re_rows] = re_sum
                out_ref[slab, pair, im_rows] = im_sum

    for step in range(steps):
        first = step * (LANES // SLAB)
        for i in range(LANES // SLAB):
            for seg in range(SEGS):
                products(first + i, seg)
        if not last:
            continue
        for pair in range(pairs):
            y = jnp.concatenate([y_ref[first + i, pair] for i in range(LANES // SLAB)], axis=-1)
            if step == 0:
                plain, packed, _ = lane_masks(0, LANES)
                mix = dot(back_ref[0], y * plain.astype(BF16)) + dot(back_ref[1], y * packed.astype(BF16))
            else:
                mix = dot(back_ref[0], y)
            mix = mix.astype(BF16)
            here = slice(step * LANES, (step + 1) * LANES)
            for c in range(2):
                rows_to = slice((2 * pair + c) * blocks, (2 * pair + c + 1) * blocks)
                left_re[rows_to, here] = mix[2 * c * blocks : (2 * c + 1) * blocks]
                left_im[rows_to, here] = mix[(2 * c + 1) * blocks : (2 * c + 2) * blocks]

    if last:
        each = blocks // shares
        for step in range(steps):
            here = slice(step * LANES, (step + 1) * LANES)
            part = dot(left_re[...], two_slabs(inv_ref, step, 0)) + dot(left_im[...], two_slabs(inv_ref, step, 1))
            for t in range(shares):
                for c in range(channels):
                    row = c * blocks + t * each
                    time_ref[t, c, :, here] = part[row : row + each]
        for d in range(shares):
            out_refs[d][...] = time_ref[me_ref[0] ^ d].astype(BF16)


def add_sources(s_list, flips, own, me, slots, hat, total, last, shares, channels, parts):
    slabs = hat.shape[1]
    bins = slabs * SLAB
    frames = parts + SEGS * KEEP
    blocks = frames - parts
    wide = 2 * SEGS * STEPS
    _, inverse = block_tables(bins)
    _, _, back = step_tables(parts, frames, channels)
    vmem = pl.BlockSpec(memory_space=pltpu.VMEM)
    smem = pl.BlockSpec(memory_space=pltpu.SMEM)

    operands = [me, slots] + list(s_list) + [pltpu.with_memory_space_constraint(hat, pltpu.VMEM)]
    aliases = {}
    if total is not None:
        if not last:
            aliases = {len(operands): 0}
        operands.append(total)
    scratch = []
    if last:
        operands += [jnp.asarray(back), jnp.asarray(inverse)]
        each = blocks // shares
        out_shape = [jax.ShapeDtypeStruct((channels, each, bins), BF16)] * shares
        scratch = [
            pltpu.VMEM((slabs, channels // 2, 2 * wide, SLAB), BF16),
            pltpu.VMEM((channels * blocks, bins), BF16),
            pltpu.VMEM((channels * blocks, bins), BF16),
            pltpu.VMEM((shares, channels, each, bins), F32),
        ]
    else:
        out_shape = jax.ShapeDtypeStruct((slabs, channels // 2, 2 * wide, SLAB), F32)
    body = functools.partial(
        mix_kernel, tuple(flips), own, channels, blocks, shares, total is not None, last
    )
    return pl.pallas_call(
        body,
        in_specs=[smem, smem] + [vmem] * (len(operands) - 2),
        out_specs=[vmem] * len(out_shape) if last else vmem,
        out_shape=out_shape,
        scratch_shapes=scratch,
        input_output_aliases=aliases,
        compiler_params=pltpu.CompilerParams(vmem_limit_bytes=12 * 2**20),
        cost_estimate=COST,
    )(*operands)


def sum_kernel(count, chips, me_ref, *refs):
    parts, mate_ref, outs, sum_ref = refs[:count], refs[count], refs[count + 1 : -1], refs[-1]
    total = parts[0][...].astype(F32)
    for part in parts[1:]:
        total = total + part[...].astype(F32)
    sum_ref[...] = total

    def piece(d):
        return sum_ref[:, pl.ds(me_ref[1] ^ d, 1), :].reshape(outs[0].shape)

    mate_ref[...] = jnp.concatenate([piece(2 * d + 1) for d in range(chips)], axis=0).astype(BF16)
    for d in range(chips):
        outs[d][...] = piece(2 * d).astype(BF16)


def sum_groups(parts, me, chips):
    channels, _, bins = parts[0].shape
    vmem = pl.BlockSpec(memory_space=pltpu.VMEM)
    return pl.pallas_call(
        functools.partial(sum_kernel, len(parts), chips),
        in_specs=[pl.BlockSpec(memory_space=pltpu.SMEM)] + [vmem] * len(parts),
        out_specs=[vmem] * (chips + 1),
        out_shape=[jax.ShapeDtypeStruct((chips * channels, bins), BF16)]
        + [jax.ShapeDtypeStruct((channels, bins), BF16)] * chips,
        scratch_shapes=[pltpu.VMEM(parts[0].shape, F32)],
        compiler_params=pltpu.CompilerParams(vmem_limit_bytes=8 * 2**20),
    )(me, *parts)


def decode_kernel(count, *refs):
    signal_refs, matrix_ref, out_ref = refs[:count], refs[count], refs[-1]
    rows = out_ref.shape[0]
    here = pl.ds(pl.multiple_of(pl.program_id(0) * rows, rows), rows)
    signal = jnp.concatenate([ref[:, here] for ref in signal_refs], axis=0)
    out_ref[...] = lax.dot_general(
        signal, matrix_ref[...], (((0,), (0,)), ((), ())), preferred_element_type=F32
    ).astype(BF16)


def decode(signals, matrix):
    samples, speakers = signals[0].shape[1], matrix.shape[1]
    rows = min(256, samples)
    vmem = pl.BlockSpec(memory_space=pltpu.VMEM)
    return pl.pallas_call(
        functools.partial(decode_kernel, len(signals)),
        grid=(samples // rows,),
        in_specs=[vmem] * (len(signals) + 1),
        out_specs=pl.BlockSpec((rows, speakers), lambda i: (i, 0)),
        out_shape=jax.ShapeDtypeStruct((samples, speakers), BF16),
        compiler_params=pltpu.CompilerParams(vmem_limit_bytes=8 * 2**20),
    )(*signals, matrix)


def per_device(src_count, ch_count, dry_signal, room_spectra, render_slot, decoder):
    rows_total, parts, channels, _, block_len = room_spectra.shape
    own = dry_signal.shape[0]
    frames = dry_signal.shape[1] // block_len
    blocks = frames - parts
    src_me = lax.axis_index("src").astype(jnp.int32)
    ch_me = lax.axis_index("ch").astype(jnp.int32)

    if own == 1:
        x_own = dry_signal.reshape(frames, block_len)
    else:
        x_own = dry_signal.reshape(own, frames, block_len).transpose(1, 0, 2)

    def swap(value, axis, count, flip):
        return lax.ppermute(value, axis, [(i, i ^ flip) for i in range(count)])

    chips = ch_count // 2
    lanes = [x_own] + [swap(x_own, "ch", ch_count, 2 * d) for d in range(1, chips)]
    me = jnp.stack([src_me, ch_me])
    hat = transform_responses(room_spectra, me)

    row = jnp.arange(ch_count * channels, dtype=jnp.int32)
    takes = ((row // channels) ^ ch_me) * channels + row % channels
    order = (takes[:, None] == row[None, :]).astype(BF16)
    own_order = dot(order, decoder).astype(BF16)

    def add(s_list, flips, total, last):
        return add_sources(
            s_list, flips, own, me, render_slot, hat, total, last, src_count, channels, parts
        )

    def transform(x_list):
        mine = transform_signals(x_list, own, block_len, parts)
        return mine, swap(mine, "ch", ch_count, 1)

    near, far = range(0, 2), range(2, chips)
    x_near, hat = lax.optimization_barrier((x_own, hat))
    near_mine, near_given = transform([x_near, lanes[1]])
    total = add([near_mine], [[2 * d for d in near]], None, False)
    *late, total = lax.optimization_barrier((*lanes[2:], total))
    far_mine, far_given = transform(late)
    flips = [[2 * d + 1 for d in near], [2 * d for d in far]]
    total = add([near_given, far_mine], flips, total, False)
    total = add([far_given], [[2 * d + 1 for d in far]], total, True)

    sums = [total[0]] + [swap(total[d], "src", src_count, d) for d in range(1, src_count)]
    if blocks == src_count * ch_count:
        to_mate, *pieces = sum_groups(sums, me, chips)
        given = swap(to_mate, "ch", ch_count, 1)
        both = [
            jnp.concatenate([pieces[d], given[d * channels : (d + 1) * channels]], axis=0)
            for d in range(chips)
        ]
        both[1:] = [swap(both[d], "ch", ch_count, 2 * d) for d in range(1, chips)]
        return decode(both, own_order)
    signal = sums[0].astype(F32)
    for part in sums[1:]:
        signal = signal + part.astype(F32)
    signal = signal.astype(BF16).reshape(channels, -1)
    return decode([lax.all_to_all(signal, "ch", split_axis=1, concat_axis=0, tiled=True)], decoder)


def solution(mesh):
    body = functools.partial(per_device, mesh.shape["src"], mesh.shape["ch"])
    return jax.shard_map(
        body,
        mesh=mesh,
        in_specs=(P(("src", "ch"), None), P("src", None, "ch", None, None), P("src"), P()),
        out_specs=P(("src", "ch"), None),
        check_vma=False,
    )
```

```python
import functools
import math

import jax
import jax.numpy as jnp
import ml_dtypes
import numpy as np
from jax import lax
from jax.experimental import pallas as pl
from jax.experimental.pallas import tpu as pltpu
from jax.sharding import PartitionSpec as P

BF16 = jnp.bfloat16
F32 = jnp.float32
LANES = 256
SLAB = 128
GROUP = 4
COST = pl.CostEstimate(flops=2**20, bytes_accessed=2**16, transcendentals=0)
ROWS = 4
STEPS = 24
SEGS = 2
KEEP = 16


def bf16_table(values):
    return np.asarray(values, dtype=np.float32).astype(ml_dtypes.bfloat16)


@functools.lru_cache(maxsize=None)
def block_tables(block_len):
    size = 2 * block_len
    n = np.arange(block_len)[:, None]
    k = np.arange(block_len)[None, :]
    angle = ((n * k) % size) * (2.0 * math.pi / size)
    fwd_real = np.cos(angle)
    fwd_imag = np.where(k == 0, 1.0 - 2.0 * (n % 2), -np.sin(angle))
    kk = np.arange(block_len)[:, None]
    m = np.arange(block_len)[None, :] + block_len
    angle = ((kk * m) % size) * (2.0 * math.pi / size)
    weight = np.where(kk == 0, 1.0, 2.0)
    inv_real = weight * np.cos(angle) / size
    inv_imag = np.where(kk == 0, (1.0 - 2.0 * (m % 2)) / size, -2.0 * np.sin(angle) / size)
    def slabs(pair):
        return bf16_table(np.stack(pair).reshape(2, block_len, -1, SLAB).transpose(0, 2, 1, 3))

    return slabs([fwd_real, fwd_imag]), slabs([inv_real, inv_imag])


@functools.lru_cache(maxsize=None)
def step_tables(parts, frames, channels, own=1):
    half = STEPS // 2
    theta = 2.0 * math.pi * (np.arange(STEPS) + 0.5) / STEPS
    first = (np.arange(STEPS) < half).astype(np.float64)[:, None]

    def forward(steps):
        cos = np.cos(theta[:, None] * steps[None, :])
        sin = np.sin(theta[:, None] * steps[None, :])
        plain = np.block([[cos, sin], [-sin, cos]])
        packed = np.block([[cos * first, cos * (1 - first)], [-sin * first, -sin * (1 - first)]])
        return plain, packed

    spec = np.zeros((2, SEGS, 2, STEPS, 2, frames))
    used = parts - 1 + KEEP
    for kind, table in enumerate(forward(np.arange(used))):
        table = table.reshape(2, STEPS, 2, used)
        for seg in range(SEGS):
            spec[kind, seg, :, :, :, seg * KEEP : seg * KEEP + used] = table
    spec = spec.reshape(2, 1, SEGS * 2 * STEPS, 2 * frames, 1) * np.eye(own)[None, :, None, None, :]
    spec = spec.reshape(2, own * SEGS * 2 * STEPS, 2 * frames * own)

    resp = np.zeros((channels // 2, 2, 2, STEPS, 2, parts, channels, 2))
    for kind, table in enumerate(forward(np.arange(parts))):
        table = table.reshape(2, STEPS, 2, parts).transpose(0, 1, 3, 2)
        for c in range(channels):
            resp[c // 2, :, c % 2, :, kind, :, c] = table
    resp = resp.reshape(channels * 2 * STEPS, 2 * parts * channels * 2)

    back = np.zeros((2, 2, 2, SEGS, KEEP, SEGS, 2, 2, STEPS))
    steps = np.arange(KEEP) + parts - 1
    cos = np.cos(theta[None, :] * steps[:, None]) / STEPS
    sin = np.sin(theta[None, :] * steps[:, None]) / STEPS
    firsts = first[:, 0][None, :]
    for seg in range(SEGS):
        for c in range(2):
            back[0, c, 0, seg, :, seg, 0, c] = cos
            back[0, c, 0, seg, :, seg, 1, c] = -sin
            back[0, c, 1, seg, :, seg, 0, c] = sin
            back[0, c, 1, seg, :, seg, 1, c] = cos
            back[1, c, 0, seg, :, seg, 0, c] = 2 * cos * firsts
            back[1, c, 0, seg, :, seg, 1, c] = -2 * sin * firsts
            back[1, c, 1, seg, :, seg, 0, c] = 2 * cos * (1 - firsts)
            back[1, c, 1, seg, :, seg, 1, c] = -2 * sin * (1 - firsts)
    back = back.reshape(2, 4 * SEGS * KEEP, 4 * SEGS * STEPS)
    return bf16_table(spec), bf16_table(resp), bf16_table(back)


def dot(left, right):
    return jnp.dot(left, right, preferred_element_type=F32)


def lane_masks(start, width):
    lane = lax.broadcasted_iota(jnp.int32, (1, width), 1) + start
    packed = (lane == 0).astype(F32)
    sign = (1 - 2 * (lane % 2)).astype(F32)
    return 1.0 - packed, packed, sign


def two_slabs(ref, step, *index):
    first = step * (LANES // SLAB)
    return jnp.concatenate([ref[(*index, first + i)] for i in range(LANES // SLAB)], axis=-1)


def response_kernel(rows, bins, me_ref, room_hbm, table_hbm, hat_ref, room_ref, table_ref, sems):
    depth = room_ref.shape[1] * room_ref.shape[2] * 2
    flat = room_ref.reshape(rows, depth, bins)
    plain, packed, _ = lane_masks(0, LANES)
    plain, packed = plain.astype(BF16), packed.astype(BF16)

    def copy(r):
        return pltpu.make_async_copy(room_hbm.at[r], room_ref.at[r], sems.at[r])

    table_copy = pltpu.make_async_copy(table_hbm, table_ref, sems.at[rows])
    table_copy.start()
    for r in range(rows):
        copy(r).start()
    table_copy.wait()

    def some(outer, carry):
        for inner in range(ROWS):
            copy(outer * ROWS + inner).wait()
        for inner in range(ROWS):
            r = outer * ROWS + inner
            for step in range(bins // LANES):
                h = flat[r, :, step * LANES : (step + 1) * LANES]
                if step == 0:
                    h = jnp.concatenate([h * plain, h * packed], axis=0)
                    hat = dot(table_ref[...], h)
                else:
                    hat = dot(table_ref[:, :depth], h)
                hat = hat.astype(BF16)
                for i in range(LANES // SLAB):
                    hat_ref[r, step * (LANES // SLAB) + i] = hat[:, i * SLAB : (i + 1) * SLAB]
        return carry

    lax.fori_loop(0, rows // ROWS, some, 0)


def transform_responses(room, me):
    rows, parts, channels, _, bins = room.shape
    slabs = bins // SLAB
    _, resp, _ = step_tables(parts, parts + SEGS * KEEP, channels)
    hbm = pl.BlockSpec(memory_space=pltpu.HBM)
    return pl.pallas_call(
        functools.partial(response_kernel, rows, bins),
        in_specs=[pl.BlockSpec(memory_space=pltpu.SMEM), hbm, hbm],
        out_specs=pl.BlockSpec(memory_space=pltpu.VMEM),
        out_shape=pltpu.VMEM((rows, slabs, channels * 2 * STEPS, SLAB), BF16),
        scratch_shapes=[
            pltpu.VMEM(room.shape, BF16),
            pltpu.VMEM(resp.shape, BF16),
            pltpu.SemaphoreType.DMA((rows + 1,)),
        ],
        compiler_params=pltpu.CompilerParams(vmem_limit_bytes=8 * 2**20),
        cost_estimate=COST,
    )(
        me,
        pltpu.with_memory_space_constraint(room, pltpu.HBM),
        pltpu.with_memory_space_constraint(jnp.asarray(resp), pltpu.HBM),
    )


def spectra_kernel(pieces, rows, *refs):
    x_refs, (table_ref, spec_ref, out_ref) = refs[:pieces], refs[pieces:]
    slabs = table_ref.shape[1]
    wide = 2 * SEGS * STEPS
    own = rows // pieces
    span = x_refs[0].shape[0] * own
    flat = x_refs if own == 1 else [ref.reshape(span, slabs * SLAB) for ref in x_refs]
    x = jnp.concatenate([ref[...] for ref in flat], axis=0)
    for step in range(slabs * SLAB // LANES):
        plain, packed, sign = lane_masks(step * LANES, LANES)
        spectra = []
        for j in range(2):
            one = dot(x, two_slabs(table_ref, step, j))
            spectra.append(one + sign * pltpu.roll(one, one.shape[0] - own, axis=0))
        for piece in range(pieces):
            both = [s[piece * span : (piece + 1) * span] for s in spectra]
            both = jnp.concatenate(both, axis=0)
            if step == 0:
                hat = dot(spec_ref[0], (both * plain).astype(BF16)) + dot(spec_ref[1], (both * packed).astype(BF16))
            else:
                hat = dot(spec_ref[0], both.astype(BF16))
            hat = hat.astype(BF16)
            for k in range(own):
                for i in range(LANES // SLAB):
                    at = slice(i * SLAB, (i + 1) * SLAB)
                    out_ref[step * (LANES // SLAB) + i, piece * own + k] = hat[k * wide : (k + 1) * wide, at]


def transform_signals(x_list, own, bins, parts):
    frames = parts + SEGS * KEEP
    rows = own * len(x_list)
    slabs = bins // SLAB
    table, _ = block_tables(bins)
    spec, _, _ = step_tables(parts, frames, 2, own)
    vmem = pl.BlockSpec(memory_space=pltpu.VMEM)
    operands = [*x_list, jnp.asarray(table), jnp.asarray(spec)]
    return pl.pallas_call(
        functools.partial(spectra_kernel, len(x_list), rows),
        in_specs=[vmem] * len(operands),
        out_specs=vmem,
        out_shape=jax.ShapeDtypeStruct((slabs, rows, 2 * SEGS * STEPS, SLAB), BF16),
        compiler_params=pltpu.CompilerParams(vmem_limit_bytes=8 * 2**20),
        cost_estimate=COST,
    )(*operands)


def mix_kernel(flips, own, channels, blocks, shares, has_total, last, me_ref, slot_ref, *refs):
    refs = list(refs)
    s_refs = [refs.pop(0) for _ in flips]
    hat_ref = refs.pop(0)
    total_ref = refs.pop(0) if has_total else None
    if last:
        back_ref, inv_ref = refs.pop(0), refs.pop(0)
        out_refs = [refs.pop(0) for _ in range(shares)]
        y_ref, left_re, left_im, time_ref = refs
    else:
        (out_ref,) = refs

    slabs = hat_ref.shape[1]
    steps = slabs * SLAB // LANES
    half = 2 * STEPS
    pairs = channels // 2
    sources = []
    for ref, some in zip(s_refs, flips):
        for k, flip in enumerate(some):
            for i in range(own):
                slot = lax.rem(slot_ref[(me_ref[1] ^ flip) * own + i], hat_ref.shape[0])
                sources.append((ref, k * own + i, slot))
    groups = -(-len(sources) // GROUP)
    size = -(-len(sources) // groups)

    def twice(rows):
        rows = rows.astype(F32)
        return jnp.concatenate([rows, rows], axis=0).astype(BF16)

    def products(slab, seg):
        re_in = slice(2 * seg * STEPS, (2 * seg + 1) * STEPS)
        im_in = slice((2 * seg + 1) * STEPS, (2 * seg + 2) * STEPS)
        re_rows = slice(2 * seg * half, (2 * seg + 1) * half)
        im_rows = slice((2 * seg + 1) * half, (2 * seg + 2) * half)
        spectra = [(twice(ref[slab, r, re_in]), twice(ref[slab, r, im_in])) for ref, r, _ in sources]
        for pair in range(pairs):
            base = pair * 2 * half
            re_sum = total_ref[slab, pair, re_rows] if has_total else None
            im_sum = total_ref[slab, pair, im_rows] if has_total else None
            for start in range(0, len(sources), size):
                re, im = None, None
                for (s_re, s_im), (_, _, slot) in list(zip(spectra, sources))[start : start + size]:
                    h_re = hat_ref[slot, slab, base : base + half]
                    h_im = hat_ref[slot, slab, base + half : base + 2 * half]
                    add_re = s_re * h_re - s_im * h_im
                    add_im = s_re * h_im + s_im * h_re
                    re = add_re if re is None else re + add_re
                    im = add_im if im is None else im + add_im
                re, im = re.astype(F32), im.astype(F32)
                re_sum = re if re_sum is None else re_sum + re
                im_sum = im if im_sum is None else im_sum + im
            if last:
                y_ref[slab, pair, re_rows] = re_sum.astype(BF16)
                y_ref[slab, pair, im_rows] = im_sum.astype(BF16)
            else:
                out_ref[slab, pair, re_rows] = re_sum
                out_ref[slab, pair, im_rows] = im_sum

    for step in range(steps):
        first = step * (LANES // SLAB)
        for i in range(LANES // SLAB):
            for seg in range(SEGS):
                products(first + i, seg)
        if not last:
            continue
        for pair in range(pairs):
            y = jnp.concatenate([y_ref[first + i, pair] for i in range(LANES // SLAB)], axis=-1)
            if step == 0:
                plain, packed, _ = lane_masks(0, LANES)
                mix = dot(back_ref[0], y * plain.astype(BF16)) + dot(back_ref[1], y * packed.astype(BF16))
            else:
                mix = dot(back_ref[0], y)
            mix = mix.astype(BF16)
            here = slice(step * LANES, (step + 1) * LANES)
            for c in range(2):
                rows_to = slice((2 * pair + c) * blocks, (2 * pair + c + 1) * blocks)
                left_re[rows_to, here] = mix[2 * c * blocks : (2 * c + 1) * blocks]
                left_im[rows_to, here] = mix[(2 * c + 1) * blocks : (2 * c + 2) * blocks]

    if last:
        each = blocks // shares
        for step in range(steps):
            here = slice(step * LANES, (step + 1) * LANES)
            part = dot(left_re[...], two_slabs(inv_ref, step, 0)) + dot(left_im[...], two_slabs(inv_ref, step, 1))
            for t in range(shares):
                for c in range(channels):
                    row = c * blocks + t * each
                    time_ref[t, c, :, here] = part[row : row + each]
        for d in range(shares):
            out_refs[d][...] = time_ref[me_ref[0] ^ d].astype(BF16)


def add_sources(s_list, flips, own, me, slots, hat, total, last, shares, channels, parts):
    slabs = hat.shape[1]
    bins = slabs * SLAB
    frames = parts + SEGS * KEEP
    blocks = frames - parts
    wide = 2 * SEGS * STEPS
    _, inverse = block_tables(bins)
    _, _, back = step_tables(parts, frames, channels)
    vmem = pl.BlockSpec(memory_space=pltpu.VMEM)
    smem = pl.BlockSpec(memory_space=pltpu.SMEM)

    operands = [me, slots] + list(s_list) + [pltpu.with_memory_space_constraint(hat, pltpu.VMEM)]
    aliases = {}
    if total is not None:
        if not last:
            aliases = {len(operands): 0}
        operands.append(total)
    scratch = []
    if last:
        operands += [jnp.asarray(back), jnp.asarray(inverse)]
        each = blocks // shares
        out_shape = [jax.ShapeDtypeStruct((channels, each, bins), BF16)] * shares
        scratch = [
            pltpu.VMEM((slabs, channels // 2, 2 * wide, SLAB), BF16),
            pltpu.VMEM((channels * blocks, bins), BF16),
            pltpu.VMEM((channels * blocks, bins), BF16),
            pltpu.VMEM((shares, channels, each, bins), F32),
        ]
    else:
        out_shape = jax.ShapeDtypeStruct((slabs, channels // 2, 2 * wide, SLAB), F32)
    body = functools.partial(
        mix_kernel, tuple(flips), own, channels, blocks, shares, total is not None, last
    )
    return pl.pallas_call(
        body,
        in_specs=[smem, smem] + [vmem] * (len(operands) - 2),
        out_specs=[vmem] * len(out_shape) if last else vmem,
        out_shape=out_shape,
        scratch_shapes=scratch,
        input_output_aliases=aliases,
        compiler_params=pltpu.CompilerParams(vmem_limit_bytes=12 * 2**20),
        cost_estimate=COST,
    )(*operands)


def sum_kernel(count, me_ref, *refs):
    parts, outs, sum_ref = refs[:count], refs[count:-1], refs[-1]
    total = parts[0][...].astype(F32)
    for part in parts[1:]:
        total = total + part[...].astype(F32)
    sum_ref[...] = total
    for d in range(len(outs)):
        outs[d][...] = sum_ref[:, pl.ds(me_ref[1] ^ d, 1), :].reshape(outs[d].shape).astype(BF16)


def sum_groups(parts, me):
    channels, each, bins = parts[0].shape
    vmem = pl.BlockSpec(memory_space=pltpu.VMEM)
    return pl.pallas_call(
        functools.partial(sum_kernel, len(parts)),
        in_specs=[pl.BlockSpec(memory_space=pltpu.SMEM)] + [vmem] * len(parts),
        out_specs=[vmem] * each,
        out_shape=[jax.ShapeDtypeStruct((channels, bins), BF16)] * each,
        scratch_shapes=[pltpu.VMEM(parts[0].shape, F32)],
        compiler_params=pltpu.CompilerParams(vmem_limit_bytes=8 * 2**20),
    )(me, *parts)


def decode(signal, matrix):
    decoded = lax.dot_general(
        signal, matrix, (((0,), (0,)), ((), ())), preferred_element_type=F32
    )
    return decoded.astype(BF16)


def per_device(src_count, ch_count, dry_signal, room_spectra, render_slot, decoder):
    rows_total, parts, channels, _, block_len = room_spectra.shape
    own = dry_signal.shape[0]
    frames = dry_signal.shape[1] // block_len
    blocks = frames - parts
    src_me = lax.axis_index("src").astype(jnp.int32)
    ch_me = lax.axis_index("ch").astype(jnp.int32)

    if own == 1:
        x_own = dry_signal.reshape(frames, block_len)
    else:
        x_own = dry_signal.reshape(own, frames, block_len).transpose(1, 0, 2)

    def swap(value, axis, count, flip):
        return lax.ppermute(value, axis, [(i, i ^ flip) for i in range(count)])

    chips = ch_count // 2
    first = chips // 2
    far = [d for d in range(chips - 1, 0, -1) if d != first]
    lanes = {d: swap(x_own, "ch", ch_count, 2 * d) for d in (first, *far)}
    me = jnp.stack([src_me, ch_me])
    hat = transform_responses(room_spectra, me)

    row = jnp.arange(ch_count * channels, dtype=jnp.int32)
    takes = ((row // channels) ^ ch_me) * channels + row % channels
    order = (takes[:, None] == row[None, :]).astype(BF16)
    own_order = lax.optimization_barrier(dot(order, decoder).astype(BF16))

    def add(s_list, flips, total, last):
        return add_sources(
            s_list, flips, own, me, render_slot, hat, total, last, src_count, channels, parts
        )

    def transform(x_list):
        mine = transform_signals(x_list, own, block_len, parts)
        return mine, swap(mine, "ch", ch_count, 1)

    near = [0, first]
    x_near, hat = lax.optimization_barrier((x_own, hat))
    near_mine, near_given = transform([x_near, lanes[first]])
    total = add([near_mine], [[2 * d for d in near]], None, False)
    *late, total = lax.optimization_barrier((*[lanes[d] for d in far], total))
    far_mine, far_given = transform(late)
    flips = [[2 * d + 1 for d in near], [2 * d for d in far]]
    total = add([near_given, far_mine], flips, total, False)
    total = add([far_given], [[2 * d + 1 for d in far]], total, True)

    sums = [total[0]] + [swap(total[d], "src", src_count, d) for d in range(1, src_count)]
    if blocks == src_count * ch_count:
        pieces = sum_groups(sums, me)
        given = swap(jnp.concatenate(pieces[1::2], axis=0), "ch", ch_count, 1)
        both = [
            jnp.concatenate([pieces[2 * d], given[d * channels : (d + 1) * channels]], axis=0)
            for d in range(chips)
        ]
        both[1:] = [swap(both[d], "ch", ch_count, 2 * d) for d in range(1, chips)]
        return decode(jnp.concatenate(both, axis=0), own_order)
    signal = sums[0].astype(F32)
    for part in sums[1:]:
        signal = signal + part.astype(F32)
    signal = signal.astype(BF16).reshape(channels, -1)
    return decode(lax.all_to_all(signal, "ch", split_axis=1, concat_axis=0, tiled=True), decoder)


def solution(mesh):
    body = functools.partial(per_device, mesh.shape["src"], mesh.shape["ch"])
    return jax.shard_map(
        body,
        mesh=mesh,
        in_specs=(P(("src", "ch"), None), P("src", None, "ch", None, None), P("src"), P()),
        out_specs=P(("src", "ch"), None),
        check_vma=False,
    )
```

```python
import functools
import math

import jax
import jax.numpy as jnp
import ml_dtypes
import numpy as np
from jax import lax
from jax.experimental import pallas as pl
from jax.experimental.pallas import tpu as pltpu
from jax.sharding import PartitionSpec as P

BF16 = jnp.bfloat16
F32 = jnp.float32
LANES = 256
SLAB = 128
GROUP = 4
COST = pl.CostEstimate(flops=2**20, bytes_accessed=2**16, transcendentals=0)
ROWS = 4
STEPS = 24
SEGS = 2
KEEP = 16


def bf16_table(values):
    return np.asarray(values, dtype=np.float32).astype(ml_dtypes.bfloat16)


@functools.lru_cache(maxsize=None)
def block_tables(block_len):
    size = 2 * block_len
    n = np.arange(block_len)[:, None]
    k = np.arange(block_len)[None, :]
    angle = ((n * k) % size) * (2.0 * math.pi / size)
    fwd_real = np.cos(angle)
    fwd_imag = np.where(k == 0, 1.0 - 2.0 * (n % 2), -np.sin(angle))
    kk = np.arange(block_len)[:, None]
    m = np.arange(block_len)[None, :] + block_len
    angle = ((kk * m) % size) * (2.0 * math.pi / size)
    weight = np.where(kk == 0, 1.0, 2.0)
    inv_real = weight * np.cos(angle) / size
    inv_imag = np.where(kk == 0, (1.0 - 2.0 * (m % 2)) / size, -2.0 * np.sin(angle) / size)
    def slabs(pair):
        return bf16_table(np.stack(pair).reshape(2, block_len, -1, SLAB).transpose(0, 2, 1, 3))

    return slabs([fwd_real, fwd_imag]), slabs([inv_real, inv_imag])


@functools.lru_cache(maxsize=None)
def step_tables(parts, frames, channels, own=1):
    half = STEPS // 2
    theta = 2.0 * math.pi * (np.arange(STEPS) + 0.5) / STEPS
    first = (np.arange(STEPS) < half).astype(np.float64)[:, None]

    def forward(steps):
        cos = np.cos(theta[:, None] * steps[None, :])
        sin = np.sin(theta[:, None] * steps[None, :])
        plain = np.block([[cos, sin], [-sin, cos]])
        packed = np.block([[cos * first, cos * (1 - first)], [-sin * first, -sin * (1 - first)]])
        return plain, packed

    spec = np.zeros((2, SEGS, 2, STEPS, 2, frames))
    used = parts - 1 + KEEP
    for kind, table in enumerate(forward(np.arange(used))):
        table = table.reshape(2, STEPS, 2, used)
        for seg in range(SEGS):
            spec[kind, seg, :, :, :, seg * KEEP : seg * KEEP + used] = table
    spec = spec.reshape(2, 1, SEGS * 2 * STEPS, 2 * frames, 1) * np.eye(own)[None, :, None, None, :]
    spec = spec.reshape(2, own * SEGS * 2 * STEPS, 2 * frames * own)

    resp = np.zeros((channels // 2, 2, 2, STEPS, 2, parts, channels, 2))
    for kind, table in enumerate(forward(np.arange(parts))):
        table = table.reshape(2, STEPS, 2, parts).transpose(0, 1, 3, 2)
        for c in range(channels):
            resp[c // 2, :, c % 2, :, kind, :, c] = table
    resp = resp.reshape(channels * 2 * STEPS, 2 * parts * channels * 2)

    back = np.zeros((2, 2, 2, SEGS, KEEP, SEGS, 2, 2, STEPS))
    steps = np.arange(KEEP) + parts - 1
    cos = np.cos(theta[None, :] * steps[:, None]) / STEPS
    sin = np.sin(theta[None, :] * steps[:, None]) / STEPS
    firsts = first[:, 0][None, :]
    for seg in range(SEGS):
        for c in range(2):
            back[0, c, 0, seg, :, seg, 0, c] = cos
            back[0, c, 0, seg, :, seg, 1, c] = -sin
            back[0, c, 1, seg, :, seg, 0, c] = sin
            back[0, c, 1, seg, :, seg, 1, c] = cos
            back[1, c, 0, seg, :, seg, 0, c] = 2 * cos * firsts
            back[1, c, 0, seg, :, seg, 1, c] = -2 * sin * firsts
            back[1, c, 1, seg, :, seg, 0, c] = 2 * cos * (1 - firsts)
            back[1, c, 1, seg, :, seg, 1, c] = -2 * sin * (1 - firsts)
    back = back.reshape(2, 4 * SEGS * KEEP, 4 * SEGS * STEPS)
    return bf16_table(spec), bf16_table(resp), bf16_table(back)


def dot(left, right):
    return jnp.dot(left, right, preferred_element_type=F32)


def lane_masks(start, width):
    lane = lax.broadcasted_iota(jnp.int32, (1, width), 1) + start
    packed = (lane == 0).astype(F32)
    sign = (1 - 2 * (lane % 2)).astype(F32)
    return 1.0 - packed, packed, sign


def two_slabs(ref, step, *index):
    first = step * (LANES // SLAB)
    return jnp.concatenate([ref[(*index, first + i)] for i in range(LANES // SLAB)], axis=-1)


def response_kernel(rows, bins, src_ref, ch_ref, slot_ref, room_hbm, table_hbm, hat_ref, room_ref, table_ref, sems):
    depth = room_ref.shape[1] * room_ref.shape[2] * 2
    flat = room_ref.reshape(rows, depth, bins)
    plain, packed, _ = lane_masks(0, LANES)
    plain, packed = plain.astype(BF16), packed.astype(BF16)

    def copy(r):
        row = lax.rem(slot_ref[r], rows)
        return pltpu.make_async_copy(room_hbm.at[row], room_ref.at[r], sems.at[r])

    table_copy = pltpu.make_async_copy(table_hbm, table_ref, sems.at[rows])
    table_copy.start()
    for r in range(rows):
        copy(r).start()
    table_copy.wait()

    def some(outer, carry):
        for inner in range(ROWS):
            copy(outer * ROWS + inner).wait()
        for inner in range(ROWS):
            r = outer * ROWS + inner
            for step in range(bins // LANES):
                h = flat[r, :, step * LANES : (step + 1) * LANES]
                if step == 0:
                    h = jnp.concatenate([h * plain, h * packed], axis=0)
                    hat = dot(table_ref[...], h)
                else:
                    hat = dot(table_ref[:, :depth], h)
                hat = hat.astype(BF16)
                for i in range(LANES // SLAB):
                    hat_ref[r, step * (LANES // SLAB) + i] = hat[:, i * SLAB : (i + 1) * SLAB]
        return carry

    lax.fori_loop(0, rows // ROWS, some, 0)


def transform_responses(room, me, slots):
    rows, parts, channels, _, bins = room.shape
    slabs = bins // SLAB
    _, resp, _ = step_tables(parts, parts + SEGS * KEEP, channels)
    hbm = pl.BlockSpec(memory_space=pltpu.HBM)
    return pl.pallas_call(
        functools.partial(response_kernel, rows, bins),
        in_specs=[pl.BlockSpec(memory_space=pltpu.SMEM)] * 3 + [hbm, hbm],
        out_specs=pl.BlockSpec(memory_space=pltpu.VMEM),
        out_shape=pltpu.VMEM((rows, slabs, channels * 2 * STEPS, SLAB), BF16),
        scratch_shapes=[
            pltpu.VMEM(room.shape, BF16),
            pltpu.VMEM(resp.shape, BF16),
            pltpu.SemaphoreType.DMA((rows + 1,)),
        ],
        compiler_params=pltpu.CompilerParams(vmem_limit_bytes=8 * 2**20),
        cost_estimate=COST,
    )(
        *me,
        slots,
        pltpu.with_memory_space_constraint(room, pltpu.HBM),
        pltpu.with_memory_space_constraint(jnp.asarray(resp), pltpu.HBM),
    )


def spectra_kernel(pieces, rows, *refs):
    x_refs, (table_ref, spec_ref, out_ref) = refs[:pieces], refs[pieces:]
    slabs = table_ref.shape[1]
    wide = 2 * SEGS * STEPS
    own = rows // pieces
    span = x_refs[0].shape[0] * own
    flat = x_refs if own == 1 else [ref.reshape(span, slabs * SLAB) for ref in x_refs]
    x = jnp.concatenate([ref[...] for ref in flat], axis=0)
    for step in range(slabs * SLAB // LANES):
        plain, packed, sign = lane_masks(step * LANES, LANES)
        spectra = []
        for j in range(2):
            one = dot(x, two_slabs(table_ref, step, j))
            spectra.append(one + sign * pltpu.roll(one, one.shape[0] - own, axis=0))
        for piece in range(pieces):
            both = [s[piece * span : (piece + 1) * span] for s in spectra]
            both = jnp.concatenate(both, axis=0)
            if step == 0:
                hat = dot(spec_ref[0], (both * plain).astype(BF16)) + dot(spec_ref[1], (both * packed).astype(BF16))
            else:
                hat = dot(spec_ref[0], both.astype(BF16))
            hat = hat.astype(BF16)
            for k in range(own):
                for i in range(LANES // SLAB):
                    at = slice(i * SLAB, (i + 1) * SLAB)
                    out_ref[step * (LANES // SLAB) + i, piece * own + k] = hat[k * wide : (k + 1) * wide, at]


def transform_signals(x_list, own, bins, parts):
    frames = parts + SEGS * KEEP
    rows = own * len(x_list)
    slabs = bins // SLAB
    table, _ = block_tables(bins)
    spec, _, _ = step_tables(parts, frames, 2, own)
    vmem = pl.BlockSpec(memory_space=pltpu.VMEM)
    operands = [*x_list, jnp.asarray(table), jnp.asarray(spec)]
    return pl.pallas_call(
        functools.partial(spectra_kernel, len(x_list), rows),
        in_specs=[vmem] * len(operands),
        out_specs=vmem,
        out_shape=jax.ShapeDtypeStruct((slabs, rows, 2 * SEGS * STEPS, SLAB), BF16),
        compiler_params=pltpu.CompilerParams(vmem_limit_bytes=8 * 2**20),
        cost_estimate=COST,
    )(*operands)


def mix_kernel(flips, own, channels, blocks, shares, has_total, last, src_ref, ch_ref, *refs):
    refs = list(refs)
    s_refs = [refs.pop(0) for _ in flips]
    hat_ref = refs.pop(0)
    total_ref = refs.pop(0) if has_total else None
    if last:
        back_ref, inv_ref = refs.pop(0), refs.pop(0)
        out_refs = [refs.pop(0) for _ in range(shares)]
        y_ref, left_re, left_im, time_ref = refs
    else:
        (out_ref,) = refs

    slabs = hat_ref.shape[1]
    steps = slabs * SLAB // LANES
    half = 2 * STEPS
    pairs = channels // 2
    sources = []
    for ref, some in zip(s_refs, flips):
        for k, flip in enumerate(some):
            for i in range(own):
                sources.append((ref, k * own + i, (ch_ref[0] ^ flip) * own + i))
    groups = -(-len(sources) // GROUP)
    size = -(-len(sources) // groups)

    def twice(rows):
        rows = rows.astype(F32)
        return jnp.concatenate([rows, rows], axis=0).astype(BF16)

    def products(slab, seg):
        re_in = slice(2 * seg * STEPS, (2 * seg + 1) * STEPS)
        im_in = slice((2 * seg + 1) * STEPS, (2 * seg + 2) * STEPS)
        re_rows = slice(2 * seg * half, (2 * seg + 1) * half)
        im_rows = slice((2 * seg + 1) * half, (2 * seg + 2) * half)
        spectra = [(twice(ref[slab, r, re_in]), twice(ref[slab, r, im_in])) for ref, r, _ in sources]
        for pair in range(pairs):
            base = pair * 2 * half
            re_sum = total_ref[slab, pair, re_rows] if has_total else None
            im_sum = total_ref[slab, pair, im_rows] if has_total else None
            for start in range(0, len(sources), size):
                re, im = None, None
                for (s_re, s_im), (_, _, slot) in list(zip(spectra, sources))[start : start + size]:
                    h_re = hat_ref[slot, slab, base : base + half]
                    h_im = hat_ref[slot, slab, base + half : base + 2 * half]
                    add_re = s_re * h_re - s_im * h_im
                    add_im = s_re * h_im + s_im * h_re
                    re = add_re if re is None else re + add_re
                    im = add_im if im is None else im + add_im
                re, im = re.astype(F32), im.astype(F32)
                re_sum = re if re_sum is None else re_sum + re
                im_sum = im if im_sum is None else im_sum + im
            if last:
                y_ref[slab, pair, re_rows] = re_sum.astype(BF16)
                y_ref[slab, pair, im_rows] = im_sum.astype(BF16)
            else:
                out_ref[slab, pair, re_rows] = re_sum
                out_ref[slab, pair, im_rows] = im_sum

    for step in range(steps):
        first = step * (LANES // SLAB)
        for i in range(LANES // SLAB):
            for seg in range(SEGS):
                products(first + i, seg)
        if not last:
            continue
        for pair in range(pairs):
            y = jnp.concatenate([y_ref[first + i, pair] for i in range(LANES // SLAB)], axis=-1)
            if step == 0:
                plain, packed, _ = lane_masks(0, LANES)
                mix = dot(back_ref[0], y * plain.astype(BF16)) + dot(back_ref[1], y * packed.astype(BF16))
            else:
                mix = dot(back_ref[0], y)
            mix = mix.astype(BF16)
            here = slice(step * LANES, (step + 1) * LANES)
            for c in range(2):
                rows_to = slice((2 * pair + c) * blocks, (2 * pair + c + 1) * blocks)
                left_re[rows_to, here] = mix[2 * c * blocks : (2 * c + 1) * blocks]
                left_im[rows_to, here] = mix[(2 * c + 1) * blocks : (2 * c + 2) * blocks]

    if last:
        each = blocks // shares
        for step in range(steps):
            here = slice(step * LANES, (step + 1) * LANES)
            part = dot(left_re[...], two_slabs(inv_ref, step, 0)) + dot(left_im[...], two_slabs(inv_ref, step, 1))
            for t in range(shares):
                for c in range(channels):
                    row = c * blocks + t * each
                    time_ref[t, c, :, here] = part[row : row + each]
        for d in range(shares):
            out_refs[d][...] = time_ref[src_ref[0] ^ d].astype(BF16)


def add_sources(s_list, flips, own, me, hat, total, last, shares, channels, parts):
    slabs = hat.shape[1]
    bins = slabs * SLAB
    frames = parts + SEGS * KEEP
    blocks = frames - parts
    wide = 2 * SEGS * STEPS
    _, inverse = block_tables(bins)
    _, _, back = step_tables(parts, frames, channels)
    vmem = pl.BlockSpec(memory_space=pltpu.VMEM)
    smem = pl.BlockSpec(memory_space=pltpu.SMEM)

    operands = [*me] + list(s_list) + [pltpu.with_memory_space_constraint(hat, pltpu.VMEM)]
    aliases = {}
    if total is not None:
        if not last:
            aliases = {len(operands): 0}
        operands.append(total)
    scratch = []
    if last:
        operands += [jnp.asarray(back), jnp.asarray(inverse)]
        each = blocks // shares
        out_shape = [jax.ShapeDtypeStruct((channels, each, bins), BF16)] * shares
        scratch = [
            pltpu.VMEM((slabs, channels // 2, 2 * wide, SLAB), BF16),
            pltpu.VMEM((channels * blocks, bins), BF16),
            pltpu.VMEM((channels * blocks, bins), BF16),
            pltpu.VMEM((shares, channels, each, bins), F32),
        ]
    else:
        out_shape = jax.ShapeDtypeStruct((slabs, channels // 2, 2 * wide, SLAB), F32)
    body = functools.partial(
        mix_kernel, tuple(flips), own, channels, blocks, shares, total is not None, last
    )
    return pl.pallas_call(
        body,
        in_specs=[smem] * 2 + [vmem] * (len(operands) - 2),
        out_specs=[vmem] * len(out_shape) if last else vmem,
        out_shape=out_shape,
        scratch_shapes=scratch,
        input_output_aliases=aliases,
        compiler_params=pltpu.CompilerParams(vmem_limit_bytes=12 * 2**20),
        cost_estimate=COST,
    )(*operands)


def sum_kernel(count, ch_ref, *refs):
    parts, outs, sum_ref = refs[:count], refs[count:-1], refs[-1]
    total = parts[0][...].astype(F32)
    for part in parts[1:]:
        total = total + part[...].astype(F32)
    sum_ref[...] = total
    for d in range(len(outs)):
        outs[d][...] = sum_ref[:, pl.ds(ch_ref[0] ^ d, 1), :].reshape(outs[d].shape).astype(BF16)


def sum_groups(parts, me):
    channels, each, bins = parts[0].shape
    vmem = pl.BlockSpec(memory_space=pltpu.VMEM)
    return pl.pallas_call(
        functools.partial(sum_kernel, len(parts)),
        in_specs=[pl.BlockSpec(memory_space=pltpu.SMEM)] + [vmem] * len(parts),
        out_specs=[vmem] * each,
        out_shape=[jax.ShapeDtypeStruct((channels, bins), BF16)] * each,
        scratch_shapes=[pltpu.VMEM(parts[0].shape, F32)],
        compiler_params=pltpu.CompilerParams(vmem_limit_bytes=8 * 2**20),
    )(me, *parts)


def decode(signal, matrix):
    decoded = lax.dot_general(
        signal, matrix, (((0,), (0,)), ((), ())), preferred_element_type=F32
    )
    return decoded.astype(BF16)


def per_device(src_count, ch_count, dry_signal, room_spectra, render_slot, decoder):
    rows_total, parts, channels, _, block_len = room_spectra.shape
    own = dry_signal.shape[0]
    frames = dry_signal.shape[1] // block_len
    blocks = frames - parts
    src_me = lax.axis_index("src").astype(jnp.int32)
    ch_me = lax.axis_index("ch").astype(jnp.int32)

    if own == 1:
        x_own = dry_signal.reshape(frames, block_len)
    else:
        x_own = dry_signal.reshape(own, frames, block_len).transpose(1, 0, 2)

    def swap(value, axis, count, flip):
        return lax.ppermute(value, axis, [(i, i ^ flip) for i in range(count)])

    chips = ch_count // 2
    first = chips // 2
    far = [first] + [d for d in range(chips - 1, 0, -1) if d != first]
    mate = swap(x_own, "ch", ch_count, 1)
    lanes = {d: swap(x_own, "ch", ch_count, 2 * d) for d in far}
    me = (src_me[None], ch_me[None])
    hat = transform_responses(room_spectra, me, render_slot)

    row = jnp.arange(ch_count * channels, dtype=jnp.int32)
    takes = ((row // channels) ^ ch_me) * channels + row % channels
    order = (takes[:, None] == row[None, :]).astype(BF16)
    own_order = lax.optimization_barrier(dot(order, decoder).astype(BF16))

    def add(s_list, flips, total, last):
        return add_sources(
            s_list, flips, own, me, hat, total, last, src_count, channels, parts
        )

    x_near, hat = lax.optimization_barrier((x_own, hat))
    near = transform_signals([x_near, mate], own, block_len, parts)
    total = add([near], [[0, 1]], None, False)
    *late, total = lax.optimization_barrier((*[lanes[d] for d in far], total))
    mine = transform_signals(late, own, block_len, parts)
    given = swap(mine, "ch", ch_count, 1)
    total = add([mine], [[2 * d for d in far]], total, False)
    total = add([given], [[2 * d + 1 for d in far]], total, True)

    sums = [total[0]] + [swap(total[d], "src", src_count, d) for d in range(1, src_count)]
    if blocks == src_count * ch_count:
        pieces = sum_groups(sums, ch_me[None])
        given = swap(jnp.concatenate(pieces[1::2], axis=0), "ch", ch_count, 1)
        both = [
            jnp.concatenate([pieces[2 * d], given[d * channels : (d + 1) * channels]], axis=0)
            for d in range(chips)
        ]
        both[1:] = [swap(both[d], "ch", ch_count, 2 * d) for d in range(1, chips)]
        return decode(jnp.concatenate(both, axis=0), own_order)
    signal = sums[0].astype(F32)
    for part in sums[1:]:
        signal = signal + part.astype(F32)
    signal = signal.astype(BF16).reshape(channels, -1)
    return decode(lax.all_to_all(signal, "ch", split_axis=1, concat_axis=0, tiled=True), decoder)


def solution(mesh):
    body = functools.partial(per_device, mesh.shape["src"], mesh.shape["ch"])
    return jax.shard_map(
        body,
        mesh=mesh,
        in_specs=(P(("src", "ch"), None), P("src", None, "ch", None, None), P("src"), P()),
        out_specs=P(("src", "ch"), None),
        check_vma=False,
    )
```

```python
import functools
import math

import jax
import jax.numpy as jnp
import ml_dtypes
import numpy as np
from jax import lax
from jax.experimental import pallas as pl
from jax.experimental.pallas import tpu as pltpu
from jax.sharding import PartitionSpec as P

BF16 = jnp.bfloat16
F32 = jnp.float32
LANES = 256
SLAB = 128
GROUP = 4
COST = pl.CostEstimate(flops=2**20, bytes_accessed=2**16, transcendentals=0)
ROWS = 4
STEPS = 24
SEGS = 2
KEEP = 16


def bf16_table(values):
    return np.asarray(values, dtype=np.float32).astype(ml_dtypes.bfloat16)


@functools.lru_cache(maxsize=None)
def block_tables(block_len):
    size = 2 * block_len
    n = np.arange(block_len)[:, None]
    k = np.arange(block_len)[None, :]
    angle = ((n * k) % size) * (2.0 * math.pi / size)
    fwd_real = np.cos(angle)
    fwd_imag = np.where(k == 0, 1.0 - 2.0 * (n % 2), -np.sin(angle))
    kk = np.arange(block_len)[:, None]
    m = np.arange(block_len)[None, :] + block_len
    angle = ((kk * m) % size) * (2.0 * math.pi / size)
    weight = np.where(kk == 0, 1.0, 2.0)
    inv_real = weight * np.cos(angle) / size
    inv_imag = np.where(kk == 0, (1.0 - 2.0 * (m % 2)) / size, -2.0 * np.sin(angle) / size)
    def slabs(pair):
        return bf16_table(np.stack(pair).reshape(2, block_len, -1, SLAB).transpose(0, 2, 1, 3))

    return slabs([fwd_real, fwd_imag]), slabs([inv_real, inv_imag])


@functools.lru_cache(maxsize=None)
def step_tables(parts, frames, channels, own=1):
    half = STEPS // 2
    theta = 2.0 * math.pi * (np.arange(STEPS) + 0.5) / STEPS
    first = (np.arange(STEPS) < half).astype(np.float64)[:, None]

    def forward(steps):
        cos = np.cos(theta[:, None] * steps[None, :])
        sin = np.sin(theta[:, None] * steps[None, :])
        plain = np.block([[cos, sin], [-sin, cos]])
        packed = np.block([[cos * first, cos * (1 - first)], [-sin * first, -sin * (1 - first)]])
        return plain, packed

    spec = np.zeros((2, SEGS, 2, STEPS, 2, frames))
    used = parts - 1 + KEEP
    for kind, table in enumerate(forward(np.arange(used))):
        table = table.reshape(2, STEPS, 2, used)
        for seg in range(SEGS):
            spec[kind, seg, :, :, :, seg * KEEP : seg * KEEP + used] = table
    spec = spec.reshape(2, 1, SEGS * 2 * STEPS, 2 * frames, 1) * np.eye(own)[None, :, None, None, :]
    spec = spec.reshape(2, own * SEGS * 2 * STEPS, 2 * frames * own)

    resp = np.zeros((channels // 2, 2, 2, STEPS, 2, parts, channels, 2))
    for kind, table in enumerate(forward(np.arange(parts))):
        table = table.reshape(2, STEPS, 2, parts).transpose(0, 1, 3, 2)
        for c in range(channels):
            resp[c // 2, :, c % 2, :, kind, :, c] = table
    resp = resp.reshape(channels * 2 * STEPS, 2 * parts * channels * 2)

    back = np.zeros((2, 2, 2, SEGS, KEEP, SEGS, 2, 2, STEPS))
    steps = np.arange(KEEP) + parts - 1
    cos = np.cos(theta[None, :] * steps[:, None]) / STEPS
    sin = np.sin(theta[None, :] * steps[:, None]) / STEPS
    firsts = first[:, 0][None, :]
    for seg in range(SEGS):
        for c in range(2):
            back[0, c, 0, seg, :, seg, 0, c] = cos
            back[0, c, 0, seg, :, seg, 1, c] = -sin
            back[0, c, 1, seg, :, seg, 0, c] = sin
            back[0, c, 1, seg, :, seg, 1, c] = cos
            back[1, c, 0, seg, :, seg, 0, c] = 2 * cos * firsts
            back[1, c, 0, seg, :, seg, 1, c] = -2 * sin * firsts
            back[1, c, 1, seg, :, seg, 0, c] = 2 * cos * (1 - firsts)
            back[1, c, 1, seg, :, seg, 1, c] = -2 * sin * (1 - firsts)
    back = back.reshape(2, 4 * SEGS * KEEP, 4 * SEGS * STEPS)
    return bf16_table(spec), bf16_table(resp), bf16_table(back)


def dot(left, right):
    return jnp.dot(left, right, preferred_element_type=F32)


def lane_masks(start, width):
    lane = lax.broadcasted_iota(jnp.int32, (1, width), 1) + start
    packed = (lane == 0).astype(F32)
    sign = (1 - 2 * (lane % 2)).astype(F32)
    return 1.0 - packed, packed, sign


def two_slabs(ref, step, *index):
    first = step * (LANES // SLAB)
    return jnp.concatenate([ref[(*index, first + i)] for i in range(LANES // SLAB)], axis=-1)


def response_kernel(rows, bins, src_ref, ch_ref, slot_ref, room_hbm, table_hbm, hat_ref, room_ref, table_ref, sems):
    depth = room_ref.shape[1] * room_ref.shape[2] * 2
    flat = room_ref.reshape(rows, depth, bins)
    plain, packed, _ = lane_masks(0, LANES)
    plain, packed = plain.astype(BF16), packed.astype(BF16)

    def copy(r):
        row = lax.rem(slot_ref[r], rows)
        return pltpu.make_async_copy(room_hbm.at[row], room_ref.at[r], sems.at[r])

    table_copy = pltpu.make_async_copy(table_hbm, table_ref, sems.at[rows])
    table_copy.start()
    for r in range(rows):
        copy(r).start()
    table_copy.wait()

    def some(outer, carry):
        for inner in range(ROWS):
            copy(outer * ROWS + inner).wait()
        for inner in range(ROWS):
            r = outer * ROWS + inner
            for step in range(bins // LANES):
                h = flat[r, :, step * LANES : (step + 1) * LANES]
                if step == 0:
                    h = jnp.concatenate([h * plain, h * packed], axis=0)
                    hat = dot(table_ref[...], h)
                else:
                    hat = dot(table_ref[:, :depth], h)
                hat = hat.astype(BF16)
                for i in range(LANES // SLAB):
                    hat_ref[r, step * (LANES // SLAB) + i] = hat[:, i * SLAB : (i + 1) * SLAB]
        return carry

    lax.fori_loop(0, rows // ROWS, some, 0)


def transform_responses(room, me, slots):
    rows, parts, channels, _, bins = room.shape
    slabs = bins // SLAB
    _, resp, _ = step_tables(parts, parts + SEGS * KEEP, channels)
    hbm = pl.BlockSpec(memory_space=pltpu.HBM)
    return pl.pallas_call(
        functools.partial(response_kernel, rows, bins),
        in_specs=[pl.BlockSpec(memory_space=pltpu.SMEM)] * 3 + [hbm, hbm],
        out_specs=pl.BlockSpec(memory_space=pltpu.VMEM),
        out_shape=pltpu.VMEM((rows, slabs, channels * 2 * STEPS, SLAB), BF16),
        scratch_shapes=[
            pltpu.VMEM(room.shape, BF16),
            pltpu.VMEM(resp.shape, BF16),
            pltpu.SemaphoreType.DMA((rows + 1,)),
        ],
        compiler_params=pltpu.CompilerParams(vmem_limit_bytes=8 * 2**20),
        cost_estimate=COST,
    )(
        *me,
        slots,
        pltpu.with_memory_space_constraint(room, pltpu.HBM),
        pltpu.with_memory_space_constraint(jnp.asarray(resp), pltpu.HBM),
    )


def spectra_kernel(pieces, rows, *refs):
    x_refs, (table_ref, spec_ref, out_ref) = refs[:pieces], refs[pieces:]
    slabs = table_ref.shape[1]
    wide = 2 * SEGS * STEPS
    own = rows // pieces
    span = x_refs[0].shape[0] * own
    flat = x_refs if own == 1 else [ref.reshape(span, slabs * SLAB) for ref in x_refs]
    x = jnp.concatenate([ref[...] for ref in flat], axis=0)
    for step in range(slabs * SLAB // LANES):
        plain, packed, sign = lane_masks(step * LANES, LANES)
        spectra = []
        for j in range(2):
            one = dot(x, two_slabs(table_ref, step, j))
            spectra.append(one + sign * pltpu.roll(one, one.shape[0] - own, axis=0))
        for piece in range(pieces):
            both = [s[piece * span : (piece + 1) * span] for s in spectra]
            both = jnp.concatenate(both, axis=0)
            if step == 0:
                hat = dot(spec_ref[0], (both * plain).astype(BF16)) + dot(spec_ref[1], (both * packed).astype(BF16))
            else:
                hat = dot(spec_ref[0], both.astype(BF16))
            hat = hat.astype(BF16)
            for k in range(own):
                for i in range(LANES // SLAB):
                    at = slice(i * SLAB, (i + 1) * SLAB)
                    out_ref[step * (LANES // SLAB) + i, piece * own + k] = hat[k * wide : (k + 1) * wide, at]


def transform_signals(x_list, own, bins, parts):
    frames = parts + SEGS * KEEP
    rows = own * len(x_list)
    slabs = bins // SLAB
    table, _ = block_tables(bins)
    spec, _, _ = step_tables(parts, frames, 2, own)
    vmem = pl.BlockSpec(memory_space=pltpu.VMEM)
    operands = [*x_list, jnp.asarray(table), jnp.asarray(spec)]
    return pl.pallas_call(
        functools.partial(spectra_kernel, len(x_list), rows),
        in_specs=[vmem] * len(operands),
        out_specs=vmem,
        out_shape=jax.ShapeDtypeStruct((slabs, rows, 2 * SEGS * STEPS, SLAB), BF16),
        compiler_params=pltpu.CompilerParams(vmem_limit_bytes=8 * 2**20),
        cost_estimate=COST,
    )(*operands)


def mix_kernel(flips, own, channels, blocks, shares, has_total, last, src_ref, ch_ref, *refs):
    refs = list(refs)
    s_refs = [refs.pop(0) for _ in flips]
    hat_ref = refs.pop(0)
    total_ref = refs.pop(0) if has_total else None
    if last:
        back_ref, inv_ref = refs.pop(0), refs.pop(0)
        out_refs = [refs.pop(0) for _ in range(shares)]
        y_ref, left_re, left_im, time_ref = refs
    else:
        (out_ref,) = refs

    slabs = hat_ref.shape[1]
    steps = slabs * SLAB // LANES
    half = 2 * STEPS
    pairs = channels // 2
    sources = []
    for ref, some in zip(s_refs, flips):
        for k, flip in enumerate(some):
            for i in range(own):
                sources.append((ref, k * own + i, (ch_ref[0] ^ flip) * own + i))
    groups = -(-len(sources) // GROUP)
    size = -(-len(sources) // groups)

    def twice(rows):
        rows = rows.astype(F32)
        return jnp.concatenate([rows, rows], axis=0).astype(BF16)

    def products(slab, seg):
        re_in = slice(2 * seg * STEPS, (2 * seg + 1) * STEPS)
        im_in = slice((2 * seg + 1) * STEPS, (2 * seg + 2) * STEPS)
        re_rows = slice(2 * seg * half, (2 * seg + 1) * half)
        im_rows = slice((2 * seg + 1) * half, (2 * seg + 2) * half)
        spectra = [(twice(ref[slab, r, re_in]), twice(ref[slab, r, im_in])) for ref, r, _ in sources]
        for pair in range(pairs):
            base = pair * 2 * half
            re_sum = total_ref[slab, pair, re_rows] if has_total else None
            im_sum = total_ref[slab, pair, im_rows] if has_total else None
            for start in range(0, len(sources), size):
                re, im = None, None
                for (s_re, s_im), (_, _, slot) in list(zip(spectra, sources))[start : start + size]:
                    h_re = hat_ref[slot, slab, base : base + half]
                    h_im = hat_ref[slot, slab, base + half : base + 2 * half]
                    add_re = s_re * h_re - s_im * h_im
                    add_im = s_re * h_im + s_im * h_re
                    re = add_re if re is None else re + add_re
                    im = add_im if im is None else im + add_im
                re, im = re.astype(F32), im.astype(F32)
                re_sum = re if re_sum is None else re_sum + re
                im_sum = im if im_sum is None else im_sum + im
            if last:
                y_ref[slab, pair, re_rows] = re_sum.astype(BF16)
                y_ref[slab, pair, im_rows] = im_sum.astype(BF16)
            else:
                out_ref[slab, pair, re_rows] = re_sum
                out_ref[slab, pair, im_rows] = im_sum

    for step in range(steps):
        first = step * (LANES // SLAB)
        for i in range(LANES // SLAB):
            for seg in range(SEGS):
                products(first + i, seg)
        if not last:
            continue
        for pair in range(pairs):
            y = jnp.concatenate([y_ref[first + i, pair] for i in range(LANES // SLAB)], axis=-1)
            if step == 0:
                plain, packed, _ = lane_masks(0, LANES)
                mix = dot(back_ref[0], y * plain.astype(BF16)) + dot(back_ref[1], y * packed.astype(BF16))
            else:
                mix = dot(back_ref[0], y)
            mix = mix.astype(BF16)
            here = slice(step * LANES, (step + 1) * LANES)
            for c in range(2):
                rows_to = slice((2 * pair + c) * blocks, (2 * pair + c + 1) * blocks)
                left_re[rows_to, here] = mix[2 * c * blocks : (2 * c + 1) * blocks]
                left_im[rows_to, here] = mix[(2 * c + 1) * blocks : (2 * c + 2) * blocks]

    if last:
        each = blocks // shares
        for step in range(steps):
            here = slice(step * LANES, (step + 1) * LANES)
            part = dot(left_re[...], two_slabs(inv_ref, step, 0)) + dot(left_im[...], two_slabs(inv_ref, step, 1))
            for t in range(shares):
                for c in range(channels):
                    row = c * blocks + t * each
                    time_ref[t, c, :, here] = part[row : row + each]
        for d in range(shares):
            out_refs[d][...] = time_ref[src_ref[0] ^ d].astype(BF16)


def add_sources(s_list, flips, own, me, hat, total, last, shares, channels, parts):
    slabs = hat.shape[1]
    bins = slabs * SLAB
    frames = parts + SEGS * KEEP
    blocks = frames - parts
    wide = 2 * SEGS * STEPS
    _, inverse = block_tables(bins)
    _, _, back = step_tables(parts, frames, channels)
    vmem = pl.BlockSpec(memory_space=pltpu.VMEM)
    smem = pl.BlockSpec(memory_space=pltpu.SMEM)

    operands = [*me] + list(s_list) + [pltpu.with_memory_space_constraint(hat, pltpu.VMEM)]
    aliases = {}
    if total is not None:
        if not last:
            aliases = {len(operands): 0}
        operands.append(total)
    scratch = []
    if last:
        operands += [jnp.asarray(back), jnp.asarray(inverse)]
        each = blocks // shares
        out_shape = [jax.ShapeDtypeStruct((channels, each, bins), BF16)] * shares
        scratch = [
            pltpu.VMEM((slabs, channels // 2, 2 * wide, SLAB), BF16),
            pltpu.VMEM((channels * blocks, bins), BF16),
            pltpu.VMEM((channels * blocks, bins), BF16),
            pltpu.VMEM((shares, channels, each, bins), F32),
        ]
    else:
        out_shape = jax.ShapeDtypeStruct((slabs, channels // 2, 2 * wide, SLAB), F32)
    body = functools.partial(
        mix_kernel, tuple(flips), own, channels, blocks, shares, total is not None, last
    )
    return pl.pallas_call(
        body,
        in_specs=[smem] * 2 + [vmem] * (len(operands) - 2),
        out_specs=[vmem] * len(out_shape) if last else vmem,
        out_shape=out_shape,
        scratch_shapes=scratch,
        input_output_aliases=aliases,
        compiler_params=pltpu.CompilerParams(vmem_limit_bytes=12 * 2**20),
        cost_estimate=COST,
    )(*operands)


def sum_kernel(count, ch_ref, *refs):
    parts, outs, sum_ref = refs[:count], refs[count:-1], refs[-1]
    total = parts[0][...].astype(F32)
    for part in parts[1:]:
        total = total + part[...].astype(F32)
    sum_ref[...] = total
    for d in range(len(outs)):
        outs[d][...] = sum_ref[:, pl.ds(ch_ref[0] ^ d, 1), :].reshape(outs[d].shape).astype(BF16)


def sum_groups(parts, me):
    channels, each, bins = parts[0].shape
    vmem = pl.BlockSpec(memory_space=pltpu.VMEM)
    return pl.pallas_call(
        functools.partial(sum_kernel, len(parts)),
        in_specs=[pl.BlockSpec(memory_space=pltpu.SMEM)] + [vmem] * len(parts),
        out_specs=[vmem] * each,
        out_shape=[jax.ShapeDtypeStruct((channels, bins), BF16)] * each,
        scratch_shapes=[pltpu.VMEM(parts[0].shape, F32)],
        compiler_params=pltpu.CompilerParams(vmem_limit_bytes=8 * 2**20),
    )(me, *parts)


def decode(signal, matrix):
    decoded = lax.dot_general(
        signal, matrix, (((0,), (0,)), ((), ())), preferred_element_type=F32
    )
    return decoded.astype(BF16)


def per_device(src_count, ch_count, dry_signal, room_spectra, render_slot, decoder):
    rows_total, parts, channels, _, block_len = room_spectra.shape
    own = dry_signal.shape[0]
    frames = dry_signal.shape[1] // block_len
    blocks = frames - parts
    src_me = lax.axis_index("src").astype(jnp.int32)
    ch_me = lax.axis_index("ch").astype(jnp.int32)

    if own == 1:
        x_own = dry_signal.reshape(frames, block_len)
    else:
        x_own = dry_signal.reshape(own, frames, block_len).transpose(1, 0, 2)

    def swap(value, axis, count, flip):
        return lax.ppermute(value, axis, [(i, i ^ flip) for i in range(count)])

    chips = ch_count // 2
    first = chips // 2
    far = [first] + [d for d in range(chips - 1, 0, -1) if d != first]
    mate = swap(x_own, "ch", ch_count, 1)
    lanes = {d: swap(x_own, "ch", ch_count, 2 * d) for d in far}
    me = (src_me[None], ch_me[None])
    hat = transform_responses(room_spectra, me, render_slot)

    row = jnp.arange(ch_count * channels, dtype=jnp.int32)
    chip_order = [0] + list(range(chips - 2, 0, -1)) + [chips - 1]
    flips = np.array([2 * d + core for d in chip_order for core in range(2)], dtype=np.int32)
    takes = (jnp.asarray(np.repeat(flips, channels)) ^ ch_me) * channels + row % channels
    order = (takes[:, None] == row[None, :]).astype(BF16)
    own_order = lax.optimization_barrier(dot(order, decoder).astype(BF16))

    def add(s_list, flips, total, last):
        return add_sources(
            s_list, flips, own, me, hat, total, last, src_count, channels, parts
        )

    x_near, hat = lax.optimization_barrier((x_own, hat))
    near = transform_signals([x_near, mate], own, block_len, parts)
    total = add([near], [[0, 1]], None, False)
    *late, total = lax.optimization_barrier((*[lanes[d] for d in far], total))
    mine = transform_signals(late, own, block_len, parts)
    given = swap(mine, "ch", ch_count, 1)
    total = add([mine], [[2 * d for d in far]], total, False)
    total = add([given], [[2 * d + 1 for d in far]], total, True)

    sums = [total[0]] + [swap(total[d], "src", src_count, d) for d in range(1, src_count)]
    if blocks == src_count * ch_count:
        pieces = sum_groups(sums, ch_me[None])
        given = swap(jnp.concatenate(pieces[1::2], axis=0), "ch", ch_count, 1)
        both = {
            d: jnp.concatenate([pieces[2 * d], given[d * channels : (d + 1) * channels]], axis=0)
            for d in chip_order
        }
        arrived = [both[0]] + [swap(both[d], "ch", ch_count, 2 * d) for d in chip_order[1:]]
        return decode(jnp.concatenate(arrived, axis=0), own_order)
    signal = sums[0].astype(F32)
    for part in sums[1:]:
        signal = signal + part.astype(F32)
    signal = signal.astype(BF16).reshape(channels, -1)
    return decode(lax.all_to_all(signal, "ch", split_axis=1, concat_axis=0, tiled=True), decoder)


def solution(mesh):
    body = functools.partial(per_device, mesh.shape["src"], mesh.shape["ch"])
    return jax.shard_map(
        body,
        mesh=mesh,
        in_specs=(P(("src", "ch"), None), P("src", None, "ch", None, None), P("src"), P()),
        out_specs=P(("src", "ch"), None),
        check_vma=False,
    )
```

```python
import functools
import math

import jax
import jax.numpy as jnp
import ml_dtypes
import numpy as np
from jax import lax
from jax.experimental import pallas as pl
from jax.experimental.pallas import tpu as pltpu
from jax.sharding import PartitionSpec as P

BF16 = jnp.bfloat16
F32 = jnp.float32
LANES = 256
SLAB = 128
GROUP = 4
COST = pl.CostEstimate(flops=2**20, bytes_accessed=2**16, transcendentals=0)
ROWS = 4
STEPS = 24
SEGS = 2
KEEP = 16


def bf16_table(values):
    return np.asarray(values, dtype=np.float32).astype(ml_dtypes.bfloat16)


@functools.lru_cache(maxsize=None)
def block_tables(block_len):
    size = 2 * block_len
    n = np.arange(block_len)[:, None]
    k = np.arange(block_len)[None, :]
    angle = ((n * k) % size) * (2.0 * math.pi / size)
    fwd_real = np.cos(angle)
    fwd_imag = np.where(k == 0, 1.0 - 2.0 * (n % 2), -np.sin(angle))
    kk = np.arange(block_len)[:, None]
    m = np.arange(block_len)[None, :] + block_len
    angle = ((kk * m) % size) * (2.0 * math.pi / size)
    weight = np.where(kk == 0, 1.0, 2.0)
    inv_real = weight * np.cos(angle) / size
    inv_imag = np.where(kk == 0, (1.0 - 2.0 * (m % 2)) / size, -2.0 * np.sin(angle) / size)
    def slabs(pair):
        return bf16_table(np.stack(pair).reshape(2, block_len, -1, SLAB).transpose(0, 2, 1, 3))

    return slabs([fwd_real, fwd_imag]), slabs([inv_real, inv_imag])


@functools.lru_cache(maxsize=None)
def step_tables(parts, frames, channels, own=1):
    half = STEPS // 2
    theta = 2.0 * math.pi * (np.arange(STEPS) + 0.5) / STEPS
    first = (np.arange(STEPS) < half).astype(np.float64)[:, None]

    def forward(steps):
        cos = np.cos(theta[:, None] * steps[None, :])
        sin = np.sin(theta[:, None] * steps[None, :])
        plain = np.block([[cos, sin], [-sin, cos]])
        packed = np.block([[cos * first, cos * (1 - first)], [-sin * first, -sin * (1 - first)]])
        return plain, packed

    spec = np.zeros((2, SEGS, 2, STEPS, 2, frames))
    used = parts - 1 + KEEP
    for kind, table in enumerate(forward(np.arange(used))):
        table = table.reshape(2, STEPS, 2, used)
        for seg in range(SEGS):
            spec[kind, seg, :, :, :, seg * KEEP : seg * KEEP + used] = table
    spec = spec.reshape(2, 1, SEGS * 2 * STEPS, 2 * frames, 1) * np.eye(own)[None, :, None, None, :]
    spec = spec.reshape(2, own * SEGS * 2 * STEPS, 2 * frames * own)

    resp = np.zeros((channels // 2, 2, 2, STEPS, 2, parts, channels, 2))
    for kind, table in enumerate(forward(np.arange(parts))):
        table = table.reshape(2, STEPS, 2, parts).transpose(0, 1, 3, 2)
        for c in range(channels):
            resp[c // 2, :, c % 2, :, kind, :, c] = table
    resp = resp.reshape(channels * 2 * STEPS, 2 * parts * channels * 2)

    back = np.zeros((2, 2, 2, SEGS, KEEP, SEGS, 2, 2, STEPS))
    steps = np.arange(KEEP) + parts - 1
    cos = np.cos(theta[None, :] * steps[:, None]) / STEPS
    sin = np.sin(theta[None, :] * steps[:, None]) / STEPS
    firsts = first[:, 0][None, :]
    for seg in range(SEGS):
        for c in range(2):
            back[0, c, 0, seg, :, seg, 0, c] = cos
            back[0, c, 0, seg, :, seg, 1, c] = -sin
            back[0, c, 1, seg, :, seg, 0, c] = sin
            back[0, c, 1, seg, :, seg, 1, c] = cos
            back[1, c, 0, seg, :, seg, 0, c] = 2 * cos * firsts
            back[1, c, 0, seg, :, seg, 1, c] = -2 * sin * firsts
            back[1, c, 1, seg, :, seg, 0, c] = 2 * cos * (1 - firsts)
            back[1, c, 1, seg, :, seg, 1, c] = -2 * sin * (1 - firsts)
    back = back.reshape(2, 4 * SEGS * KEEP, 4 * SEGS * STEPS)
    return bf16_table(spec), bf16_table(resp), bf16_table(back)


def dot(left, right):
    return jnp.dot(left, right, preferred_element_type=F32)


def lane_masks(start, width):
    lane = lax.broadcasted_iota(jnp.int32, (1, width), 1) + start
    packed = (lane == 0).astype(F32)
    sign = (1 - 2 * (lane % 2)).astype(F32)
    return 1.0 - packed, packed, sign


def two_slabs(ref, step, *index):
    first = step * (LANES // SLAB)
    return jnp.concatenate([ref[(*index, first + i)] for i in range(LANES // SLAB)], axis=-1)


def response_kernel(rows, bins, src_ref, ch_ref, slot_ref, room_hbm, table_hbm, hat_ref, room_ref, table_ref, sems):
    depth = room_ref.shape[1] * room_ref.shape[2] * 2
    flat = room_ref.reshape(rows, depth, bins)
    plain, packed, _ = lane_masks(0, LANES)
    plain, packed = plain.astype(BF16), packed.astype(BF16)

    def copy(r):
        row = lax.rem(slot_ref[r], rows)
        return pltpu.make_async_copy(room_hbm.at[row], room_ref.at[r], sems.at[r])

    table_copy = pltpu.make_async_copy(table_hbm, table_ref, sems.at[rows])
    table_copy.start()
    for r in range(rows):
        copy(r).start()
    table_copy.wait()

    def some(outer, carry):
        for inner in range(ROWS):
            copy(outer * ROWS + inner).wait()
        for inner in range(ROWS):
            r = outer * ROWS + inner
            for step in range(bins // LANES):
                h = flat[r, :, step * LANES : (step + 1) * LANES]
                if step == 0:
                    h = jnp.concatenate([h * plain, h * packed], axis=0)
                    hat = dot(table_ref[...], h)
                else:
                    hat = dot(table_ref[:, :depth], h)
                hat = hat.astype(BF16)
                for i in range(LANES // SLAB):
                    hat_ref[r, step * (LANES // SLAB) + i] = hat[:, i * SLAB : (i + 1) * SLAB]
        return carry

    lax.fori_loop(0, rows // ROWS, some, 0)


def transform_responses(room, me, slots):
    rows, parts, channels, _, bins = room.shape
    slabs = bins // SLAB
    _, resp, _ = step_tables(parts, parts + SEGS * KEEP, channels)
    hbm = pl.BlockSpec(memory_space=pltpu.HBM)
    return pl.pallas_call(
        functools.partial(response_kernel, rows, bins),
        in_specs=[pl.BlockSpec(memory_space=pltpu.SMEM)] * 3 + [hbm, hbm],
        out_specs=pl.BlockSpec(memory_space=pltpu.VMEM),
        out_shape=pltpu.VMEM((rows, slabs, channels * 2 * STEPS, SLAB), BF16),
        scratch_shapes=[
            pltpu.VMEM(room.shape, BF16),
            pltpu.VMEM(resp.shape, BF16),
            pltpu.SemaphoreType.DMA((rows + 1,)),
        ],
        compiler_params=pltpu.CompilerParams(vmem_limit_bytes=8 * 2**20),
        cost_estimate=COST,
    )(
        *me,
        slots,
        pltpu.with_memory_space_constraint(room, pltpu.HBM),
        pltpu.with_memory_space_constraint(jnp.asarray(resp), pltpu.HBM),
    )


def spectra_kernel(pieces, rows, *refs):
    x_refs, (table_ref, spec_ref, out_ref) = refs[:pieces], refs[pieces:]
    slabs = table_ref.shape[1]
    wide = 2 * SEGS * STEPS
    own = rows // pieces
    span = x_refs[0].shape[0] * own
    flat = x_refs if own == 1 else [ref.reshape(span, slabs * SLAB) for ref in x_refs]
    x = jnp.concatenate([ref[...] for ref in flat], axis=0)
    for step in range(slabs * SLAB // LANES):
        plain, packed, sign = lane_masks(step * LANES, LANES)
        spectra = []
        for j in range(2):
            one = dot(x, two_slabs(table_ref, step, j))
            spectra.append(one + sign * pltpu.roll(one, one.shape[0] - own, axis=0))
        for piece in range(pieces):
            both = [s[piece * span : (piece + 1) * span] for s in spectra]
            both = jnp.concatenate(both, axis=0)
            if step == 0:
                hat = dot(spec_ref[0], (both * plain).astype(BF16)) + dot(spec_ref[1], (both * packed).astype(BF16))
            else:
                hat = dot(spec_ref[0], both.astype(BF16))
            hat = hat.astype(BF16)
            for k in range(own):
                for i in range(LANES // SLAB):
                    at = slice(i * SLAB, (i + 1) * SLAB)
                    out_ref[step * (LANES // SLAB) + i, piece * own + k] = hat[k * wide : (k + 1) * wide, at]


def transform_signals(x_list, own, bins, parts):
    frames = parts + SEGS * KEEP
    rows = own * len(x_list)
    slabs = bins // SLAB
    table, _ = block_tables(bins)
    spec, _, _ = step_tables(parts, frames, 2, own)
    vmem = pl.BlockSpec(memory_space=pltpu.VMEM)
    operands = [*x_list, jnp.asarray(table), jnp.asarray(spec)]
    return pl.pallas_call(
        functools.partial(spectra_kernel, len(x_list), rows),
        in_specs=[vmem] * len(operands),
        out_specs=vmem,
        out_shape=jax.ShapeDtypeStruct((slabs, rows, 2 * SEGS * STEPS, SLAB), BF16),
        compiler_params=pltpu.CompilerParams(vmem_limit_bytes=8 * 2**20),
        cost_estimate=COST,
    )(*operands)


def mix_kernel(flips, own, channels, blocks, shares, has_total, last, src_ref, ch_ref, *refs):
    refs = list(refs)
    s_refs = [refs.pop(0) for _ in flips]
    hat_ref = refs.pop(0)
    total_ref = refs.pop(0) if has_total else None
    if last:
        back_ref, inv_ref = refs.pop(0), refs.pop(0)
        out_refs = [refs.pop(0) for _ in range(shares)]
        y_ref, left_re, left_im, time_ref = refs
    else:
        (out_ref,) = refs

    slabs = hat_ref.shape[1]
    steps = slabs * SLAB // LANES
    half = 2 * STEPS
    pairs = channels // 2
    sources = []
    for ref, some in zip(s_refs, flips):
        for k, flip in enumerate(some):
            for i in range(own):
                sources.append((ref, k * own + i, (ch_ref[0] ^ flip) * own + i))
    groups = -(-len(sources) // GROUP)
    size = -(-len(sources) // groups)

    def twice(rows):
        rows = rows.astype(F32)
        return jnp.concatenate([rows, rows], axis=0).astype(BF16)

    def products(slab, seg):
        re_in = slice(2 * seg * STEPS, (2 * seg + 1) * STEPS)
        im_in = slice((2 * seg + 1) * STEPS, (2 * seg + 2) * STEPS)
        re_rows = slice(2 * seg * half, (2 * seg + 1) * half)
        im_rows = slice((2 * seg + 1) * half, (2 * seg + 2) * half)
        spectra = [(twice(ref[slab, r, re_in]), twice(ref[slab, r, im_in])) for ref, r, _ in sources]
        for pair in range(pairs):
            base = pair * 2 * half
            re_sum = total_ref[slab, pair, re_rows] if has_total else None
            im_sum = total_ref[slab, pair, im_rows] if has_total else None
            for start in range(0, len(sources), size):
                re, im = None, None
                for (s_re, s_im), (_, _, slot) in list(zip(spectra, sources))[start : start + size]:
                    h_re = hat_ref[slot, slab, base : base + half]
                    h_im = hat_ref[slot, slab, base + half : base + 2 * half]
                    add_re = s_re * h_re - s_im * h_im
                    add_im = s_re * h_im + s_im * h_re
                    re = add_re if re is None else re + add_re
                    im = add_im if im is None else im + add_im
                re, im = re.astype(F32), im.astype(F32)
                re_sum = re if re_sum is None else re_sum + re
                im_sum = im if im_sum is None else im_sum + im
            if last:
                y_ref[slab, pair, re_rows] = re_sum.astype(BF16)
                y_ref[slab, pair, im_rows] = im_sum.astype(BF16)
            else:
                out_ref[slab, pair, re_rows] = re_sum
                out_ref[slab, pair, im_rows] = im_sum

    for step in range(steps):
        first = step * (LANES // SLAB)
        for i in range(LANES // SLAB):
            for seg in range(SEGS):
                products(first + i, seg)
        if not last:
            continue
        for pair in range(pairs):
            y = jnp.concatenate([y_ref[first + i, pair] for i in range(LANES // SLAB)], axis=-1)
            if step == 0:
                plain, packed, _ = lane_masks(0, LANES)
                mix = dot(back_ref[0], y * plain.astype(BF16)) + dot(back_ref[1], y * packed.astype(BF16))
            else:
                mix = dot(back_ref[0], y)
            mix = mix.astype(BF16)
            here = slice(step * LANES, (step + 1) * LANES)
            for c in range(2):
                rows_to = slice((2 * pair + c) * blocks, (2 * pair + c + 1) * blocks)
                left_re[rows_to, here] = mix[2 * c * blocks : (2 * c + 1) * blocks]
                left_im[rows_to, here] = mix[(2 * c + 1) * blocks : (2 * c + 2) * blocks]

    if last:
        each = blocks // shares
        for step in range(steps):
            here = slice(step * LANES, (step + 1) * LANES)
            part = dot(left_re[...], two_slabs(inv_ref, step, 0)) + dot(left_im[...], two_slabs(inv_ref, step, 1))
            for t in range(shares):
                for c in range(channels):
                    row = c * blocks + t * each
                    time_ref[t, c, :, here] = part[row : row + each]
        for d in range(shares):
            out_refs[d][...] = time_ref[src_ref[0] ^ d].astype(BF16)


def add_sources(s_list, flips, own, me, hat, total, last, shares, channels, parts):
    slabs = hat.shape[1]
    bins = slabs * SLAB
    frames = parts + SEGS * KEEP
    blocks = frames - parts
    wide = 2 * SEGS * STEPS
    _, inverse = block_tables(bins)
    _, _, back = step_tables(parts, frames, channels)
    vmem = pl.BlockSpec(memory_space=pltpu.VMEM)
    smem = pl.BlockSpec(memory_space=pltpu.SMEM)

    operands = [*me] + list(s_list) + [pltpu.with_memory_space_constraint(hat, pltpu.VMEM)]
    aliases = {}
    if total is not None:
        if not last:
            aliases = {len(operands): 0}
        operands.append(total)
    scratch = []
    if last:
        operands += [jnp.asarray(back), jnp.asarray(inverse)]
        each = blocks // shares
        out_shape = [jax.ShapeDtypeStruct((channels, each, bins), BF16)] * shares
        scratch = [
            pltpu.VMEM((slabs, channels // 2, 2 * wide, SLAB), BF16),
            pltpu.VMEM((channels * blocks, bins), BF16),
            pltpu.VMEM((channels * blocks, bins), BF16),
            pltpu.VMEM((shares, channels, each, bins), F32),
        ]
    else:
        out_shape = jax.ShapeDtypeStruct((slabs, channels // 2, 2 * wide, SLAB), F32)
    body = functools.partial(
        mix_kernel, tuple(flips), own, channels, blocks, shares, total is not None, last
    )
    return pl.pallas_call(
        body,
        in_specs=[smem] * 2 + [vmem] * (len(operands) - 2),
        out_specs=[vmem] * len(out_shape) if last else vmem,
        out_shape=out_shape,
        scratch_shapes=scratch,
        input_output_aliases=aliases,
        compiler_params=pltpu.CompilerParams(vmem_limit_bytes=12 * 2**20),
        cost_estimate=COST,
    )(*operands)


def sum_kernel(count, ch_ref, *refs):
    parts, outs, sum_ref = refs[:count], refs[count:-1], refs[-1]
    total = parts[0][...].astype(F32)
    for part in parts[1:]:
        total = total + part[...].astype(F32)
    sum_ref[...] = total
    for d in range(len(outs)):
        outs[d][...] = sum_ref[:, pl.ds(ch_ref[0] ^ d, 1), :].reshape(outs[d].shape).astype(BF16)


def sum_groups(parts, me):
    channels, each, bins = parts[0].shape
    vmem = pl.BlockSpec(memory_space=pltpu.VMEM)
    return pl.pallas_call(
        functools.partial(sum_kernel, len(parts)),
        in_specs=[pl.BlockSpec(memory_space=pltpu.SMEM)] + [vmem] * len(parts),
        out_specs=[vmem] * each,
        out_shape=[jax.ShapeDtypeStruct((channels, bins), BF16)] * each,
        scratch_shapes=[pltpu.VMEM(parts[0].shape, F32)],
        compiler_params=pltpu.CompilerParams(vmem_limit_bytes=8 * 2**20),
    )(me, *parts)


def decode(signal, matrix):
    decoded = lax.dot_general(
        signal, matrix, (((0,), (0,)), ((), ())), preferred_element_type=F32
    )
    return decoded.astype(BF16)


def per_device(src_count, ch_count, dry_signal, room_spectra, render_slot, decoder):
    rows_total, parts, channels, _, block_len = room_spectra.shape
    own = dry_signal.shape[0]
    frames = dry_signal.shape[1] // block_len
    blocks = frames - parts
    src_me = lax.axis_index("src").astype(jnp.int32)
    ch_me = lax.axis_index("ch").astype(jnp.int32)

    if own == 1:
        x_own = dry_signal.reshape(frames, block_len)
    else:
        x_own = dry_signal.reshape(own, frames, block_len).transpose(1, 0, 2)

    def swap(value, axis, count, flip):
        return lax.ppermute(value, axis, [(i, i ^ flip) for i in range(count)])

    chips = ch_count // 2
    first = chips // 2
    far = [first] + [d for d in range(chips - 1, 0, -1) if d != first]
    mate = swap(x_own, "ch", ch_count, 1)
    lanes = {d: swap(x_own, "ch", ch_count, 2 * d) for d in far}
    me = (src_me[None], ch_me[None])
    hat = transform_responses(room_spectra, me, render_slot)

    row = jnp.arange(ch_count * channels, dtype=jnp.int32)
    chip_order = [0] + list(range(chips - 2, 0, -1)) + [chips - 1]
    flips = np.array([2 * d + core for d in chip_order for core in range(2)], dtype=np.int32)
    takes = (jnp.asarray(np.repeat(flips, channels)) ^ ch_me) * channels + row % channels
    order = (takes[:, None] == row[None, :]).astype(BF16)
    own_order = lax.optimization_barrier(dot(order, decoder).astype(BF16))

    def add(s_list, flips, total, last):
        return add_sources(
            s_list, flips, own, me, hat, total, last, src_count, channels, parts
        )

    x_near, hat = lax.optimization_barrier((x_own, hat))
    near = transform_signals([x_near, mate], own, block_len, parts)
    total = add([near], [[0, 1]], None, False)
    *late, total = lax.optimization_barrier((*[lanes[d] for d in far], total))
    mine = transform_signals(late, own, block_len, parts)
    given = swap(mine, "ch", ch_count, 1)
    total = add([mine], [[2 * d for d in far]], total, False)
    total = add([given], [[2 * d + 1 for d in far]], total, True)

    sums = [total[0]] + [swap(total[d], "src", src_count, d) for d in range(1, src_count)]
    if blocks == src_count * ch_count:
        pieces = sum_groups(sums, ch_me[None])
        given = swap(jnp.concatenate(pieces[1::2], axis=0), "ch", ch_count, 1)
        both = {
            d: jnp.concatenate([pieces[2 * d], given[d * channels : (d + 1) * channels]], axis=0)
            for d in chip_order
        }
        if chips == 4:
            size = 2 * channels
            two = swap(jnp.concatenate([both[2], both[3]], axis=0), "ch", ch_count, 4)
            one = swap(jnp.concatenate([both[1], two[size:]], axis=0), "ch", ch_count, 2)
            arrived = [both[0], two[:size], one]
        else:
            arrived = [both[0]] + [swap(both[d], "ch", ch_count, 2 * d) for d in chip_order[1:]]
        return decode(jnp.concatenate(arrived, axis=0), own_order)
    signal = sums[0].astype(F32)
    for part in sums[1:]:
        signal = signal + part.astype(F32)
    signal = signal.astype(BF16).reshape(channels, -1)
    return decode(lax.all_to_all(signal, "ch", split_axis=1, concat_axis=0, tiled=True), decoder)


def solution(mesh):
    body = functools.partial(per_device, mesh.shape["src"], mesh.shape["ch"])
    return jax.shard_map(
        body,
        mesh=mesh,
        in_specs=(P(("src", "ch"), None), P("src", None, "ch", None, None), P("src"), P()),
        out_specs=P(("src", "ch"), None),
        check_vma=False,
    )
```

```python
import functools
import math

import jax
import jax.numpy as jnp
import ml_dtypes
import numpy as np
from jax import lax
from jax.experimental import pallas as pl
from jax.experimental.pallas import tpu as pltpu
from jax.sharding import PartitionSpec as P

BF16 = jnp.bfloat16
F32 = jnp.float32
LANES = 256
SLAB = 128
GROUP = 4
COST = pl.CostEstimate(flops=2**20, bytes_accessed=2**16, transcendentals=0)
ROWS = 4
STEPS = 24
SEGS = 2
KEEP = 16


def bf16_table(values):
    return np.asarray(values, dtype=np.float32).astype(ml_dtypes.bfloat16)


@functools.lru_cache(maxsize=None)
def block_tables(block_len):
    size = 2 * block_len
    n = np.arange(block_len)[:, None]
    k = np.arange(block_len)[None, :]
    angle = ((n * k) % size) * (2.0 * math.pi / size)
    fwd_real = np.cos(angle)
    fwd_imag = np.where(k == 0, 1.0 - 2.0 * (n % 2), -np.sin(angle))
    kk = np.arange(block_len)[:, None]
    m = np.arange(block_len)[None, :] + block_len
    angle = ((kk * m) % size) * (2.0 * math.pi / size)
    weight = np.where(kk == 0, 1.0, 2.0)
    inv_real = weight * np.cos(angle) / size
    inv_imag = np.where(kk == 0, (1.0 - 2.0 * (m % 2)) / size, -2.0 * np.sin(angle) / size)
    def slabs(pair):
        return bf16_table(np.stack(pair).reshape(2, block_len, -1, SLAB).transpose(0, 2, 1, 3))

    return slabs([fwd_real, fwd_imag]), slabs([inv_real, inv_imag])


@functools.lru_cache(maxsize=None)
def step_tables(parts, frames, channels, own=1):
    half = STEPS // 2
    theta = 2.0 * math.pi * (np.arange(STEPS) + 0.5) / STEPS
    first = (np.arange(STEPS) < half).astype(np.float64)[:, None]

    def forward(steps):
        cos = np.cos(theta[:, None] * steps[None, :])
        sin = np.sin(theta[:, None] * steps[None, :])
        plain = np.block([[cos, sin], [-sin, cos]])
        packed = np.block([[cos * first, cos * (1 - first)], [-sin * first, -sin * (1 - first)]])
        return plain, packed

    spec = np.zeros((2, SEGS, 2, STEPS, 2, frames))
    used = parts - 1 + KEEP
    for kind, table in enumerate(forward(np.arange(used))):
        table = table.reshape(2, STEPS, 2, used)
        for seg in range(SEGS):
            spec[kind, seg, :, :, :, seg * KEEP : seg * KEEP + used] = table
    spec = spec.reshape(2, 1, SEGS * 2 * STEPS, 2 * frames, 1) * np.eye(own)[None, :, None, None, :]
    spec = spec.reshape(2, own * SEGS * 2 * STEPS, 2 * frames * own)

    resp = np.zeros((channels // 2, 2, 2, STEPS, 2, parts, channels, 2))
    for kind, table in enumerate(forward(np.arange(parts))):
        table = table.reshape(2, STEPS, 2, parts).transpose(0, 1, 3, 2)
        for c in range(channels):
            resp[c // 2, :, c % 2, :, kind, :, c] = table
    resp = resp.reshape(channels * 2 * STEPS, 2 * parts * channels * 2)

    back = np.zeros((2, 2, 2, SEGS, KEEP, SEGS, 2, 2, STEPS))
    steps = np.arange(KEEP) + parts - 1
    cos = np.cos(theta[None, :] * steps[:, None]) / STEPS
    sin = np.sin(theta[None, :] * steps[:, None]) / STEPS
    firsts = first[:, 0][None, :]
    for seg in range(SEGS):
        for c in range(2):
            back[0, c, 0, seg, :, seg, 0, c] = cos
            back[0, c, 0, seg, :, seg, 1, c] = -sin
            back[0, c, 1, seg, :, seg, 0, c] = sin
            back[0, c, 1, seg, :, seg, 1, c] = cos
            back[1, c, 0, seg, :, seg, 0, c] = 2 * cos * firsts
            back[1, c, 0, seg, :, seg, 1, c] = -2 * sin * firsts
            back[1, c, 1, seg, :, seg, 0, c] = 2 * cos * (1 - firsts)
            back[1, c, 1, seg, :, seg, 1, c] = -2 * sin * (1 - firsts)
    back = back.reshape(2, 4 * SEGS * KEEP, 4 * SEGS * STEPS)
    return bf16_table(spec), bf16_table(resp), bf16_table(back)


def dot(left, right):
    return jnp.dot(left, right, preferred_element_type=F32)


def lane_masks(start, width):
    lane = lax.broadcasted_iota(jnp.int32, (1, width), 1) + start
    packed = (lane == 0).astype(F32)
    sign = (1 - 2 * (lane % 2)).astype(F32)
    return 1.0 - packed, packed, sign


def two_slabs(ref, step, *index):
    first = step * (LANES // SLAB)
    return jnp.concatenate([ref[(*index, first + i)] for i in range(LANES // SLAB)], axis=-1)


def response_kernel(rows, bins, src_ref, ch_ref, slot_ref, room_hbm, table_hbm, hat_ref, room_ref, table_ref, sems):
    depth = room_ref.shape[1] * room_ref.shape[2] * 2
    flat = room_ref.reshape(rows, depth, bins)
    plain, packed, _ = lane_masks(0, LANES)
    plain, packed = plain.astype(BF16), packed.astype(BF16)

    def copy(r):
        row = lax.rem(slot_ref[r], rows)
        return pltpu.make_async_copy(room_hbm.at[row], room_ref.at[r], sems.at[r])

    table_copy = pltpu.make_async_copy(table_hbm, table_ref, sems.at[rows])
    table_copy.start()
    for r in range(rows):
        copy(r).start()
    table_copy.wait()

    def some(outer, carry):
        for inner in range(ROWS):
            copy(outer * ROWS + inner).wait()
        for inner in range(ROWS):
            r = outer * ROWS + inner
            for step in range(bins // LANES):
                h = flat[r, :, step * LANES : (step + 1) * LANES]
                if step == 0:
                    h = jnp.concatenate([h * plain, h * packed], axis=0)
                    hat = dot(table_ref[...], h)
                else:
                    hat = dot(table_ref[:, :depth], h)
                hat = hat.astype(BF16)
                for i in range(LANES // SLAB):
                    hat_ref[r, step * (LANES // SLAB) + i] = hat[:, i * SLAB : (i + 1) * SLAB]
        return carry

    lax.fori_loop(0, rows // ROWS, some, 0)


def transform_responses(room, me, slots):
    rows, parts, channels, _, bins = room.shape
    slabs = bins // SLAB
    _, resp, _ = step_tables(parts, parts + SEGS * KEEP, channels)
    hbm = pl.BlockSpec(memory_space=pltpu.HBM)
    return pl.pallas_call(
        functools.partial(response_kernel, rows, bins),
        in_specs=[pl.BlockSpec(memory_space=pltpu.SMEM)] * 3 + [hbm, hbm],
        out_specs=pl.BlockSpec(memory_space=pltpu.VMEM),
        out_shape=pltpu.VMEM((rows, slabs, channels * 2 * STEPS, SLAB), BF16),
        scratch_shapes=[
            pltpu.VMEM(room.shape, BF16),
            pltpu.VMEM(resp.shape, BF16),
            pltpu.SemaphoreType.DMA((rows + 1,)),
        ],
        compiler_params=pltpu.CompilerParams(vmem_limit_bytes=8 * 2**20),
        cost_estimate=COST,
    )(
        *me,
        slots,
        pltpu.with_memory_space_constraint(room, pltpu.HBM),
        pltpu.with_memory_space_constraint(jnp.asarray(resp), pltpu.HBM),
    )


def spectra_kernel(pieces, rows, *refs):
    x_refs, (table_ref, spec_ref, out_ref) = refs[:pieces], refs[pieces:]
    slabs = table_ref.shape[1]
    wide = 2 * SEGS * STEPS
    own = rows // pieces
    span = x_refs[0].shape[0] * own
    flat = x_refs if own == 1 else [ref.reshape(span, slabs * SLAB) for ref in x_refs]
    x = jnp.concatenate([ref[...] for ref in flat], axis=0)
    for step in range(slabs * SLAB // LANES):
        plain, packed, sign = lane_masks(step * LANES, LANES)
        spectra = []
        for j in range(2):
            one = dot(x, two_slabs(table_ref, step, j))
            spectra.append(one + sign * pltpu.roll(one, one.shape[0] - own, axis=0))
        for piece in range(pieces):
            both = [s[piece * span : (piece + 1) * span] for s in spectra]
            both = jnp.concatenate(both, axis=0)
            if step == 0:
                hat = dot(spec_ref[0], (both * plain).astype(BF16)) + dot(spec_ref[1], (both * packed).astype(BF16))
            else:
                hat = dot(spec_ref[0], both.astype(BF16))
            hat = hat.astype(BF16)
            for k in range(own):
                for i in range(LANES // SLAB):
                    at = slice(i * SLAB, (i + 1) * SLAB)
                    out_ref[step * (LANES // SLAB) + i, piece * own + k] = hat[k * wide : (k + 1) * wide, at]


def transform_signals(x_list, own, bins, parts):
    frames = parts + SEGS * KEEP
    rows = own * len(x_list)
    slabs = bins // SLAB
    table, _ = block_tables(bins)
    spec, _, _ = step_tables(parts, frames, 2, own)
    vmem = pl.BlockSpec(memory_space=pltpu.VMEM)
    operands = [*x_list, jnp.asarray(table), jnp.asarray(spec)]
    return pl.pallas_call(
        functools.partial(spectra_kernel, len(x_list), rows),
        in_specs=[vmem] * len(operands),
        out_specs=vmem,
        out_shape=jax.ShapeDtypeStruct((slabs, rows, 2 * SEGS * STEPS, SLAB), BF16),
        compiler_params=pltpu.CompilerParams(vmem_limit_bytes=8 * 2**20),
        cost_estimate=COST,
    )(*operands)


def mix_kernel(flips, own, channels, blocks, shares, has_total, last, src_ref, ch_ref, *refs):
    refs = list(refs)
    s_refs = [refs.pop(0) for _ in flips]
    hat_ref = refs.pop(0)
    total_ref = refs.pop(0) if has_total else None
    if last:
        back_ref, inv_ref = refs.pop(0), refs.pop(0)
        out_refs = [refs.pop(0) for _ in range(shares)]
        y_ref, left_re, left_im, time_ref = refs
    else:
        (out_ref,) = refs

    slabs = hat_ref.shape[1]
    steps = slabs * SLAB // LANES
    half = 2 * STEPS
    pairs = channels // 2
    sources = []
    for ref, some in zip(s_refs, flips):
        for k, flip in enumerate(some):
            for i in range(own):
                sources.append((ref, k * own + i, (ch_ref[0] ^ flip) * own + i))
    groups = -(-len(sources) // GROUP)
    size = -(-len(sources) // groups)

    def twice(rows):
        rows = rows.astype(F32)
        return jnp.concatenate([rows, rows], axis=0).astype(BF16)

    def products(slab, seg):
        re_in = slice(2 * seg * STEPS, (2 * seg + 1) * STEPS)
        im_in = slice((2 * seg + 1) * STEPS, (2 * seg + 2) * STEPS)
        re_rows = slice(2 * seg * half, (2 * seg + 1) * half)
        im_rows = slice((2 * seg + 1) * half, (2 * seg + 2) * half)
        spectra = [(twice(ref[slab, r, re_in]), twice(ref[slab, r, im_in])) for ref, r, _ in sources]
        for pair in range(pairs):
            base = pair * 2 * half
            re_sum = total_ref[slab, pair, re_rows] if has_total else None
            im_sum = total_ref[slab, pair, im_rows] if has_total else None
            for start in range(0, len(sources), size):
                re, im = None, None
                for (s_re, s_im), (_, _, slot) in list(zip(spectra, sources))[start : start + size]:
                    h_re = hat_ref[slot, slab, base : base + half]
                    h_im = hat_ref[slot, slab, base + half : base + 2 * half]
                    add_re = s_re * h_re - s_im * h_im
                    add_im = s_re * h_im + s_im * h_re
                    re = add_re if re is None else re + add_re
                    im = add_im if im is None else im + add_im
                re, im = re.astype(F32), im.astype(F32)
                re_sum = re if re_sum is None else re_sum + re
                im_sum = im if im_sum is None else im_sum + im
            if last:
                y_ref[slab, pair, re_rows] = re_sum.astype(BF16)
                y_ref[slab, pair, im_rows] = im_sum.astype(BF16)
            else:
                out_ref[slab, pair, re_rows] = re_sum
                out_ref[slab, pair, im_rows] = im_sum

    for step in range(steps):
        first = step * (LANES // SLAB)
        for i in range(LANES // SLAB):
            for seg in range(SEGS):
                products(first + i, seg)
        if not last:
            continue
        for pair in range(pairs):
            y = jnp.concatenate([y_ref[first + i, pair] for i in range(LANES // SLAB)], axis=-1)
            if step == 0:
                plain, packed, _ = lane_masks(0, LANES)
                mix = dot(back_ref[0], y * plain.astype(BF16)) + dot(back_ref[1], y * packed.astype(BF16))
            else:
                mix = dot(back_ref[0], y)
            mix = mix.astype(BF16)
            here = slice(step * LANES, (step + 1) * LANES)
            for c in range(2):
                rows_to = slice((2 * pair + c) * blocks, (2 * pair + c + 1) * blocks)
                left_re[rows_to, here] = mix[2 * c * blocks : (2 * c + 1) * blocks]
                left_im[rows_to, here] = mix[(2 * c + 1) * blocks : (2 * c + 2) * blocks]

    if last:
        each = blocks // shares
        for step in range(steps):
            here = slice(step * LANES, (step + 1) * LANES)
            part = dot(left_re[...], two_slabs(inv_ref, step, 0)) + dot(left_im[...], two_slabs(inv_ref, step, 1))
            for t in range(shares):
                for c in range(channels):
                    row = c * blocks + t * each
                    time_ref[t, c, :, here] = part[row : row + each]
        for d in range(shares):
            out_refs[d][...] = time_ref[src_ref[0] ^ d].astype(BF16)


def add_sources(s_list, flips, own, me, hat, total, last, shares, channels, parts):
    slabs = hat.shape[1]
    bins = slabs * SLAB
    frames = parts + SEGS * KEEP
    blocks = frames - parts
    wide = 2 * SEGS * STEPS
    _, inverse = block_tables(bins)
    _, _, back = step_tables(parts, frames, channels)
    vmem = pl.BlockSpec(memory_space=pltpu.VMEM)
    smem = pl.BlockSpec(memory_space=pltpu.SMEM)

    operands = [*me] + list(s_list) + [pltpu.with_memory_space_constraint(hat, pltpu.VMEM)]
    aliases = {}
    if total is not None:
        if not last:
            aliases = {len(operands): 0}
        operands.append(total)
    scratch = []
    if last:
        operands += [jnp.asarray(back), jnp.asarray(inverse)]
        each = blocks // shares
        out_shape = [jax.ShapeDtypeStruct((channels, each, bins), BF16)] * shares
        scratch = [
            pltpu.VMEM((slabs, channels // 2, 2 * wide, SLAB), BF16),
            pltpu.VMEM((channels * blocks, bins), BF16),
            pltpu.VMEM((channels * blocks, bins), BF16),
            pltpu.VMEM((shares, channels, each, bins), F32),
        ]
    else:
        out_shape = jax.ShapeDtypeStruct((slabs, channels // 2, 2 * wide, SLAB), F32)
    body = functools.partial(
        mix_kernel, tuple(flips), own, channels, blocks, shares, total is not None, last
    )
    return pl.pallas_call(
        body,
        in_specs=[smem] * 2 + [vmem] * (len(operands) - 2),
        out_specs=[vmem] * len(out_shape) if last else vmem,
        out_shape=out_shape,
        scratch_shapes=scratch,
        input_output_aliases=aliases,
        compiler_params=pltpu.CompilerParams(vmem_limit_bytes=12 * 2**20),
        cost_estimate=COST,
    )(*operands)


def sum_kernel(count, ch_ref, *refs):
    parts, outs, sum_ref = refs[:count], refs[count:-1], refs[-1]
    total = parts[0][...].astype(F32)
    for part in parts[1:]:
        total = total + part[...].astype(F32)
    sum_ref[...] = total
    for d in range(len(outs)):
        outs[d][...] = sum_ref[:, pl.ds(ch_ref[0] ^ d, 1), :].reshape(outs[d].shape).astype(BF16)


def sum_groups(parts, me):
    channels, each, bins = parts[0].shape
    vmem = pl.BlockSpec(memory_space=pltpu.VMEM)
    return pl.pallas_call(
        functools.partial(sum_kernel, len(parts)),
        in_specs=[pl.BlockSpec(memory_space=pltpu.SMEM)] + [vmem] * len(parts),
        out_specs=[vmem] * each,
        out_shape=[jax.ShapeDtypeStruct((channels, bins), BF16)] * each,
        scratch_shapes=[pltpu.VMEM(parts[0].shape, F32)],
        compiler_params=pltpu.CompilerParams(vmem_limit_bytes=8 * 2**20),
    )(me, *parts)


def decode(signal, matrix):
    decoded = lax.dot_general(
        signal, matrix, (((0,), (0,)), ((), ())), preferred_element_type=F32
    )
    return decoded.astype(BF16)


def per_device(src_count, ch_count, dry_signal, room_spectra, render_slot, decoder):
    rows_total, parts, channels, _, block_len = room_spectra.shape
    own = dry_signal.shape[0]
    frames = dry_signal.shape[1] // block_len
    blocks = frames - parts
    src_me = lax.axis_index("src").astype(jnp.int32)
    ch_me = lax.axis_index("ch").astype(jnp.int32)

    if own == 1:
        x_own = dry_signal.reshape(frames, block_len)
    else:
        x_own = dry_signal.reshape(own, frames, block_len).transpose(1, 0, 2)

    def swap(value, axis, count, flip):
        return lax.ppermute(value, axis, [(i, i ^ flip) for i in range(count)])

    chips = ch_count // 2
    first = chips // 2
    far = list(range(1, chips))
    mate = swap(x_own, "ch", ch_count, 1)
    lanes = {d: swap(x_own, "ch", ch_count, 2 * d) for d in far}
    me = (src_me[None], ch_me[None])
    hat = transform_responses(room_spectra, me, render_slot)

    row = jnp.arange(ch_count * channels, dtype=jnp.int32)
    chip_order = [0] + list(range(chips - 2, 0, -1)) + [chips - 1]
    flips = np.array([2 * d + core for d in chip_order for core in range(2)], dtype=np.int32)
    takes = (jnp.asarray(np.repeat(flips, channels)) ^ ch_me) * channels + row % channels
    order = (takes[:, None] == row[None, :]).astype(BF16)
    own_order = lax.optimization_barrier(dot(order, decoder).astype(BF16))

    def add(s_list, flips, total, last):
        return add_sources(
            s_list, flips, own, me, hat, total, last, src_count, channels, parts
        )

    x_near, hat = lax.optimization_barrier((x_own, hat))
    near = transform_signals([x_near, mate], own, block_len, parts)
    total = add([near], [[0, 1]], None, False)
    *late, total = lax.optimization_barrier((*[lanes[d] for d in far], total))
    mine = transform_signals(late, own, block_len, parts)
    given = swap(mine, "ch", ch_count, 1)
    total = add([mine], [[2 * d for d in far]], total, False)
    total = add([given], [[2 * d + 1 for d in far]], total, True)

    sums = [total[0]] + [swap(total[d], "src", src_count, d) for d in range(1, src_count)]
    if blocks == src_count * ch_count:
        pieces = sum_groups(sums, ch_me[None])
        given = swap(jnp.concatenate(pieces[1::2], axis=0), "ch", ch_count, 1)
        both = {
            d: jnp.concatenate([pieces[2 * d], given[d * channels : (d + 1) * channels]], axis=0)
            for d in chip_order
        }
        arrived = [both[0]] + [swap(both[d], "ch", ch_count, 2 * d) for d in chip_order[1:]]
        return decode(jnp.concatenate(arrived, axis=0), own_order)
    signal = sums[0].astype(F32)
    for part in sums[1:]:
        signal = signal + part.astype(F32)
    signal = signal.astype(BF16).reshape(channels, -1)
    return decode(lax.all_to_all(signal, "ch", split_axis=1, concat_axis=0, tiled=True), decoder)


def solution(mesh):
    body = functools.partial(per_device, mesh.shape["src"], mesh.shape["ch"])
    return jax.shard_map(
        body,
        mesh=mesh,
        in_specs=(P(("src", "ch"), None), P("src", None, "ch", None, None), P("src"), P()),
        out_specs=P(("src", "ch"), None),
        check_vma=False,
    )
```

```python
import functools
import math

import jax
import jax.numpy as jnp
import ml_dtypes
import numpy as np
from jax import lax
from jax.experimental import pallas as pl
from jax.experimental.pallas import tpu as pltpu
from jax.sharding import PartitionSpec as P

BF16 = jnp.bfloat16
F32 = jnp.float32
LANES = 256
SLAB = 128
GROUP = 4
COST = pl.CostEstimate(flops=2**20, bytes_accessed=2**16, transcendentals=0)
ROWS = 4
STEPS = 24
SEGS = 2
KEEP = 16


def bf16_table(values):
    return np.asarray(values, dtype=np.float32).astype(ml_dtypes.bfloat16)


@functools.lru_cache(maxsize=None)
def block_tables(block_len):
    size = 2 * block_len
    n = np.arange(block_len)[:, None]
    k = np.arange(block_len)[None, :]
    angle = ((n * k) % size) * (2.0 * math.pi / size)
    fwd_real = np.cos(angle)
    fwd_imag = np.where(k == 0, 1.0 - 2.0 * (n % 2), -np.sin(angle))
    kk = np.arange(block_len)[:, None]
    m = np.arange(block_len)[None, :] + block_len
    angle = ((kk * m) % size) * (2.0 * math.pi / size)
    weight = np.where(kk == 0, 1.0, 2.0)
    inv_real = weight * np.cos(angle) / size
    inv_imag = np.where(kk == 0, (1.0 - 2.0 * (m % 2)) / size, -2.0 * np.sin(angle) / size)
    def slabs(pair):
        return bf16_table(np.stack(pair).reshape(2, block_len, -1, SLAB).transpose(0, 2, 1, 3))

    return slabs([fwd_real, fwd_imag]), slabs([inv_real, inv_imag])


@functools.lru_cache(maxsize=None)
def step_tables(parts, frames, channels, own=1):
    half = STEPS // 2
    theta = 2.0 * math.pi * (np.arange(STEPS) + 0.5) / STEPS
    first = (np.arange(STEPS) < half).astype(np.float64)[:, None]

    def forward(steps):
        cos = np.cos(theta[:, None] * steps[None, :])
        sin = np.sin(theta[:, None] * steps[None, :])
        plain = np.block([[cos, sin], [-sin, cos]])
        packed = np.block([[cos * first, cos * (1 - first)], [-sin * first, -sin * (1 - first)]])
        return plain, packed

    spec = np.zeros((2, SEGS, 2, STEPS, 2, frames))
    used = parts - 1 + KEEP
    for kind, table in enumerate(forward(np.arange(used))):
        table = table.reshape(2, STEPS, 2, used)
        for seg in range(SEGS):
            spec[kind, seg, :, :, :, seg * KEEP : seg * KEEP + used] = table
    spec = spec.reshape(2, 1, SEGS * 2 * STEPS, 2 * frames, 1) * np.eye(own)[None, :, None, None, :]
    spec = spec.reshape(2, own * SEGS * 2 * STEPS, 2 * frames * own)

    resp = np.zeros((channels // 2, 2, 2, STEPS, 2, parts, channels, 2))
    for kind, table in enumerate(forward(np.arange(parts))):
        table = table.reshape(2, STEPS, 2, parts).transpose(0, 1, 3, 2)
        for c in range(channels):
            resp[c // 2, :, c % 2, :, kind, :, c] = table
    resp = resp.reshape(channels * 2 * STEPS, 2 * parts * channels * 2)

    back = np.zeros((2, 2, 2, SEGS, KEEP, SEGS, 2, 2, STEPS))
    steps = np.arange(KEEP) + parts - 1
    cos = np.cos(theta[None, :] * steps[:, None]) / STEPS
    sin = np.sin(theta[None, :] * steps[:, None]) / STEPS
    firsts = first[:, 0][None, :]
    for seg in range(SEGS):
        for c in range(2):
            back[0, c, 0, seg, :, seg, 0, c] = cos
            back[0, c, 0, seg, :, seg, 1, c] = -sin
            back[0, c, 1, seg, :, seg, 0, c] = sin
            back[0, c, 1, seg, :, seg, 1, c] = cos
            back[1, c, 0, seg, :, seg, 0, c] = 2 * cos * firsts
            back[1, c, 0, seg, :, seg, 1, c] = -2 * sin * firsts
            back[1, c, 1, seg, :, seg, 0, c] = 2 * cos * (1 - firsts)
            back[1, c, 1, seg, :, seg, 1, c] = -2 * sin * (1 - firsts)
    back = back.reshape(2, 4 * SEGS * KEEP, 4 * SEGS * STEPS)
    return bf16_table(spec), bf16_table(resp), bf16_table(back)


def dot(left, right):
    return jnp.dot(left, right, preferred_element_type=F32)


def lane_masks(start, width):
    lane = lax.broadcasted_iota(jnp.int32, (1, width), 1) + start
    packed = (lane == 0).astype(F32)
    sign = (1 - 2 * (lane % 2)).astype(F32)
    return 1.0 - packed, packed, sign


def two_slabs(ref, step, *index):
    first = step * (LANES // SLAB)
    return jnp.concatenate([ref[(*index, first + i)] for i in range(LANES // SLAB)], axis=-1)


def response_kernel(rows, bins, src_ref, ch_ref, slot_ref, room_hbm, table_hbm, hat_ref, room_ref, table_ref, sems):
    depth = room_ref.shape[1] * room_ref.shape[2] * 2
    flat = room_ref.reshape(rows, depth, bins)
    plain, packed, _ = lane_masks(0, LANES)
    plain, packed = plain.astype(BF16), packed.astype(BF16)

    def copy(r):
        row = lax.rem(slot_ref[r], rows)
        return pltpu.make_async_copy(room_hbm.at[row], room_ref.at[r], sems.at[r])

    table_copy = pltpu.make_async_copy(table_hbm, table_ref, sems.at[rows])
    table_copy.start()
    for r in range(rows):
        copy(r).start()
    table_copy.wait()

    def some(outer, carry):
        for inner in range(ROWS):
            copy(outer * ROWS + inner).wait()
        for inner in range(ROWS):
            r = outer * ROWS + inner
            for step in range(bins // LANES):
                h = flat[r, :, step * LANES : (step + 1) * LANES]
                if step == 0:
                    h = jnp.concatenate([h * plain, h * packed], axis=0)
                    hat = dot(table_ref[...], h)
                else:
                    hat = dot(table_ref[:, :depth], h)
                hat = hat.astype(BF16)
                for i in range(LANES // SLAB):
                    hat_ref[r, step * (LANES // SLAB) + i] = hat[:, i * SLAB : (i + 1) * SLAB]
        return carry

    lax.fori_loop(0, rows // ROWS, some, 0)


def transform_responses(room, me, slots):
    rows, parts, channels, _, bins = room.shape
    slabs = bins // SLAB
    _, resp, _ = step_tables(parts, parts + SEGS * KEEP, channels)
    hbm = pl.BlockSpec(memory_space=pltpu.HBM)
    return pl.pallas_call(
        functools.partial(response_kernel, rows, bins),
        in_specs=[pl.BlockSpec(memory_space=pltpu.SMEM)] * 3 + [hbm, hbm],
        out_specs=pl.BlockSpec(memory_space=pltpu.VMEM),
        out_shape=pltpu.VMEM((rows, slabs, channels * 2 * STEPS, SLAB), BF16),
        scratch_shapes=[
            pltpu.VMEM(room.shape, BF16),
            pltpu.VMEM(resp.shape, BF16),
            pltpu.SemaphoreType.DMA((rows + 1,)),
        ],
        compiler_params=pltpu.CompilerParams(vmem_limit_bytes=8 * 2**20),
        cost_estimate=COST,
    )(
        *me,
        slots,
        pltpu.with_memory_space_constraint(room, pltpu.HBM),
        pltpu.with_memory_space_constraint(jnp.asarray(resp), pltpu.HBM),
    )


def spectra_kernel(pieces, rows, *refs):
    x_refs, (table_ref, spec_ref, out_ref) = refs[:pieces], refs[pieces:]
    slabs = table_ref.shape[1]
    wide = 2 * SEGS * STEPS
    own = rows // pieces
    span = x_refs[0].shape[0] * own
    flat = x_refs if own == 1 else [ref.reshape(span, slabs * SLAB) for ref in x_refs]
    x = jnp.concatenate([ref[...] for ref in flat], axis=0)
    for step in range(slabs * SLAB // LANES):
        plain, packed, sign = lane_masks(step * LANES, LANES)
        spectra = []
        for j in range(2):
            one = dot(x, two_slabs(table_ref, step, j))
            spectra.append(one + sign * pltpu.roll(one, one.shape[0] - own, axis=0))
        for piece in range(pieces):
            both = [s[piece * span : (piece + 1) * span] for s in spectra]
            both = jnp.concatenate(both, axis=0)
            if step == 0:
                hat = dot(spec_ref[0], (both * plain).astype(BF16)) + dot(spec_ref[1], (both * packed).astype(BF16))
            else:
                hat = dot(spec_ref[0], both.astype(BF16))
            hat = hat.astype(BF16)
            for k in range(own):
                for i in range(LANES // SLAB):
                    at = slice(i * SLAB, (i + 1) * SLAB)
                    out_ref[step * (LANES // SLAB) + i, piece * own + k] = hat[k * wide : (k + 1) * wide, at]


def transform_signals(x_list, own, bins, parts):
    frames = parts + SEGS * KEEP
    rows = own * len(x_list)
    slabs = bins // SLAB
    table, _ = block_tables(bins)
    spec, _, _ = step_tables(parts, frames, 2, own)
    vmem = pl.BlockSpec(memory_space=pltpu.VMEM)
    operands = [*x_list, jnp.asarray(table), jnp.asarray(spec)]
    return pl.pallas_call(
        functools.partial(spectra_kernel, len(x_list), rows),
        in_specs=[vmem] * len(operands),
        out_specs=vmem,
        out_shape=jax.ShapeDtypeStruct((slabs, rows, 2 * SEGS * STEPS, SLAB), BF16),
        compiler_params=pltpu.CompilerParams(vmem_limit_bytes=8 * 2**20),
        cost_estimate=COST,
    )(*operands)


def mix_kernel(flips, own, channels, blocks, shares, has_total, last, src_ref, ch_ref, *refs):
    refs = list(refs)
    s_refs = [refs.pop(0) for _ in flips]
    hat_ref = refs.pop(0)
    total_ref = refs.pop(0) if has_total else None
    if last:
        back_ref, inv_ref = refs.pop(0), refs.pop(0)
        out_refs = [refs.pop(0) for _ in range(shares)]
        y_ref, left_re, left_im, time_ref = refs
    else:
        (out_ref,) = refs

    slabs = hat_ref.shape[1]
    steps = slabs * SLAB // LANES
    half = 2 * STEPS
    pairs = channels // 2
    sources = []
    for ref, some in zip(s_refs, flips):
        for k, flip in enumerate(some):
            for i in range(own):
                sources.append((ref, k * own + i, (ch_ref[0] ^ flip) * own + i))
    groups = -(-len(sources) // GROUP)
    size = -(-len(sources) // groups)

    def twice(rows):
        rows = rows.astype(F32)
        return jnp.concatenate([rows, rows], axis=0).astype(BF16)

    def products(slab, seg):
        re_in = slice(2 * seg * STEPS, (2 * seg + 1) * STEPS)
        im_in = slice((2 * seg + 1) * STEPS, (2 * seg + 2) * STEPS)
        re_rows = slice(2 * seg * half, (2 * seg + 1) * half)
        im_rows = slice((2 * seg + 1) * half, (2 * seg + 2) * half)
        spectra = [(twice(ref[slab, r, re_in]), twice(ref[slab, r, im_in])) for ref, r, _ in sources]
        for pair in range(pairs):
            base = pair * 2 * half
            re_sum = total_ref[slab, pair, re_rows] if has_total else None
            im_sum = total_ref[slab, pair, im_rows] if has_total else None
            for start in range(0, len(sources), size):
                re, im = None, None
                for (s_re, s_im), (_, _, slot) in list(zip(spectra, sources))[start : start + size]:
                    h_re = hat_ref[slot, slab, base : base + half]
                    h_im = hat_ref[slot, slab, base + half : base + 2 * half]
                    add_re = s_re * h_re - s_im * h_im
                    add_im = s_re * h_im + s_im * h_re
                    re = add_re if re is None else re + add_re
                    im = add_im if im is None else im + add_im
                re, im = re.astype(F32), im.astype(F32)
                re_sum = re if re_sum is None else re_sum + re
                im_sum = im if im_sum is None else im_sum + im
            if last:
                y_ref[slab, pair, re_rows] = re_sum.astype(BF16)
                y_ref[slab, pair, im_rows] = im_sum.astype(BF16)
            else:
                out_ref[slab, pair, re_rows] = re_sum
                out_ref[slab, pair, im_rows] = im_sum

    for step in range(steps):
        first = step * (LANES // SLAB)
        for i in range(LANES // SLAB):
            for seg in range(SEGS):
                products(first + i, seg)
        if not last:
            continue
        for pair in range(pairs):
            y = jnp.concatenate([y_ref[first + i, pair] for i in range(LANES // SLAB)], axis=-1)
            if step == 0:
                plain, packed, _ = lane_masks(0, LANES)
                mix = dot(back_ref[0], y * plain.astype(BF16)) + dot(back_ref[1], y * packed.astype(BF16))
            else:
                mix = dot(back_ref[0], y)
            mix = mix.astype(BF16)
            here = slice(step * LANES, (step + 1) * LANES)
            for c in range(2):
                rows_to = slice((2 * pair + c) * blocks, (2 * pair + c + 1) * blocks)
                left_re[rows_to, here] = mix[2 * c * blocks : (2 * c + 1) * blocks]
                left_im[rows_to, here] = mix[(2 * c + 1) * blocks : (2 * c + 2) * blocks]

    if last:
        each = blocks // shares
        for step in range(steps):
            here = slice(step * LANES, (step + 1) * LANES)
            part = dot(left_re[...], two_slabs(inv_ref, step, 0)) + dot(left_im[...], two_slabs(inv_ref, step, 1))
            for t in range(shares):
                for c in range(channels):
                    row = c * blocks + t * each
                    time_ref[t, c, :, here] = part[row : row + each]
        for d in range(shares):
            out_refs[d][...] = time_ref[src_ref[0] ^ d].astype(BF16)


def add_sources(s_list, flips, own, me, hat, total, last, shares, channels, parts):
    slabs = hat.shape[1]
    bins = slabs * SLAB
    frames = parts + SEGS * KEEP
    blocks = frames - parts
    wide = 2 * SEGS * STEPS
    _, inverse = block_tables(bins)
    _, _, back = step_tables(parts, frames, channels)
    vmem = pl.BlockSpec(memory_space=pltpu.VMEM)
    smem = pl.BlockSpec(memory_space=pltpu.SMEM)

    operands = [*me] + list(s_list) + [pltpu.with_memory_space_constraint(hat, pltpu.VMEM)]
    aliases = {}
    if total is not None:
        if not last:
            aliases = {len(operands): 0}
        operands.append(total)
    scratch = []
    if last:
        operands += [jnp.asarray(back), jnp.asarray(inverse)]
        each = blocks // shares
        out_shape = [jax.ShapeDtypeStruct((channels, each, bins), BF16)] * shares
        scratch = [
            pltpu.VMEM((slabs, channels // 2, 2 * wide, SLAB), BF16),
            pltpu.VMEM((channels * blocks, bins), BF16),
            pltpu.VMEM((channels * blocks, bins), BF16),
            pltpu.VMEM((shares, channels, each, bins), F32),
        ]
    else:
        out_shape = jax.ShapeDtypeStruct((slabs, channels // 2, 2 * wide, SLAB), F32)
    body = functools.partial(
        mix_kernel, tuple(flips), own, channels, blocks, shares, total is not None, last
    )
    return pl.pallas_call(
        body,
        in_specs=[smem] * 2 + [vmem] * (len(operands) - 2),
        out_specs=[vmem] * len(out_shape) if last else vmem,
        out_shape=out_shape,
        scratch_shapes=scratch,
        input_output_aliases=aliases,
        compiler_params=pltpu.CompilerParams(vmem_limit_bytes=12 * 2**20),
        cost_estimate=COST,
    )(*operands)


def sum_kernel(count, ch_ref, *refs):
    parts, outs, sum_ref = refs[:count], refs[count:-1], refs[-1]
    total = parts[0][...].astype(F32)
    for part in parts[1:]:
        total = total + part[...].astype(F32)
    sum_ref[...] = total
    for d in range(len(outs)):
        outs[d][...] = sum_ref[:, pl.ds(ch_ref[0] ^ d, 1), :].reshape(outs[d].shape).astype(BF16)


def sum_groups(parts, me):
    channels, each, bins = parts[0].shape
    vmem = pl.BlockSpec(memory_space=pltpu.VMEM)
    return pl.pallas_call(
        functools.partial(sum_kernel, len(parts)),
        in_specs=[pl.BlockSpec(memory_space=pltpu.SMEM)] + [vmem] * len(parts),
        out_specs=[vmem] * each,
        out_shape=[jax.ShapeDtypeStruct((channels, bins), BF16)] * each,
        scratch_shapes=[pltpu.VMEM(parts[0].shape, F32)],
        compiler_params=pltpu.CompilerParams(vmem_limit_bytes=8 * 2**20),
    )(me, *parts)


def decode(signal, matrix):
    decoded = lax.dot_general(
        signal, matrix, (((0,), (0,)), ((), ())), preferred_element_type=F32
    )
    return decoded.astype(BF16)


def per_device(src_count, ch_count, dry_signal, room_spectra, render_slot, decoder):
    rows_total, parts, channels, _, block_len = room_spectra.shape
    own = dry_signal.shape[0]
    frames = dry_signal.shape[1] // block_len
    blocks = frames - parts
    src_me = lax.axis_index("src").astype(jnp.int32)
    ch_me = lax.axis_index("ch").astype(jnp.int32)

    if own == 1:
        x_own = dry_signal.reshape(frames, block_len)
    else:
        x_own = dry_signal.reshape(own, frames, block_len).transpose(1, 0, 2)

    def swap(value, axis, count, flip):
        return lax.ppermute(value, axis, [(i, i ^ flip) for i in range(count)])

    chips = ch_count // 2
    first = chips // 2
    far = [first] + [d for d in range(chips - 1, 0, -1) if d != first]
    mate = swap(x_own, "ch", ch_count, 1)
    lanes = {d: swap(x_own, "ch", ch_count, 2 * d) for d in far}
    me = (src_me[None], ch_me[None])
    hat = transform_responses(room_spectra, me, render_slot)

    row = jnp.arange(ch_count * channels, dtype=jnp.int32)
    chip_order = [0] + list(range(chips - 2, 0, -1)) + [chips - 1]
    flips = np.array([2 * d + core for d in chip_order for core in range(2)], dtype=np.int32)
    takes = (jnp.asarray(np.repeat(flips, channels)) ^ ch_me) * channels + row % channels
    order = (takes[:, None] == row[None, :]).astype(BF16)
    own_order = lax.optimization_barrier(dot(order, decoder).astype(BF16))

    def add(s_list, flips, total, last):
        return add_sources(
            s_list, flips, own, me, hat, total, last, src_count, channels, parts
        )

    x_near, hat = lax.optimization_barrier((x_own, hat))
    near = transform_signals([x_near, mate], own, block_len, parts)
    total = add([near], [[0, 1]], None, False)
    *late, total = lax.optimization_barrier((*[lanes[d] for d in far], total))
    mine = transform_signals(late, own, block_len, parts)
    given = swap(mine, "ch", ch_count, 1)
    total = add([mine], [[2 * d for d in far]], total, False)
    total = add([given], [[2 * d + 1 for d in far]], total, True)

    sums = [total[0]] + [swap(total[d], "src", src_count, d) for d in range(src_count - 1, 0, -1)]
    if blocks == src_count * ch_count:
        pieces = sum_groups(sums, ch_me[None])
        given = swap(jnp.concatenate(pieces[1::2], axis=0), "ch", ch_count, 1)
        both = {
            d: jnp.concatenate([pieces[2 * d], given[d * channels : (d + 1) * channels]], axis=0)
            for d in chip_order
        }
        arrived = [both[0]] + [swap(both[d], "ch", ch_count, 2 * d) for d in chip_order[1:]]
        return decode(jnp.concatenate(arrived, axis=0), own_order)
    signal = sums[0].astype(F32)
    for part in sums[1:]:
        signal = signal + part.astype(F32)
    signal = signal.astype(BF16).reshape(channels, -1)
    return decode(lax.all_to_all(signal, "ch", split_axis=1, concat_axis=0, tiled=True), decoder)


def solution(mesh):
    body = functools.partial(per_device, mesh.shape["src"], mesh.shape["ch"])
    return jax.shard_map(
        body,
        mesh=mesh,
        in_specs=(P(("src", "ch"), None), P("src", None, "ch", None, None), P("src"), P()),
        out_specs=P(("src", "ch"), None),
        check_vma=False,
    )
```
